32 devices in a mesh: dp: 8 (over y, x, core), seq: 4 (over z).
Axes of the slice: x: 2, y: 2, z: 4, core: 2. Of those that a mesh axis runs over, the one named last changes fastest.
Arguments:
- hidden: bfloat16 [16, 3, 1024, 1024], P('dp', None, 'seq'), may hold values from -6 to 6
- encoder_out: bfloat16 [16, 1024, 1024], P('dp', 'seq'), may hold values from -6 to 6
- cotangent: bfloat16 [16, 3, 1024, 1024], P('dp', None, 'seq'), may hold values from -6 to 6
- dec_lengths: int32 [16], P('dp'), may hold values from 512 to 1024, as said below
- enc_lengths: int32 [16], P('dp'), may hold values from 512 to 1024, as said below
- self_qkv: bfloat16 [3, 1024, 1024], replicated, may hold values from -0.1875 to 0.1875
- self_qv_bias: bfloat16 [2, 1024], replicated, may hold values from -3 to 3
- self_out: bfloat16 [1024, 1024], replicated, may hold values from -3 to 3
- self_out_bias: bfloat16 [1024], replicated, may hold values from -2 to 2
- rel_weight: bfloat16 [1024, 512], replicated, may hold values from -0.1875 to 0.1875
- rel_bias: bfloat16 [512], replicated, may hold values from -4 to 4
- cross_qkv: bfloat16 [3, 1024, 1024], replicated, may hold values from -0.1875 to 0.1875
- cross_qv_bias: bfloat16 [2, 1024], replicated, may hold values from -3 to 3
- cross_out: bfloat16 [1024, 1024], replicated, may hold values from -3 to 3
- cross_out_bias: bfloat16 [1024], replicated, may hold values from -2 to 2
- ffn_in: bfloat16 [1024, 4096], replicated, may hold values from -0.1875 to 0.1875
- ffn_in_bias: bfloat16 [4096], replicated, may hold values from -3 to 3
- ffn_out: bfloat16 [4096, 1024], replicated, may hold values from -0.09375 to 0.09375
- ffn_out_bias: bfloat16 [1024], replicated, may hold values from -2 to 2
- norm_gain: bfloat16 [3, 1024], replicated, may hold values from 0.5 to 1.5
- norm_bias: bfloat16 [3, 1024], replicated, may hold values from -2 to 2
Outputs:
- output: bfloat16 [16, 3, 1024, 1024], P('dp', None, 'seq')
- grad_hidden: bfloat16 [16, 3, 1024, 1024], P('dp', None, 'seq')
- grad_encoder: bfloat16 [16, 1024, 1024], P('dp', 'seq')
- grad_self_qkv: float32 [3145728], P(('dp', 'seq'))
- grad_self_qv_bias: float32 [2048], P('seq')
- grad_self_out: float32 [1048576], P(('dp', 'seq'))
- grad_self_out_bias: float32 [1024], P('seq')
- grad_rel_weight: float32 [524288], P(('dp', 'seq'))
- grad_rel_bias: float32 [512], P('seq')
- grad_cross_qkv: float32 [3145728], P(('dp', 'seq'))
- grad_cross_qv_bias: float32 [2048], P('seq')
- grad_cross_out: float32 [1048576], P(('dp', 'seq'))
- grad_cross_out_bias: float32 [1024], P('seq')
- grad_ffn_in: float32 [4194304], P(('dp', 'seq'))
- grad_ffn_in_bias: float32 [4096], P('seq')
- grad_ffn_out: float32 [4194304], P(('dp', 'seq'))
- grad_ffn_out_bias: float32 [1024], P('seq')
- grad_norm_gain: float32 [3072], P('seq')
- grad_norm_bias: float32 [3072], P('seq')
The draws below stay inside these ranges and needn't reach their ends.
Inputs may be any that keep to these rules, and one draw needn't show every extreme that they name: `dec_lengths`: in each group of 2 consecutive sequences one, drawn from the seed, has all 1024 decoder positions valid. `enc_lengths`: in each group of 2 consecutive sequences one, drawn from the seed, has all 1024 encoder positions valid.
All inputs are finite; a program needn't handle non-finite values.
Results may differ from the reference program's by a relative error of at most 0.028.
Values may be sent and summed in bfloat16 or wider, within the bound.
No kernel may reach another device: no remote copies, remote signals or barrier semaphores. Data moves between devices by JAX's collectives and lax.ppermute only.
A program may use at most 576 MiB of HBM per device.

```python
import math
import jax
import jax.numpy as jnp
from jax import lax

D = 1024
HEADS = 16
FF = 4096
BUCKETS = 32
MAX_DIST = 128
NGRAM = 2
SEQS = 2
LENGTH = 1024
BATCH = 16


def pick_lengths(key, salt_value):
    base_key = jax.random.fold_in(key, salt_value)
    drawn = jax.random.randint(jax.random.fold_in(base_key, 1), (BATCH,), LENGTH // 2, LENGTH + 1)
    chosen = jax.random.randint(jax.random.fold_in(base_key, 2), (BATCH // SEQS,), 0, SEQS)
    slot_index = jnp.arange(BATCH, dtype=jnp.int32)
    target = chosen[slot_index // SEQS]
    return jnp.where(slot_index % SEQS == target, LENGTH, drawn).astype(jnp.int32)


def draw_dec_lengths(key, part):
    return pick_lengths(key, 11)


def draw_enc_lengths(key, part):
    return pick_lengths(key, 23)


def block_levels(stream_key, shape, cuts, low, top_value):
    def one(axis_at, parts):
        steps = jax.random.uniform(jax.random.fold_in(jax.random.fold_in(stream_key, 6), axis_at), (parts,), jnp.float32, low / len(cuts), top_value / len(cuts))
        return jnp.repeat(jnp.exp(steps), shape[axis_at] // parts).reshape((-1,) + (1,) * (len(shape) - axis_at - 1))

    loudness = one(*cuts[0])
    for cut in cuts[1:]:
        loudness = loudness * one(*cut)
    return loudness


def noise(own_key, shape, scale, reach, shards=(), kind=jnp.bfloat16):
    entries = scale * jax.random.normal(own_key, shape, jnp.float32)
    if shards:
        entries = entries * block_levels(own_key, shape, shards, -0.22, 0.18)
    return jnp.clip(entries, -reach, reach).astype(kind)


def setup_inputs(seed: int = 0) -> dict:
    splits = jax.random.split(jax.random.key(seed), 22)
    return {
        "hidden": noise(splits[0], (BATCH, NGRAM + 1, LENGTH, D), 1.0, 6.0, ((0, 8), (2, 4))),
        "encoder_out": noise(splits[1], (BATCH, LENGTH, D), 1.0, 6.0, ((0, 8), (1, 4))),
        "cotangent": noise(splits[2], (BATCH, NGRAM + 1, LENGTH, D), 1.0, 6.0, ((0, 8), (2, 4))),
        "dec_lengths": draw_dec_lengths(jax.random.fold_in(splits[21], 71), 0),
        "enc_lengths": draw_enc_lengths(jax.random.fold_in(splits[21], 71), 0),
        "self_qkv": noise(splits[5], (3, D, D), D ** -0.5, 0.1875),
        "self_qv_bias": noise(splits[6], (2, D), 0.5, 3.0),
        "self_out": noise(splits[7], (D, D), (max(4 * D // LENGTH, 1)) ** -0.5, 3.0),
        "self_out_bias": noise(splits[8], (D,), 0.3, 2.0),
        "rel_weight": noise(splits[9], (D, HEADS * BUCKETS), D ** -0.5, 0.1875),
        "rel_bias": noise(splits[10], (HEADS * BUCKETS,), 1.0, 4.0),
        "cross_qkv": noise(splits[11], (3, D, D), D ** -0.5, 0.1875),
        "cross_qv_bias": noise(splits[12], (2, D), 0.5, 3.0),
        "cross_out": noise(splits[13], (D, D), (max(4 * D // LENGTH, 1)) ** -0.5, 3.0),
        "cross_out_bias": noise(splits[14], (D,), 0.3, 2.0),
        "ffn_in": noise(splits[15], (D, FF), D ** -0.5, 0.1875),
        "ffn_in_bias": noise(splits[16], (FF,), 0.5, 3.0),
        "ffn_out": noise(splits[17], (FF, D), FF ** -0.5, 0.09375),
        "ffn_out_bias": noise(splits[18], (D,), 0.3, 2.0),
        "norm_gain": jnp.clip(1.0 + 0.1 * jax.random.normal(splits[19], (3, D), jnp.float32), 0.5, 1.5).astype(jnp.bfloat16),
        "norm_bias": noise(splits[20], (3, D), 0.3, 2.0),
    }


@jax.custom_vjp
def low(v):
    return lax.optimization_barrier(v.astype(jnp.bfloat16)).astype(jnp.float32)

@jax.custom_vjp
def low_back(v):
    return v

def low_keep(v):
    return (low(v), None)

def low_pass(kept, grad):
    return (grad,)

def back_keep(v):
    return (v, None)

def back_low(kept, grad):
    return (low(grad),)
low.defvjp(low_keep, low_pass)
low_back.defvjp(back_keep, back_low)
HIGHEST = lax.Precision.HIGHEST
negative = -1e+30
epsilon = 1e-05

def rounded_both(value):
    return low_back(low(value))

def matmul(left, right):
    return jnp.dot(left, right, precision=HIGHEST)

def layer_norm(value, gain, shift):
    center = value - lax.optimization_barrier(jnp.mean(value, -1, keepdims=True))
    spread = lax.optimization_barrier(jnp.mean(center * center, -1, keepdims=True))
    return center * lax.rsqrt(spread + epsilon) * gain + shift

def gelu_exact(value):
    return jax.nn.gelu(value, approximate=False)

def bucket_of(distance):
    half = BUCKETS // 2
    counted = jnp.zeros_like(distance)
    for level in range(1, half):
        bound = math.ceil(half * (MAX_DIST / half) ** (level / half))
        counted = counted + (distance >= bound).astype(jnp.int32)
    return jnp.where(distance < half, distance, half + counted)

def self_attention(query, key, value, rel, dec_len):
    streams, length, heads, size = query.shape
    scale = size ** (-0.5)
    positions = jnp.arange(length, dtype=jnp.int32)
    distance = positions[:, None] - positions[None, :]
    lookup = jnp.broadcast_to(bucket_of(jnp.maximum(distance, 0))[None], (heads, length, length))
    valid = positions[None, :] < dec_len
    results = []
    for stream in range(streams):
        rel_heads = jnp.transpose(rel[stream], (1, 0, 2))
        scores = scale * jnp.einsum('qhd,khd->hqk', query[stream], key[0], precision=HIGHEST)
        scores = scores + jnp.take_along_axis(rel_heads, lookup, axis=2)
        if stream == 0:
            allowed = (distance >= 0) & valid
            weights = low(jax.nn.softmax(jnp.where(allowed[None], low_back(scores), negative), axis=-1))
            mixed = jnp.einsum('hqk,khd->qhd', weights, value[0], precision=HIGHEST)
        else:
            own_score = scale * jnp.transpose(lax.optimization_barrier(jnp.sum(query[stream] * key[stream], -1))) + rel_heads[:, :, 0]
            joined = low_back(jnp.concatenate([scores, own_score[:, :, None]], -1))
            allowed = jnp.concatenate([(distance >= 1) & valid, jnp.ones((length, 1), dtype=jnp.bool_)], -1)
            weights = low(jax.nn.softmax(jnp.where(allowed[None], joined, negative), axis=-1))
            mixed = jnp.einsum('hqk,khd->qhd', weights[:, :, :length], value[0], precision=HIGHEST)
            mixed = mixed + jnp.transpose(weights[:, :, length])[:, :, None] * value[stream]
        results.append(mixed)
    return jnp.stack(results)

def cross_attention(query, key, value, enc_len):
    streams, length, heads, size = query.shape
    scale = size ** (-0.5)
    flat_query = query.reshape(streams * length, heads, size)
    scores = low_back(scale * jnp.einsum('qhd,khd->hqk', flat_query, key, precision=HIGHEST))
    allowed = (jnp.arange(key.shape[0], dtype=jnp.int32) < enc_len)[None, None, :]
    weights = low(jax.nn.softmax(jnp.where(allowed, scores, negative), axis=-1))
    return jnp.einsum('hqk,khd->qhd', weights, value, precision=HIGHEST)

def sequence_forward(hidden_seq, encoder_seq, dec_len, enc_len, params):
    self_qkv, self_qv_bias, self_out, self_out_bias, rel_weight, rel_bias, cross_qkv, cross_qv_bias, cross_out, cross_out_bias, ffn_in, ffn_in_bias, ffn_out, ffn_out_bias, norm_gain, norm_bias = params
    streams, length, width = hidden_seq.shape
    heads = HEADS
    size = width // heads
    shape = (streams, length, heads, size)
    rows = hidden_seq.reshape(streams * length, width)
    query = rounded_both(matmul(rows, self_qkv[0]) + self_qv_bias[0]).reshape(shape)
    key = rounded_both(matmul(rows, self_qkv[1])).reshape(shape)
    value = rounded_both(matmul(rows, self_qkv[2]) + self_qv_bias[1]).reshape(shape)
    rel = low_back(matmul(rows, rel_weight) + rel_bias).reshape(streams, length, heads, BUCKETS)
    mixed = rounded_both(self_attention(query, key, value, rel, dec_len)).reshape(streams * length, width)
    branch = low_back(matmul(mixed, self_out) + self_out_bias)
    first_norm = layer_norm(rows + branch, norm_gain[0], norm_bias[0])
    first_low = low(first_norm)
    cross_query = rounded_both(matmul(first_low, cross_qkv[0]) + cross_qv_bias[0]).reshape(shape)
    cross_key = rounded_both(matmul(encoder_seq, cross_qkv[1])).reshape(-1, heads, size)
    cross_value = rounded_both(matmul(encoder_seq, cross_qkv[2]) + cross_qv_bias[1]).reshape(-1, heads, size)
    cross_mixed = rounded_both(cross_attention(cross_query, cross_key, cross_value, enc_len)).reshape(streams * length, width)
    cross_branch = low_back(matmul(cross_mixed, cross_out) + cross_out_bias)
    second_norm = layer_norm(first_norm + cross_branch, norm_gain[1], norm_bias[1])
    second_low = low(second_norm)
    hidden_pre = low_back(matmul(second_low, ffn_in) + ffn_in_bias)
    activated = low(gelu_exact(hidden_pre))
    ffn_branch = low_back(matmul(activated, ffn_out) + ffn_out_bias)
    result = layer_norm(second_norm + ffn_branch, norm_gain[2], norm_bias[2])
    return result.reshape(streams, length, width)

def reference(hidden, encoder_out, cotangent, dec_lengths, enc_lengths, self_qkv, self_qv_bias, self_out, self_out_bias, rel_weight, rel_bias, cross_qkv, cross_qv_bias, cross_out, cross_out_bias, ffn_in, ffn_in_bias, ffn_out, ffn_out_bias, norm_gain, norm_bias):
    params = tuple((weight.astype(jnp.float32) for weight in (self_qkv, self_qv_bias, self_out, self_out_bias, rel_weight, rel_bias, cross_qkv, cross_qv_bias, cross_out, cross_out_bias, ffn_in, ffn_in_bias, ffn_out, ffn_out_bias, norm_gain, norm_bias)))

    def one_sequence(carry, item):
        hidden_seq, encoder_seq, cotangent_seq, dec_len, enc_len = item

        def forward(states, encoded, weights):
            return sequence_forward(states, encoded, dec_len, enc_len, weights)
        result, pullback = jax.vjp(forward, hidden_seq.astype(jnp.float32), encoder_seq.astype(jnp.float32), params)
        grad_states, grad_encoded, grad_weights = pullback(cotangent_seq.astype(jnp.float32))
        carry = jax.tree.map(jnp.add, carry, grad_weights)
        return (carry, (result.astype(jnp.bfloat16), grad_states.astype(jnp.bfloat16), grad_encoded.astype(jnp.bfloat16)))
    start = jax.tree.map(jnp.zeros_like, params)
    totals, outputs = lax.scan(one_sequence, start, (hidden, encoder_out, cotangent, dec_lengths, enc_lengths))
    output, grad_hidden, grad_encoder = outputs
    return (output, grad_hidden, grad_encoder, totals[0].reshape(-1), totals[1].reshape(-1), totals[2].reshape(-1), totals[3], totals[4].reshape(-1), totals[5], totals[6].reshape(-1), totals[7].reshape(-1), totals[8].reshape(-1), totals[9], totals[10].reshape(-1), totals[11], totals[12].reshape(-1), totals[13], totals[14].reshape(-1), totals[15].reshape(-1))
```

```python
import functools
import math

import jax
import jax.numpy as jnp
import numpy as np
from jax import lax
from jax.experimental import pallas as pl
from jax.experimental.pallas import tpu as pltpu
from jax.sharding import PartitionSpec as P

HEADS = 16
BUCKETS = 32
MAX_DIST = 128
SIZE = 64
SCALE = 0.125
TILE = 128
NEGATIVE = -1e30
EPSILON = 1e-05
VMEM_LIMIT = 56 * 2**20

low_type = jnp.bfloat16
high_type = jnp.float32


def contract(left, right, left_dim, right_dim):
    return lax.dot_general(
        left, right, (((left_dim,), (right_dim,)), ((), ())), preferred_element_type=high_type
    )


def split_two(value):
    top = value.astype(low_type)
    return top, (value - top.astype(high_type)).astype(low_type)


def feature_rows(first, value):
    a = value.astype(low_type).astype(high_type)
    b = (value - a).astype(low_type).astype(high_type)
    c = value - a - b
    count = value.shape[1]
    at = lax.broadcasted_iota(jnp.int32, (16, count), 0)
    out = jnp.where(at == 0, first, 0.0)
    for index, piece in enumerate((a, b, c)):
        out = jnp.where(at == index + 1, piece, out)
    return out.astype(low_type)


def key_features(valid):
    mask = jnp.where(valid, 0.0, NEGATIVE)[:, None, :]
    ones = jnp.ones_like(mask)
    return jnp.concatenate([mask, ones, ones, ones] + [jnp.zeros_like(mask)] * 12, 1).astype(
        low_type
    )


def bucket_table():
    half = BUCKETS // 2
    distance = (TILE - np.arange(2 * TILE)) % (2 * TILE)
    counted = np.zeros_like(distance)
    for level in range(1, half):
        counted = counted + (distance >= math.ceil(half * (MAX_DIST / half) ** (level / half)))
    bucket = np.where(distance < half, distance, half + counted)
    table = (bucket[None, :] == np.arange(BUCKETS)[:, None]).astype(np.float32)
    table[BUCKETS - 1] = -(bucket < BUCKETS - 1).astype(np.float32)
    return table


def near_bias(rel, table):
    top, rest = split_two(rel)
    return contract(
        jnp.concatenate([top, rest], 0), jnp.concatenate([table, table], 0), 0, 0
    )


def cross_forward_kernel(q_ref, k_ref, v_ref, mark_ref, o_ref, total_ref):
    count, keys = q_ref.shape[1], k_ref.shape[1]
    k1 = jnp.concatenate([k_ref[...], mark_ref[...]], 0)
    v1 = jnp.concatenate([v_ref[...], jnp.ones((16, keys), low_type)], 0)
    zero = jnp.zeros((1, count), high_type)
    q1 = jnp.concatenate([q_ref[...], feature_rows(1.0, zero)], 0)
    scores = contract(k1, q1, 0, 0)
    peak = jnp.max(scores, 0, keepdims=True)
    weights = jnp.exp(scores - peak).astype(low_type)
    mixed = contract(v1, weights, 1, 0)
    total = mixed[SIZE : SIZE + 1]
    o_ref[...] = (mixed[:SIZE] * (1.0 / total)).astype(low_type)
    total_ref[...] = peak + jnp.log(total)


def cross_backward_kernel(
    q_ref, k_ref, v_ref, mark_ref, o_ref, total_ref, do_ref, dq_ref, dk_ref, dv_ref, dk_acc, dv_acc, *, step
):
    count, keys = q_ref.shape[1], k_ref.shape[1]
    k = k_ref[...]
    k1 = jnp.concatenate([k, mark_ref[...]], 0)
    v1 = jnp.concatenate([v_ref[...], mark_ref[...]], 0)
    for n in range(0, count, step):
        q, do = q_ref[:, n : n + step], do_ref[:, n : n + step]
        delta = jnp.sum(
            do.astype(high_type) * o_ref[:, n : n + step].astype(high_type), 0, keepdims=True
        )
        q1 = jnp.concatenate([q, feature_rows(1.0, -total_ref[:, n : n + step])], 0)
        do1 = jnp.concatenate([do, feature_rows(0.0, -delta)], 0)
        weights = jnp.exp(contract(q1, k1, 0, 0))
        grad_scores = (weights * contract(do1, v1, 0, 0)).astype(low_type)
        weights = weights.astype(low_type)
        dq_ref[:, n : n + step] = (contract(k, grad_scores, 1, 1) * SCALE).astype(low_type)
        dk = contract(q, grad_scores, 1, 0)
        dv = contract(do, weights, 1, 0)
        if n == 0:
            dk_acc[...] = dk
            dv_acc[...] = dv
        else:
            dk_acc[...] += dk
            dv_acc[...] += dv
    dk_ref[...] = dk_acc[...].astype(low_type)
    dv_ref[...] = dv_acc[...].astype(low_type)


def self_forward_kernel(q_ref, k_ref, v_ref, rel_ref, mark_ref, table_ref, o_ref, total_ref, *, T, S):
    n, tile = S * T, min(TILE, T)
    keys = k_ref.shape[1] - n + T
    q, rel = q_ref[...], rel_ref[...]
    k1 = jnp.concatenate([k_ref[:, :keys], mark_ref[...]], 0)
    v1 = jnp.concatenate([v_ref[:, :keys], jnp.ones((16, keys), low_type)], 0)
    q1 = jnp.concatenate([q, feature_rows(1.0, rel[BUCKETS - 1 :])], 0)
    scores = contract(q1, k1, 0, 0)
    near = near_bias(rel, table_ref[...])
    at = lax.broadcasted_iota(jnp.int32, (tile, tile), 0)
    to = lax.broadcasted_iota(jnp.int32, (tile, tile), 1)
    weights, peaks = [], []
    for s in range(S):
        for r in range(T // tile):
            row, first = s * T + r * tile, keys - T + r * tile - TILE
            bias = pltpu.roll(near[row : row + tile], 0, 1, stride=1, stride_axis=0)
            block = scores[row : row + tile]
            left = block[:, first : first + TILE] + bias[:, :TILE]
            right = block[:, first + TILE : first + TILE + tile] + bias[:, TILE : TILE + tile]
            right = jnp.where((to <= at) if s == 0 else (to < at), right, NEGATIVE)
            parts = [left, right]
            peak = jnp.max(
                jnp.maximum(left, right) if tile == TILE else jnp.concatenate(parts, 1),
                1,
                keepdims=True,
            )
            if first > 0:
                far = block[:, :first]
                peak = jnp.maximum(peak, jnp.max(far, 1, keepdims=True))
                parts = [far] + parts
            parts = [jnp.exp(part - peak).astype(low_type) for part in parts]
            if first + TILE + tile < keys:
                parts.append(jnp.zeros((tile, keys - first - TILE - tile), low_type))
            weights.append(jnp.concatenate(parts, 1))
            peaks.append(jnp.broadcast_to(peak, (tile, tile)).T[0:1])
    mixed = contract(v1, jnp.concatenate(weights, 0), 1, 1)
    peak = jnp.concatenate(peaks, 1)
    total, mixed = mixed[SIZE : SIZE + 1], mixed[:SIZE]
    own_k = k_ref[:, keys:].astype(high_type)
    own_v = v_ref[:, keys:].astype(high_type)
    own = jnp.sum(q[:, T:].astype(high_type) * own_k, 0, keepdims=True) + rel[0:1, T:]
    top = jnp.maximum(peak[:, T:], own)
    main_part, own_part = jnp.exp(peak[:, T:] - top), jnp.exp(own - top)
    joined = total[:, T:] * main_part + own_part
    inverse = 1.0 / joined
    o_ref[:, :T] = (mixed[:, :T] * (1.0 / total[:, :T])).astype(low_type)
    o_ref[:, T:] = (mixed[:, T:] * (main_part * inverse) + own_v * (own_part * inverse)).astype(
        low_type
    )
    total_ref[:, :T] = peak[:, :T] + jnp.log(total[:, :T])
    total_ref[:, T:] = top + jnp.log(joined)


def self_backward_kernel(
    q_ref,
    k_ref,
    v_ref,
    rel_ref,
    mark_ref,
    table_ref,
    o_ref,
    total_ref,
    do_ref,
    dq_ref,
    dk_ref,
    dv_ref,
    drel_ref,
    *,
    T,
    S,
):
    n, tile = S * T, min(TILE, T)
    keys = k_ref.shape[1] - n + T
    q, rel, do, total = q_ref[...], rel_ref[...], do_ref[...], total_ref[...]
    table = table_ref[...]
    k1 = jnp.concatenate([k_ref[:, :keys], mark_ref[...]], 0)
    v1 = jnp.concatenate([v_ref[:, :keys], mark_ref[...]], 0)
    do_high = do.astype(high_type)
    delta = jnp.sum(do_high * o_ref[...].astype(high_type), 0, keepdims=True)
    q1 = jnp.concatenate([q, feature_rows(1.0, rel[BUCKETS - 1 :] - total)], 0)
    do1 = jnp.concatenate([do, feature_rows(0.0, -delta)], 0)
    scores = contract(q1, k1, 0, 0)
    slopes = contract(do1, v1, 0, 0)
    near = near_bias(rel, table)
    at = lax.broadcasted_iota(jnp.int32, (tile, tile), 0)
    to = lax.broadcasted_iota(jnp.int32, (tile, tile), 1)
    mirror = (at + to == tile - 1).astype(high_type).astype(low_type)
    weights, grads, rels = [], [], []
    for s in range(S):
        for r in range(T // tile):
            row, first = s * T + r * tile, keys - T + r * tile - TILE
            bias = pltpu.roll(near[row : row + tile], 0, 1, stride=1, stride_axis=0)
            block, slope = scores[row : row + tile], slopes[row : row + tile]
            left = block[:, first : first + TILE] + bias[:, :TILE]
            right = block[:, first + TILE : first + TILE + tile] + bias[:, TILE : TILE + tile]
            right = jnp.where((to <= at) if s == 0 else (to < at), right, NEGATIVE)
            part = jnp.exp(jnp.concatenate([left, right], 1))
            grad = (part * slope[:, first : first + TILE + tile]).astype(low_type)
            turned = contract(mirror, grad, 1, 0)
            if tile < TILE:
                turned = jnp.concatenate([turned, jnp.zeros((tile, TILE - tile), high_type)], 1)
            turned = pltpu.roll(turned, 2 * TILE - tile + 1, 1, stride=1, stride_axis=0)
            turned = turned.astype(low_type)
            top, rest = split_two(contract(table, turned, 1, 1))
            both = contract(jnp.concatenate([top, rest], 0), mirror, 1, 0)
            rels.append(both[:BUCKETS] + both[BUCKETS:])
            parts, pieces = [part.astype(low_type)], [grad]
            if first > 0:
                part = jnp.exp(block[:, :first])
                pieces = [(part * slope[:, :first]).astype(low_type)] + pieces
                parts = [part.astype(low_type)] + parts
            if first + TILE + tile < keys:
                zero = jnp.zeros((tile, keys - first - TILE - tile), low_type)
                parts.append(zero)
                pieces.append(zero)
            weights.append(jnp.concatenate(parts, 1))
            grads.append(jnp.concatenate(pieces, 1))
    weights, grads = jnp.concatenate(weights, 0), jnp.concatenate(grads, 0)
    dq = contract(k1, grads, 1, 1)
    dk_ref[:, :keys] = contract(q, grads, 1, 0).astype(low_type)
    dv_ref[:, :keys] = contract(do, weights, 1, 0).astype(low_type)
    row_sums = dq[SIZE + 1 : SIZE + 2]
    own_k = k_ref[:, keys:].astype(high_type)
    own_v = v_ref[:, keys:].astype(high_type)
    own_q, own_do = q[:, T:].astype(high_type), do_high[:, T:]
    own = jnp.sum(own_q * own_k, 0, keepdims=True) + rel[0:1, T:]
    own_part = jnp.exp(own - total[:, T:])
    own_grad = own_part * (jnp.sum(own_do * own_v, 0, keepdims=True) - delta[:, T:])
    own_grad = own_grad.astype(low_type).astype(high_type)
    dq_ref[:, :T] = (dq[:SIZE, :T] * SCALE).astype(low_type)
    dq_ref[:, T:] = ((dq[:SIZE, T:] + own_grad * own_k) * SCALE).astype(low_type)
    dk_ref[:, keys:] = (own_grad * own_q).astype(low_type)
    dv_ref[:, keys:] = (own_part.astype(low_type).astype(high_type) * own_do).astype(low_type)
    bucket = lax.broadcasted_iota(jnp.int32, (BUCKETS, n), 0)
    drel = jnp.concatenate(rels, 1) + jnp.where(bucket == BUCKETS - 1, row_sums, 0.0)
    own_all = jnp.concatenate([jnp.zeros((1, T), high_type), own_grad], 1)
    drel_ref[...] = (drel + jnp.where(bucket == 0, own_all, 0.0)).astype(low_type)


def per_head(rows, count):
    return pl.BlockSpec((rows, count), lambda b, h: (h, b))


def per_sequence(keys):
    return pl.BlockSpec((None, 16, keys), lambda b, h: (b, 0, 0))


def per_total(count):
    return pl.BlockSpec((None, None, 1, count), lambda b, h: (b, h, 0, 0))


def like(array):
    return jax.ShapeDtypeStruct(array.shape, low_type)


def cost(B, rows, keys, products):
    return pl.CostEstimate(
        flops=2 * B * HEADS * rows * keys * 256 * products,
        bytes_accessed=B * HEADS * SIZE * (rows + keys) * 4 * products,
        transcendentals=B * HEADS * rows * keys,
    )


def cross_forward(q, k, v, mark):
    B, _, keys = mark.shape
    count = q.shape[1] // B
    return pl.pallas_call(
        cross_forward_kernel,
        grid=(B, HEADS),
        in_specs=[per_head(SIZE, count), per_head(SIZE, keys), per_head(SIZE, keys), per_sequence(keys)],
        out_specs=[per_head(SIZE, count), per_total(count)],
        out_shape=[like(q), jax.ShapeDtypeStruct((B, HEADS, 1, count), high_type)],
        cost_estimate=cost(B, count, keys, 2),
        compiler_params=pltpu.CompilerParams(vmem_limit_bytes=VMEM_LIMIT),
        name="cross_forward",
    )(q, k, v, mark)


def cross_backward(q, k, v, mark, o, total, do):
    B, _, keys = mark.shape
    count = q.shape[1] // B
    row, key = per_head(SIZE, count), per_head(SIZE, keys)
    return pl.pallas_call(
        functools.partial(cross_backward_kernel, step=count // 2),
        grid=(B, HEADS),
        in_specs=[row, key, key, per_sequence(keys), row, per_total(count), row],
        out_specs=[row, key, key],
        out_shape=[like(q), like(k), like(v)],
        scratch_shapes=[pltpu.VMEM((SIZE, keys), high_type)] * 2,
        cost_estimate=cost(B, count, keys, 5),
        compiler_params=pltpu.CompilerParams(vmem_limit_bytes=VMEM_LIMIT),
        name="cross_backward",
    )(q, k, v, mark, o, total, do)


def self_forward(q, k, v, rel, mark, table, T, S):
    B, _, keys = mark.shape
    count = S * T
    row, key, rels = per_head(SIZE, count), per_head(SIZE, keys + count - T), per_head(BUCKETS, count)
    return pl.pallas_call(
        functools.partial(self_forward_kernel, T=T, S=S),
        grid=(B, HEADS),
        in_specs=[row, key, key, rels, per_sequence(keys), pl.BlockSpec(table.shape, lambda b, h: (0, 0))],
        out_specs=[row, per_total(count)],
        out_shape=[like(q), jax.ShapeDtypeStruct((B, HEADS, 1, count), high_type)],
        cost_estimate=cost(B, count, keys, 2),
        compiler_params=pltpu.CompilerParams(vmem_limit_bytes=VMEM_LIMIT),
        name="self_forward",
    )(q, k, v, rel, mark, table)


def self_backward(q, k, v, rel, mark, table, o, total, do, T, S):
    B, _, keys = mark.shape
    count = S * T
    row, key, rels = per_head(SIZE, count), per_head(SIZE, keys + count - T), per_head(BUCKETS, count)
    return pl.pallas_call(
        functools.partial(self_backward_kernel, T=T, S=S),
        grid=(B, HEADS),
        in_specs=[
            row,
            key,
            key,
            rels,
            per_sequence(keys),
            pl.BlockSpec(table.shape, lambda b, h: (0, 0)),
            row,
            per_total(count),
            row,
        ],
        out_specs=[row, key, key, rels],
        out_shape=[like(q), like(k), like(v), like(rel)],
        cost_estimate=cost(B, count, keys, 5),
        compiler_params=pltpu.CompilerParams(vmem_limit_bytes=VMEM_LIMIT),
        name="self_backward",
    )(q, k, v, rel, mark, table, o, total, do)


def ffn_kernel(x_ref, w_ref, b_ref, g_ref, slope_ref):
    u = contract(x_ref[...], w_ref[...], 1, 0) + b_ref[...]
    z = jnp.abs(u) * (0.5**0.5)
    t = 1.0 / (1.0 + 0.3275911 * z)
    bell = jnp.exp(-z * z)
    poly = t * (
        0.254829592
        + t * (-0.284496736 + t * (1.421413741 + t * (-1.453152027 + t * 1.061405429)))
    )
    tail = 0.5 * poly * bell
    phi = jnp.where(u < 0.0, tail, 1.0 - tail)
    g_ref[...] = (u * phi).astype(low_type)
    slope_ref[...] = (phi + u * (bell * (2.0 * math.pi) ** -0.5)).astype(low_type)


def ffn_first(x, w, b):
    rows, width = x.shape
    hidden = w.shape[1]
    tm, tn = math.gcd(rows, 512), math.gcd(hidden, 1024)
    block = pl.BlockSpec((tm, tn), lambda j, i: (i, j))
    out = jax.ShapeDtypeStruct((rows, hidden), low_type)
    return pl.pallas_call(
        ffn_kernel,
        grid=(hidden // tn, rows // tm),
        in_specs=[
            pl.BlockSpec((tm, width), lambda j, i: (i, 0)),
            pl.BlockSpec((width, tn), lambda j, i: (0, j)),
            pl.BlockSpec((1, tn), lambda j, i: (0, j)),
        ],
        out_specs=[block, block],
        out_shape=[out, out],
        cost_estimate=pl.CostEstimate(
            flops=2 * rows * width * hidden, bytes_accessed=4 * rows * hidden, transcendentals=rows * hidden
        ),
        compiler_params=pltpu.CompilerParams(vmem_limit_bytes=VMEM_LIMIT),
        name="ffn_first",
    )(x, w, b)


def column_sum(value):
    return jnp.sum(value.astype(high_type), 0)


def row_sum(value):
    return jnp.sum(value.astype(high_type), 1)


def dot(spec, left, right):
    return jnp.einsum(spec, left, right, preferred_element_type=high_type)


def norm_parts(value):
    center = value - jnp.mean(value, -1, keepdims=True)
    inverse = lax.rsqrt(jnp.mean(center * center, -1, keepdims=True) + EPSILON)
    return center * inverse, inverse


def norm_back(value, grad, gain):
    unit, inverse = norm_parts(value)
    scaled = grad * gain
    back = inverse * (
        scaled
        - jnp.mean(scaled, -1, keepdims=True)
        - unit * jnp.mean(scaled * unit, -1, keepdims=True)
    )
    return back, jnp.sum(grad * unit, 0), jnp.sum(grad, 0)


def rounded(value):
    return lax.optimization_barrier(value.astype(jnp.bfloat16)).astype(jnp.float32)


def layer_norm(value, gain, shift):
    center = value - jnp.mean(value, -1, keepdims=True)
    spread = jnp.mean(center * center, -1, keepdims=True)
    return center * lax.rsqrt(spread + EPSILON) * gain + shift


def gelu_exact(value):
    return jax.nn.gelu(value, approximate=False)


def bucket_of(distance):
    half = BUCKETS // 2
    counted = jnp.zeros_like(distance)
    for level in range(1, half):
        bound = math.ceil(half * (MAX_DIST / half) ** (level / half))
        counted = counted + (distance >= bound).astype(jnp.int32)
    return jnp.where(distance < half, distance, half + counted)


def self_logits(query_s, key_s, rel_s, keys_s, dec_len, offset_pos):
    streams, local_len, heads, size = query_s.shape
    full_len = keys_s.shape[0]
    scale = size ** (-0.5)
    positions = offset_pos + jnp.arange(local_len, dtype=jnp.int32)
    key_positions = jnp.arange(full_len, dtype=jnp.int32)
    distance = positions[:, None] - key_positions[None, :]
    one_hot = (
        bucket_of(jnp.maximum(distance, 0))[:, :, None] == jnp.arange(BUCKETS, dtype=jnp.int32)
    ).astype(jnp.float32)
    scores = scale * jnp.einsum(
        "sqhd,khd->shqk", query_s, keys_s, preferred_element_type=jnp.float32
    )
    scores = scores + jnp.einsum("sqhb,qkb->shqk", rel_s, one_hot, precision=lax.Precision.HIGHEST)
    stream_ids = jnp.arange(streams, dtype=jnp.int32)
    allowed = (distance[None] >= jnp.minimum(stream_ids, 1)[:, None, None]) & (
        key_positions < dec_len
    )[None, None, :]
    scores = jnp.where(allowed[:, None], scores, NEGATIVE)
    own_score = (
        scale * jnp.sum(query_s.astype(jnp.float32) * key_s.astype(jnp.float32), -1) + rel_s[..., 0]
    )
    own_score = jnp.where(
        (stream_ids > 0)[:, None, None], jnp.transpose(own_score, (0, 2, 1)), NEGATIVE
    )
    return (scores, own_score, one_hot)


def plain_self_forward(items, offset_pos):
    query_s, key_s, value_s, rel_s, keys_s, values_s, dec_len = items
    scores, own_score, one_hot = self_logits(query_s, key_s, rel_s, keys_s, dec_len, offset_pos)
    peak = jnp.maximum(jnp.max(scores, -1), own_score)
    log_total = peak + jnp.log(
        jnp.sum(jnp.exp(scores - peak[..., None]), -1) + jnp.exp(own_score - peak)
    )
    weights = jnp.exp(scores - log_total[..., None]).astype(jnp.bfloat16)
    own_weight = rounded(jnp.exp(own_score - log_total))
    mixed = jnp.einsum("shqk,khd->sqhd", weights, values_s, preferred_element_type=jnp.float32)
    mixed = mixed + jnp.transpose(own_weight, (0, 2, 1))[..., None] * value_s.astype(jnp.float32)
    return (mixed.astype(jnp.bfloat16), log_total)


def plain_self_backward(items, offset_pos):
    query_s, key_s, value_s, rel_s, keys_s, values_s, dec_len, log_total, grad_s = items
    scores, own_score, one_hot = self_logits(query_s, key_s, rel_s, keys_s, dec_len, offset_pos)
    scale = query_s.shape[3] ** (-0.5)
    weights = jnp.exp(scores - log_total[..., None])
    own_weight = jnp.exp(own_score - log_total)
    grad_float = grad_s.astype(jnp.float32)
    grad_weights = jnp.einsum(
        "sqhd,khd->shqk", grad_s, values_s, preferred_element_type=jnp.float32
    )
    grad_own = jnp.transpose(jnp.sum(grad_float * value_s.astype(jnp.float32), -1), (0, 2, 1))
    delta = jnp.sum(grad_weights * weights, -1) + grad_own * own_weight
    grad_scores = (weights * (grad_weights - delta[..., None])).astype(jnp.bfloat16)
    grad_own_score = rounded(own_weight * (grad_own - delta))
    own_term = jnp.transpose(grad_own_score, (0, 2, 1))[..., None]
    grad_query = scale * (
        jnp.einsum("shqk,khd->sqhd", grad_scores, keys_s, preferred_element_type=jnp.float32)
        + own_term * key_s.astype(jnp.float32)
    )
    grad_keys = scale * jnp.einsum(
        "shqk,sqhd->khd", grad_scores, query_s, preferred_element_type=jnp.float32
    )
    grad_key_own = scale * own_term * query_s.astype(jnp.float32)
    grad_values = jnp.einsum(
        "shqk,sqhd->khd", weights.astype(jnp.bfloat16), grad_s, preferred_element_type=jnp.float32
    )
    grad_value_own = jnp.transpose(rounded(own_weight), (0, 2, 1))[..., None] * grad_float
    grad_rel = jnp.einsum(
        "shqk,qkb->sqhb", grad_scores.astype(jnp.float32), one_hot, precision=lax.Precision.HIGHEST
    )
    grad_rel = grad_rel.at[..., 0].add(jnp.transpose(grad_own_score, (0, 2, 1)))
    return (grad_query, grad_key_own, grad_value_own, grad_keys, grad_values, grad_rel)


def cross_logits(query_s, keys_s, enc_len):
    scale = query_s.shape[3] ** (-0.5)
    scores = scale * jnp.einsum(
        "sqhd,khd->shqk", query_s, keys_s, preferred_element_type=jnp.float32
    )
    key_positions = jnp.arange(keys_s.shape[0], dtype=jnp.int32)
    return jnp.where(key_positions < enc_len, scores, NEGATIVE)


def plain_cross_forward(items):
    query_s, keys_s, values_s, enc_len = items
    scores = cross_logits(query_s, keys_s, enc_len)
    peak = jnp.max(scores, -1)
    log_total = peak + jnp.log(jnp.sum(jnp.exp(scores - peak[..., None]), -1))
    weights = jnp.exp(scores - log_total[..., None]).astype(jnp.bfloat16)
    mixed = jnp.einsum("shqk,khd->sqhd", weights, values_s, preferred_element_type=jnp.float32)
    return (mixed.astype(jnp.bfloat16), log_total)


def plain_cross_backward(items):
    query_s, keys_s, values_s, enc_len, log_total, grad_s = items
    scale = query_s.shape[3] ** (-0.5)
    scores = cross_logits(query_s, keys_s, enc_len)
    weights = jnp.exp(scores - log_total[..., None])
    grad_weights = jnp.einsum(
        "sqhd,khd->shqk", grad_s, values_s, preferred_element_type=jnp.float32
    )
    delta = jnp.sum(grad_weights * weights, -1)
    grad_scores = (weights * (grad_weights - delta[..., None])).astype(jnp.bfloat16)
    grad_query = scale * jnp.einsum(
        "shqk,khd->sqhd", grad_scores, keys_s, preferred_element_type=jnp.float32
    )
    grad_keys = scale * jnp.einsum(
        "shqk,sqhd->khd", grad_scores, query_s, preferred_element_type=jnp.float32
    )
    grad_values = jnp.einsum(
        "shqk,sqhd->khd", weights.astype(jnp.bfloat16), grad_s, preferred_element_type=jnp.float32
    )
    return (grad_query, grad_keys, grad_values)


def plain_on_device(
    hidden,
    encoder_out,
    cotangent,
    dec_lengths,
    enc_lengths,
    self_qkv,
    self_qv_bias,
    self_out,
    self_out_bias,
    rel_weight,
    rel_bias,
    cross_qkv,
    cross_qv_bias,
    cross_out,
    cross_out_bias,
    ffn_in,
    ffn_in_bias,
    ffn_out,
    ffn_out_bias,
    norm_gain,
    norm_bias,
):
    seq_count, streams, local_len, width = hidden.shape
    seq_parts = lax.axis_size("seq")
    dp_parts = lax.axis_size("dp")
    full_len = local_len * seq_parts
    offset_pos = lax.axis_index("seq") * local_len
    heads = HEADS
    size = width // heads
    head_shape = (seq_count, streams, local_len, heads, size)
    all_shape = (seq_count, full_len, heads, size)
    kv_shape = (seq_count, full_len, width)
    rows = hidden.reshape(-1, width)
    row_count = rows.shape[0]
    gains = norm_gain.astype(high_type)
    shifts = norm_bias.astype(high_type)
    self_bias = self_qv_bias.astype(high_type)
    cross_bias = cross_qv_bias.astype(high_type)
    projected = jnp.einsum("rd,cde->cre", rows, self_qkv, preferred_element_type=high_type)
    query = (projected[0] + self_bias[0]).astype(low_type)
    key = projected[1].astype(low_type)
    value = (projected[2] + self_bias[1]).astype(low_type)
    rel_logits = jnp.dot(rows, rel_weight, preferred_element_type=high_type) + rel_bias.astype(
        high_type
    )
    rel_heads = rel_logits.reshape(seq_count, streams, local_len, heads, BUCKETS)
    key_main = key.reshape(seq_count, streams, local_len, width)[:, 0]
    value_main = value.reshape(seq_count, streams, local_len, width)[:, 0]
    keys_all, values_all = (
        lax.all_gather(key_main, "seq", axis=1, tiled=True),
        lax.all_gather(value_main, "seq", axis=1, tiled=True),
    )
    self_items = (
        query.reshape(head_shape),
        key.reshape(head_shape),
        value.reshape(head_shape),
        rel_heads,
        keys_all.reshape(all_shape),
        values_all.reshape(all_shape),
        dec_lengths,
    )
    attended, self_total = lax.map(lambda items: plain_self_forward(items, offset_pos), self_items)
    attended = attended.reshape(row_count, width)
    self_branch = jnp.dot(
        attended, self_out, preferred_element_type=high_type
    ) + self_out_bias.astype(high_type)
    first_sum = rows.astype(high_type) + self_branch
    first_norm = layer_norm(first_sum, gains[0], shifts[0])
    first_low = first_norm.astype(low_type)
    cross_query = (
        jnp.dot(first_low, cross_qkv[0], preferred_element_type=high_type) + cross_bias[0]
    ).astype(low_type)
    encoder_rows = encoder_out.reshape(-1, width)
    encoder_proj = jnp.einsum(
        "rd,cde->cre", encoder_rows, cross_qkv[1:], preferred_element_type=high_type
    )
    cross_key = encoder_proj[0].astype(low_type).reshape(seq_count, local_len, width)
    cross_value = (
        (encoder_proj[1] + cross_bias[1]).astype(low_type).reshape(seq_count, local_len, width)
    )
    cross_keys, cross_values = (
        lax.all_gather(cross_key, "seq", axis=1, tiled=True),
        lax.all_gather(cross_value, "seq", axis=1, tiled=True),
    )
    cross_items = (
        cross_query.reshape(head_shape),
        cross_keys.reshape(all_shape),
        cross_values.reshape(all_shape),
        enc_lengths,
    )
    cross_mixed, cross_total = lax.map(plain_cross_forward, cross_items)
    cross_mixed = cross_mixed.reshape(row_count, width)
    cross_branch = jnp.dot(
        cross_mixed, cross_out, preferred_element_type=high_type
    ) + cross_out_bias.astype(high_type)
    second_sum = first_norm + cross_branch
    second_norm = layer_norm(second_sum, gains[1], shifts[1])
    second_low = second_norm.astype(low_type)
    hidden_pre = jnp.dot(second_low, ffn_in, preferred_element_type=high_type) + ffn_in_bias.astype(
        high_type
    )
    activated = gelu_exact(hidden_pre).astype(low_type)
    ffn_branch = jnp.dot(
        activated, ffn_out, preferred_element_type=high_type
    ) + ffn_out_bias.astype(high_type)
    third_sum = second_norm + ffn_branch
    output = layer_norm(third_sum, gains[2], shifts[2]).astype(low_type).reshape(hidden.shape)
    third_value, norm_pull = jax.vjp(layer_norm, third_sum, gains[2], shifts[2])
    grad_third, grad_gain_ffn, grad_shift_ffn = norm_pull(
        cotangent.reshape(-1, width).astype(high_type)
    )
    grad_ffn = grad_third.astype(low_type)
    grad_ffn_out = jnp.einsum("rf,rd->fd", activated, grad_ffn, preferred_element_type=high_type)
    grad_ffn_out_bias = column_sum(grad_ffn)
    grad_activated = jnp.einsum("rd,fd->rf", grad_ffn, ffn_out, preferred_element_type=high_type)
    gelu_value, gelu_pull = jax.vjp(gelu_exact, hidden_pre)
    grad_pre = gelu_pull(grad_activated)[0].astype(low_type)
    grad_ffn_in = jnp.einsum("rd,rf->df", second_low, grad_pre, preferred_element_type=high_type)
    grad_ffn_in_bias = column_sum(grad_pre)
    grad_second = grad_third + jnp.einsum(
        "rf,df->rd", grad_pre, ffn_in, preferred_element_type=high_type
    )
    second_value, norm_pull = jax.vjp(layer_norm, second_sum, gains[1], shifts[1])
    grad_second_sum, grad_gain_cross, grad_shift_cross = norm_pull(grad_second)
    grad_cross = grad_second_sum.astype(low_type)
    grad_cross_out = jnp.einsum(
        "rd,re->de", cross_mixed, grad_cross, preferred_element_type=high_type
    )
    grad_cross_out_bias = column_sum(grad_cross)
    grad_cross_mixed = jnp.einsum(
        "re,de->rd", grad_cross, cross_out, preferred_element_type=high_type
    ).astype(low_type)
    cross_back_items = (
        cross_query.reshape(head_shape),
        cross_keys.reshape(all_shape),
        cross_values.reshape(all_shape),
        enc_lengths,
        cross_total,
        grad_cross_mixed.reshape(head_shape),
    )
    grad_cross_query, grad_cross_keys, grad_cross_values = lax.map(plain_cross_backward, cross_back_items)
    cross_key_sum, cross_value_sum = (
        lax.psum_scatter(
            grad_cross_keys.reshape(kv_shape).astype(jnp.bfloat16),
            "seq",
            scatter_dimension=1,
            tiled=True,
        ).astype(jnp.float32),
        lax.psum_scatter(
            grad_cross_values.reshape(kv_shape).astype(jnp.bfloat16),
            "seq",
            scatter_dimension=1,
            tiled=True,
        ).astype(jnp.float32),
    )
    query_low = grad_cross_query.reshape(row_count, width).astype(low_type)
    encoder_grads = jnp.stack(
        [cross_key_sum.reshape(-1, width), cross_value_sum.reshape(-1, width)]
    ).astype(low_type)
    grad_cross_query_weight = jnp.einsum(
        "rd,re->de", first_low, query_low, preferred_element_type=high_type
    )
    grad_cross_kv_weight = jnp.einsum(
        "rd,cre->cde", encoder_rows, encoder_grads, preferred_element_type=high_type
    )
    grad_cross_qkv = jnp.concatenate([grad_cross_query_weight[None], grad_cross_kv_weight], 0)
    grad_cross_bias = jnp.stack([column_sum(query_low), column_sum(encoder_grads[1])])
    grad_encoder = jnp.einsum(
        "cre,cde->rd", encoder_grads, cross_qkv[1:], preferred_element_type=high_type
    )
    grad_encoder = grad_encoder.astype(low_type).reshape(encoder_out.shape)
    grad_first = grad_second_sum + jnp.einsum(
        "re,de->rd", query_low, cross_qkv[0], preferred_element_type=high_type
    )
    first_value, norm_pull = jax.vjp(layer_norm, first_sum, gains[0], shifts[0])
    grad_first_sum, grad_gain_self, grad_shift_self = norm_pull(grad_first)
    grad_self = grad_first_sum.astype(low_type)
    grad_self_out = jnp.einsum("rd,re->de", attended, grad_self, preferred_element_type=high_type)
    grad_self_out_bias = column_sum(grad_self)
    grad_attended = jnp.einsum(
        "re,de->rd", grad_self, self_out, preferred_element_type=high_type
    ).astype(low_type)
    self_back_items = (
        query.reshape(head_shape),
        key.reshape(head_shape),
        value.reshape(head_shape),
        rel_heads,
        keys_all.reshape(all_shape),
        values_all.reshape(all_shape),
        dec_lengths,
        self_total,
        grad_attended.reshape(head_shape),
    )
    grad_query, grad_key_own, grad_value_own, grad_keys, grad_values, grad_rel = lax.map(
        lambda items: plain_self_backward(items, offset_pos), self_back_items
    )
    key_sum, value_sum = (
        lax.psum_scatter(
            grad_keys.reshape(kv_shape).astype(jnp.bfloat16), "seq", scatter_dimension=1, tiled=True
        ).astype(jnp.float32),
        lax.psum_scatter(
            grad_values.reshape(kv_shape).astype(jnp.bfloat16),
            "seq",
            scatter_dimension=1,
            tiled=True,
        ).astype(jnp.float32),
    )
    own_shape = (seq_count, streams, local_len, width)
    key_total = jnp.concatenate([key_sum[:, None], grad_key_own.reshape(own_shape)[:, 1:]], 1)
    value_total = jnp.concatenate([value_sum[:, None], grad_value_own.reshape(own_shape)[:, 1:]], 1)
    stacked_grad = jnp.stack(
        [
            grad_query.reshape(row_count, width),
            key_total.reshape(row_count, width),
            value_total.reshape(row_count, width),
        ]
    ).astype(low_type)
    rel_low = grad_rel.reshape(row_count, heads * BUCKETS).astype(low_type)
    grad_self_qkv = jnp.einsum("rd,cre->cde", rows, stacked_grad, preferred_element_type=high_type)
    grad_self_bias = jnp.stack([column_sum(stacked_grad[0]), column_sum(stacked_grad[2])])
    grad_rel_weight = jnp.einsum("rd,rb->db", rows, rel_low, preferred_element_type=high_type)
    grad_rel_bias = column_sum(rel_low)
    grad_rows = grad_first_sum + jnp.einsum(
        "cre,cde->rd", stacked_grad, self_qkv, preferred_element_type=high_type
    )
    grad_rows = grad_rows + jnp.einsum(
        "rb,db->rd", rel_low, rel_weight, preferred_element_type=high_type
    )
    grad_hidden = grad_rows.astype(low_type).reshape(hidden.shape)
    matrices = [
        grad_self_qkv,
        grad_self_out,
        grad_rel_weight,
        grad_cross_qkv,
        grad_cross_out,
        grad_ffn_in,
        grad_ffn_out,
    ]
    vectors = [
        grad_self_bias.reshape(-1),
        grad_self_out_bias,
        grad_rel_bias,
        grad_cross_bias.reshape(-1),
        grad_cross_out_bias,
        grad_ffn_in_bias,
        grad_ffn_out_bias,
        jnp.stack([grad_gain_self, grad_gain_cross, grad_gain_ffn]).reshape(-1),
        jnp.stack([grad_shift_self, grad_shift_cross, grad_shift_ffn]).reshape(-1),
    ]
    vec_blocks = [piece.reshape(seq_parts, -1) for piece in vectors]
    mat_blocks = [piece.reshape(dp_parts, seq_parts, -1) for piece in matrices]
    reduced = (
        lax.psum_scatter(
            mat_blocks[0].astype(jnp.bfloat16), "seq", scatter_dimension=1, tiled=True
        ).astype(jnp.float32),
        lax.psum_scatter(
            mat_blocks[1].astype(jnp.bfloat16), "seq", scatter_dimension=1, tiled=True
        ).astype(jnp.float32),
        lax.psum_scatter(
            mat_blocks[2].astype(jnp.bfloat16), "seq", scatter_dimension=1, tiled=True
        ).astype(jnp.float32),
        lax.psum_scatter(
            mat_blocks[3].astype(jnp.bfloat16), "seq", scatter_dimension=1, tiled=True
        ).astype(jnp.float32),
        lax.psum_scatter(
            mat_blocks[4].astype(jnp.bfloat16), "seq", scatter_dimension=1, tiled=True
        ).astype(jnp.float32),
        lax.psum_scatter(
            mat_blocks[5].astype(jnp.bfloat16), "seq", scatter_dimension=1, tiled=True
        ).astype(jnp.float32),
        lax.psum_scatter(
            mat_blocks[6].astype(jnp.bfloat16), "seq", scatter_dimension=1, tiled=True
        ).astype(jnp.float32),
        lax.psum_scatter(
            vec_blocks[0].astype(jnp.bfloat16), "seq", scatter_dimension=0, tiled=True
        ).astype(jnp.float32),
        lax.psum_scatter(
            vec_blocks[1].astype(jnp.bfloat16), "seq", scatter_dimension=0, tiled=True
        ).astype(jnp.float32),
        lax.psum_scatter(
            vec_blocks[2].astype(jnp.bfloat16), "seq", scatter_dimension=0, tiled=True
        ).astype(jnp.float32),
        lax.psum_scatter(
            vec_blocks[3].astype(jnp.bfloat16), "seq", scatter_dimension=0, tiled=True
        ).astype(jnp.float32),
        lax.psum_scatter(
            vec_blocks[4].astype(jnp.bfloat16), "seq", scatter_dimension=0, tiled=True
        ).astype(jnp.float32),
        lax.psum_scatter(
            vec_blocks[5].astype(jnp.bfloat16), "seq", scatter_dimension=0, tiled=True
        ).astype(jnp.float32),
        lax.psum_scatter(
            vec_blocks[6].astype(jnp.bfloat16), "seq", scatter_dimension=0, tiled=True
        ).astype(jnp.float32),
        lax.psum_scatter(
            vec_blocks[7].astype(jnp.bfloat16), "seq", scatter_dimension=0, tiled=True
        ).astype(jnp.float32),
        lax.psum_scatter(
            vec_blocks[8].astype(jnp.bfloat16), "seq", scatter_dimension=0, tiled=True
        ).astype(jnp.float32),
    )
    mat_done = (
        lax.psum_scatter(
            reduced[0].astype(jnp.bfloat16), "dp", scatter_dimension=0, tiled=True
        ).astype(jnp.float32),
        lax.psum_scatter(
            reduced[1].astype(jnp.bfloat16), "dp", scatter_dimension=0, tiled=True
        ).astype(jnp.float32),
        lax.psum_scatter(
            reduced[2].astype(jnp.bfloat16), "dp", scatter_dimension=0, tiled=True
        ).astype(jnp.float32),
        lax.psum_scatter(
            reduced[3].astype(jnp.bfloat16), "dp", scatter_dimension=0, tiled=True
        ).astype(jnp.float32),
        lax.psum_scatter(
            reduced[4].astype(jnp.bfloat16), "dp", scatter_dimension=0, tiled=True
        ).astype(jnp.float32),
        lax.psum_scatter(
            reduced[5].astype(jnp.bfloat16), "dp", scatter_dimension=0, tiled=True
        ).astype(jnp.float32),
        lax.psum_scatter(
            reduced[6].astype(jnp.bfloat16), "dp", scatter_dimension=0, tiled=True
        ).astype(jnp.float32),
    )
    vec_part = [reduced[7 + index] for index in range(9)]
    vec_done = lax.psum(
        (
            vec_part[0],
            vec_part[1],
            vec_part[2],
            vec_part[3],
            vec_part[4],
            vec_part[5],
            vec_part[6],
            vec_part[7],
            vec_part[8],
        ),
        "dp",
    )
    mats = [piece.reshape(-1) for piece in mat_done]
    vecs = [piece.reshape(-1) for piece in vec_done]
    return (
        output,
        grad_hidden,
        grad_encoder,
        mats[0],
        vecs[0],
        mats[1],
        vecs[1],
        mats[2],
        vecs[2],
        mats[3],
        vecs[3],
        mats[4],
        vecs[4],
        mats[5],
        vecs[5],
        mats[6],
        vecs[6],
        vecs[7],
        vecs[8],
    )


def on_device(
    hidden,
    encoder_out,
    cotangent,
    dec_lengths,
    enc_lengths,
    self_qkv,
    self_qv_bias,
    self_out,
    self_out_bias,
    rel_weight,
    rel_bias,
    cross_qkv,
    cross_qv_bias,
    cross_out,
    cross_out_bias,
    ffn_in,
    ffn_in_bias,
    ffn_out,
    ffn_out_bias,
    norm_gain,
    norm_bias,
):
    B, S, T, width = hidden.shape
    if T % TILE:
        return plain_on_device(
            hidden,
            encoder_out,
            cotangent,
            dec_lengths,
            enc_lengths,
            self_qkv,
            self_qv_bias,
            self_out,
            self_out_bias,
            rel_weight,
            rel_bias,
            cross_qkv,
            cross_qv_bias,
            cross_out,
            cross_out_bias,
            ffn_in,
            ffn_in_bias,
            ffn_out,
            ffn_out_bias,
            norm_gain,
            norm_bias,
        )
    seq_parts = lax.axis_size("seq")
    keys = T * seq_parts
    far = keys - T
    place = lax.axis_index("seq")
    up = [(i, i + 1) for i in range(seq_parts - 1)]
    down = [(i + 1, i) for i in range(seq_parts - 1)]
    gains, shifts = norm_gain.astype(high_type), norm_bias.astype(high_type)
    self_bias, cross_bias = self_qv_bias.astype(high_type), cross_qv_bias.astype(high_type)
    table = jnp.asarray(bucket_table(), low_type)

    x = hidden.reshape(B * S * T, width)
    rows = B * S * T
    moving, pieces = hidden[:, 0], []
    for _ in range(seq_parts - 1):
        moving = lax.ppermute(moving, "seq", up)
        pieces.append(moving)
    x_all = jnp.concatenate(pieces[::-1] + [hidden.reshape(B, S * T, width)], 1)
    x_keys = x_all.reshape(-1, width)
    key_at = place * T - far + jnp.arange(keys, dtype=jnp.int32)
    self_mark = key_features((key_at >= 0) & (key_at < dec_lengths[:, None]))
    cross_mark = key_features(jnp.arange(keys, dtype=jnp.int32) < enc_lengths[:, None])

    q = ((dot("de,rd->er", self_qkv[0], x) + self_bias[0][:, None]) * SCALE).astype(low_type)
    rel = dot("db,rd->br", rel_weight, x) + rel_bias.astype(high_type)[:, None]
    k = dot("de,rd->er", self_qkv[1], x_keys).astype(low_type)
    v = (dot("de,rd->er", self_qkv[2], x_keys) + self_bias[1][:, None]).astype(low_type)
    attended, self_total = self_forward(q, k, v, rel, self_mark, table, T, S)
    first_sum = (
        x.astype(high_type)
        + dot("er,ed->rd", attended, self_out)
        + self_out_bias.astype(high_type)
    )
    first_unit, _ = norm_parts(first_sum)
    first_norm = first_unit * gains[0] + shifts[0]
    first_low = first_norm.astype(low_type)

    e_all = lax.all_gather(encoder_out, "seq", axis=1, tiled=True).reshape(-1, width)
    qc = ((dot("de,rd->er", cross_qkv[0], first_low) + cross_bias[0][:, None]) * SCALE).astype(
        low_type
    )
    kc = dot("de,rd->er", cross_qkv[1], e_all).astype(low_type)
    vc = (dot("de,rd->er", cross_qkv[2], e_all) + cross_bias[1][:, None]).astype(low_type)
    cross_mixed, cross_total = cross_forward(qc, kc, vc, cross_mark)
    second_sum = (
        first_norm
        + dot("er,ed->rd", cross_mixed, cross_out)
        + cross_out_bias.astype(high_type)
    )
    second_unit, _ = norm_parts(second_sum)
    second_norm = second_unit * gains[1] + shifts[1]
    second_low = second_norm.astype(low_type)

    activated, slope = ffn_first(second_low, ffn_in, ffn_in_bias.astype(high_type)[None])
    third_sum = (
        second_norm + dot("rf,fd->rd", activated, ffn_out) + ffn_out_bias.astype(high_type)
    )
    third_unit, _ = norm_parts(third_sum)
    output = (third_unit * gains[2] + shifts[2]).astype(low_type).reshape(hidden.shape)

    grad_third, grad_gain_ffn, grad_shift_ffn = norm_back(
        third_sum, cotangent.reshape(rows, width).astype(high_type), gains[2]
    )
    grad_ffn = grad_third.astype(low_type)

    def over_dp(piece):
        return lax.psum_scatter(piece.astype(low_type), "dp", scatter_dimension=0, tiled=True)

    def over_seq(piece):
        return (
            lax.psum_scatter(piece, "seq", scatter_dimension=0, tiled=True)
            .astype(high_type)
            .reshape(-1)
        )

    grad_pre = (dot("rd,fd->rf", grad_ffn, ffn_out) * slope.astype(high_type)).astype(low_type)
    mat_ffn_out = over_dp(dot("rf,rd->fd", activated, grad_ffn))
    mat_ffn_in = over_dp(dot("rd,rf->df", second_low, grad_pre))
    grad_second = grad_third + dot("rf,df->rd", grad_pre, ffn_in)
    grad_second_sum, grad_gain_cross, grad_shift_cross = norm_back(
        second_sum, grad_second, gains[1]
    )
    grad_cross = grad_second_sum.astype(low_type)
    mat_cross_out = over_dp(dot("er,rd->ed", cross_mixed, grad_cross))
    grad_cross_mixed = dot("ed,rd->er", cross_out, grad_cross).astype(low_type)
    dqc, dkc, dvc = cross_backward(
        qc, kc, vc, cross_mark, cross_mixed, cross_total, grad_cross_mixed
    )
    grad_encoder = dot("er,de->rd", dkc, cross_qkv[1]) + dot("er,de->rd", dvc, cross_qkv[2])
    grad_encoder = lax.psum_scatter(
        grad_encoder.astype(low_type).reshape(B, keys, width),
        "seq",
        scatter_dimension=1,
        tiled=True,
    )
    mat_cross_qkv = over_dp(
        jnp.concatenate(
            [
                dot("rd,er->de", first_low, dqc),
                dot("rd,er->de", e_all, dkc),
                dot("rd,er->de", e_all, dvc),
            ]
        )
    )
    grad_first = grad_second_sum + dot("er,de->rd", dqc, cross_qkv[0])
    grad_first_sum, grad_gain_self, grad_shift_self = norm_back(first_sum, grad_first, gains[0])
    grad_self = grad_first_sum.astype(low_type)
    mat_self_out = over_dp(dot("er,rd->ed", attended, grad_self))
    grad_attended = dot("ed,rd->er", self_out, grad_self).astype(low_type)
    dq, dk, dv, drel = self_backward(
        q, k, v, rel, self_mark, table, attended, self_total, grad_attended, T, S
    )
    count = far + S * T
    dk_parts, dv_parts = dk.reshape(width, B, count), dv.reshape(width, B, count)
    away = dot("ebr,de->brd", dk_parts[:, :, :far], self_qkv[1]) + dot(
        "ebr,de->brd", dv_parts[:, :, :far], self_qkv[2]
    )
    away = away.astype(low_type)
    moving = away[:, :T]
    for hop in range(1, seq_parts):
        moving = lax.ppermute(moving, "seq", down).astype(high_type)
        if hop < seq_parts - 1:
            moving = (moving + away[:, hop * T : (hop + 1) * T].astype(high_type)).astype(low_type)
    home = (
        grad_first_sum.reshape(B, S * T, width)
        + dot("ebr,de->brd", dq.reshape(width, B, S * T), self_qkv[0])
        + dot("ebr,de->brd", dk_parts[:, :, far:], self_qkv[1])
        + dot("ebr,de->brd", dv_parts[:, :, far:], self_qkv[2])
        + dot("jbr,dj->brd", drel.reshape(-1, B, S * T), rel_weight)
    ).reshape(B, S, T, width)
    mat_self_qkv = over_dp(
        jnp.concatenate(
            [
                dot("rd,er->de", x, dq),
                dot("rd,er->de", x_keys, dk),
                dot("rd,er->de", x_keys, dv),
            ]
        )
    )
    mat_rel = over_dp(dot("rd,jr->dj", x, drel))
    grad_hidden = jnp.concatenate(
        [(home[:, :1] + moving[:, None]).astype(low_type), home[:, 1:].astype(low_type)], 1
    )

    vectors = [
        jnp.stack([row_sum(dq), row_sum(dv)]),
        column_sum(grad_self),
        row_sum(drel),
        jnp.stack([row_sum(dqc), row_sum(dvc)]),
        column_sum(grad_cross),
        column_sum(grad_pre),
        column_sum(grad_ffn),
        jnp.stack([grad_gain_self, grad_gain_cross, grad_gain_ffn]),
        jnp.stack([grad_shift_self, grad_shift_cross, grad_shift_ffn]),
    ]
    blocks = [piece.reshape(seq_parts, -1) for piece in vectors]
    ends = np.cumsum([piece.shape[1] for piece in blocks])
    summed = lax.psum(jnp.concatenate(blocks, 1), ("dp", "seq"))
    mine = lax.dynamic_index_in_dim(summed, place, 0, keepdims=False)
    vecs = [mine[end - piece.shape[1] : end] for piece, end in zip(blocks, ends, strict=True)]
    return (
        output,
        grad_hidden,
        grad_encoder,
        over_seq(mat_self_qkv),
        vecs[0],
        over_seq(mat_self_out),
        vecs[1],
        over_seq(mat_rel),
        vecs[2],
        over_seq(mat_cross_qkv),
        vecs[3],
        over_seq(mat_cross_out),
        vecs[4],
        over_seq(mat_ffn_in),
        vecs[5],
        over_seq(mat_ffn_out),
        vecs[6],
        vecs[7],
        vecs[8],
    )


def solution(mesh):
    rows, vector, matrix = P("dp", None, "seq", None), P("seq"), P(("dp", "seq"))
    return jax.shard_map(
        on_device,
        mesh=mesh,
        in_specs=(rows, P("dp", "seq", None), rows, P("dp"), P("dp")) + (P(),) * 16,
        out_specs=(rows, rows, P("dp", "seq", None))
        + (matrix, vector) * 7
        + (vector, vector),
        check_vma=False,
    )
```

```python
import functools
import math

import jax
import jax.numpy as jnp
import numpy as np
from jax import lax
from jax.experimental import pallas as pl
from jax.experimental.pallas import tpu as pltpu
from jax.sharding import PartitionSpec as P

HEADS = 16
BUCKETS = 32
MAX_DIST = 128
SIZE = 64
SCALE = 0.125
TILE = 128
NEGATIVE = -1e30
EPSILON = 1e-05
VMEM_LIMIT = 56 * 2**20

low_type = jnp.bfloat16
high_type = jnp.float32


def contract(left, right, left_dim, right_dim):
    return lax.dot_general(
        left, right, (((left_dim,), (right_dim,)), ((), ())), preferred_element_type=high_type
    )


def split_two(value):
    top = value.astype(low_type)
    return top, (value - top.astype(high_type)).astype(low_type)


def feature_rows(first, value):
    a = value.astype(low_type).astype(high_type)
    b = (value - a).astype(low_type).astype(high_type)
    c = value - a - b
    count = value.shape[1]
    at = lax.broadcasted_iota(jnp.int32, (16, count), 0)
    out = jnp.where(at == 0, first, 0.0)
    for index, piece in enumerate((a, b, c)):
        out = jnp.where(at == index + 1, piece, out)
    return out.astype(low_type)


def key_features(valid):
    mask = jnp.where(valid, 0.0, NEGATIVE)[:, None, :]
    ones = jnp.ones_like(mask)
    return jnp.concatenate([mask, ones, ones, ones] + [jnp.zeros_like(mask)] * 12, 1).astype(
        low_type
    )


def bucket_table():
    half = BUCKETS // 2
    distance = (TILE - np.arange(2 * TILE)) % (2 * TILE)
    counted = np.zeros_like(distance)
    for level in range(1, half):
        counted = counted + (distance >= math.ceil(half * (MAX_DIST / half) ** (level / half)))
    bucket = np.where(distance < half, distance, half + counted)
    table = (bucket[None, :] == np.arange(BUCKETS)[:, None]).astype(np.float32)
    table[BUCKETS - 1] = -(bucket < BUCKETS - 1).astype(np.float32)
    return table


def near_bias(rel, table):
    top, rest = split_two(rel)
    return contract(
        jnp.concatenate([top, rest], 0), jnp.concatenate([table, table], 0), 0, 0
    )


def cross_forward_kernel(q_ref, k_ref, v_ref, mark_ref, o_ref, total_ref):
    count, keys = q_ref.shape[1], k_ref.shape[1]
    k1 = jnp.concatenate([k_ref[...], mark_ref[...]], 0)
    v1 = jnp.concatenate([v_ref[...], jnp.ones((16, keys), low_type)], 0)
    zero = jnp.zeros((1, count), high_type)
    q1 = jnp.concatenate([q_ref[...], feature_rows(1.0, zero)], 0)
    scores = contract(k1, q1, 0, 0)
    peak = jnp.max(scores, 0, keepdims=True)
    weights = jnp.exp(scores - peak).astype(low_type)
    mixed = contract(v1, weights, 1, 0)
    total = mixed[SIZE : SIZE + 1]
    o_ref[...] = (mixed[:SIZE] * (1.0 / total)).astype(low_type)
    total_ref[...] = peak + jnp.log(total)


def cross_backward_kernel(
    q_ref, k_ref, v_ref, mark_ref, o_ref, total_ref, do_ref, dq_ref, dk_ref, dv_ref, dk_acc, dv_acc, *, step
):
    count, keys = q_ref.shape[1], k_ref.shape[1]
    k = k_ref[...]
    k1 = jnp.concatenate([k, mark_ref[...]], 0)
    v1 = jnp.concatenate([v_ref[...], mark_ref[...]], 0)
    for n in range(0, count, step):
        q, do = q_ref[:, n : n + step], do_ref[:, n : n + step]
        delta = jnp.sum(
            do.astype(high_type) * o_ref[:, n : n + step].astype(high_type), 0, keepdims=True
        )
        q1 = jnp.concatenate([q, feature_rows(1.0, -total_ref[:, n : n + step])], 0)
        do1 = jnp.concatenate([do, feature_rows(0.0, -delta)], 0)
        weights = jnp.exp(contract(q1, k1, 0, 0))
        grad_scores = (weights * contract(do1, v1, 0, 0)).astype(low_type)
        weights = weights.astype(low_type)
        dq_ref[:, n : n + step] = (contract(k, grad_scores, 1, 1) * SCALE).astype(low_type)
        dk = contract(q, grad_scores, 1, 0)
        dv = contract(do, weights, 1, 0)
        if n == 0:
            dk_acc[...] = dk
            dv_acc[...] = dv
        else:
            dk_acc[...] += dk
            dv_acc[...] += dv
    dk_ref[...] = dk_acc[...].astype(low_type)
    dv_ref[...] = dv_acc[...].astype(low_type)


def near_biases(rel, table):
    near = near_bias(rel, table)
    return [
        pltpu.roll(near[row : row + TILE], 0, 1, stride=1, stride_axis=0)
        for row in range(0, near.shape[0], TILE)
    ]


def main_and_own(far_ref, near_ref, T):
    near = near_ref[...]
    return jnp.concatenate([far_ref[...], near[:, :T]], 1), near[:, T:]


def near_window(block, bias, first, main_row):
    at = lax.broadcasted_iota(jnp.int32, (TILE, TILE), 0)
    to = lax.broadcasted_iota(jnp.int32, (TILE, TILE), 1)
    left = block[:, first : first + TILE] + bias[:, :TILE]
    right = block[:, first + TILE : first + 2 * TILE] + bias[:, TILE:]
    return left, jnp.where((to <= at) if main_row else (to < at), right, NEGATIVE)


def self_forward_kernel(*refs, T, S):
    q_ref, k_ref, v_ref, k_far_ref, v_far_ref, rel_ref, mark_ref, table_ref = refs[:8]
    o_ref, total_ref = refs[-2:]
    n, keys = S * T, k_far_ref.shape[1] + T
    q, rel = q_ref[...], rel_ref[...]
    k, own_k = main_and_own(k_far_ref, k_ref, T)
    v, own_v = main_and_own(v_far_ref, v_ref, T)
    biases = near_biases(rel, table_ref[...])
    k1 = jnp.concatenate([k, mark_ref[...]], 0)
    v1 = jnp.concatenate([v, jnp.ones((16, keys), low_type)], 0)
    q1 = jnp.concatenate([q, feature_rows(1.0, rel[BUCKETS - 1 :])], 0)
    scores = contract(q1, k1, 0, 0)
    weights, peaks = [], []
    for s in range(S):
        for r in range(T // TILE):
            row, first = s * T + r * TILE, keys - T + (r - 1) * TILE
            block = scores[row : row + TILE]
            left, right = near_window(block, biases[row // TILE], first, s == 0)
            parts = [left, right]
            peak = jnp.max(jnp.maximum(left, right), 1, keepdims=True)
            if first > 0:
                far = block[:, :first]
                peak = jnp.maximum(peak, jnp.max(far, 1, keepdims=True))
                parts = [far] + parts
            parts = [jnp.exp(part - peak).astype(low_type) for part in parts]
            if first + 2 * TILE < keys:
                parts.append(jnp.zeros((TILE, keys - first - 2 * TILE), low_type))
            weights.append(jnp.concatenate(parts, 1))
            peaks.append(jnp.broadcast_to(peak, (TILE, TILE)).T[0:1])
    mixed = contract(v1, jnp.concatenate(weights, 0), 1, 1)
    peak = jnp.concatenate(peaks, 1)
    total, mixed = mixed[SIZE : SIZE + 1], mixed[:SIZE]
    own_k, own_v = own_k.astype(high_type), own_v.astype(high_type)
    own = jnp.sum(q[:, T:].astype(high_type) * own_k, 0, keepdims=True) + rel[0:1, T:]
    top = jnp.maximum(peak[:, T:], own)
    main_part, own_part = jnp.exp(peak[:, T:] - top), jnp.exp(own - top)
    joined = total[:, T:] * main_part + own_part
    inverse = 1.0 / joined
    o_ref[:, :T] = (mixed[:, :T] * (1.0 / total[:, :T])).astype(low_type)
    o_ref[:, T:] = (mixed[:, T:] * (main_part * inverse) + own_v * (own_part * inverse)).astype(
        low_type
    )
    total_ref[:, :T] = peak[:, :T] + jnp.log(total[:, :T])
    total_ref[:, T:] = top + jnp.log(joined)


def self_backward_kernel(*refs, T, S):
    q_ref, k_ref, v_ref, k_far_ref, v_far_ref, rel_ref, mark_ref, table_ref = refs[:8]
    o_ref, total_ref, do_ref = refs[8:11]
    dq_ref, dkv_ref, drel_ref, far_ref = refs[-4:]
    n, keys = S * T, k_far_ref.shape[1] + T
    far = keys - T
    q, rel, do, total = q_ref[...], rel_ref[...], do_ref[...], total_ref[...]
    table = table_ref[...]
    k, own_k = main_and_own(k_far_ref, k_ref, T)
    v, own_v = main_and_own(v_far_ref, v_ref, T)
    biases = near_biases(rel, table)
    k1 = jnp.concatenate([k, mark_ref[...]], 0)
    v1 = jnp.concatenate([v, mark_ref[...]], 0)
    do_high = do.astype(high_type)
    delta = jnp.sum(do_high * o_ref[...].astype(high_type), 0, keepdims=True)
    q1 = jnp.concatenate([q, feature_rows(1.0, rel[BUCKETS - 1 :] - total)], 0)
    do1 = jnp.concatenate([do, feature_rows(0.0, -delta)], 0)
    scores = contract(q1, k1, 0, 0)
    slopes = contract(do1, v1, 0, 0)
    weights, grads, nears = [], [], []
    for s in range(S):
        for r in range(T // TILE):
            row, first = s * T + r * TILE, keys - T + (r - 1) * TILE
            block, slope = scores[row : row + TILE], slopes[row : row + TILE]
            part = jnp.exp(
                jnp.concatenate(near_window(block, biases[row // TILE], first, s == 0), 1)
            )
            grad = (part * slope[:, first : first + 2 * TILE]).astype(low_type)
            nears.append(grad)
            parts, pieces = [part.astype(low_type)], [grad]
            if first > 0:
                part = jnp.exp(block[:, :first])
                pieces = [(part * slope[:, :first]).astype(low_type)] + pieces
                parts = [part.astype(low_type)] + parts
            if first + 2 * TILE < keys:
                zero = jnp.zeros((TILE, keys - first - 2 * TILE), low_type)
                parts.append(zero)
                pieces.append(zero)
            weights.append(jnp.concatenate(parts, 1))
            grads.append(jnp.concatenate(pieces, 1))
    weights, grads = jnp.concatenate(weights, 0), jnp.concatenate(grads, 0)
    dq = contract(k1, grads, 1, 1)
    dk = contract(q, grads, 1, 0).astype(low_type)
    dv = contract(do, weights, 1, 0).astype(low_type)
    far_ref[0] = dk[:, :far]
    far_ref[1] = dv[:, :far]
    at = lax.broadcasted_iota(jnp.int32, (TILE, TILE), 0)
    to = lax.broadcasted_iota(jnp.int32, (TILE, TILE), 1)
    mirror = (at + to == TILE - 1).astype(high_type).astype(low_type)
    flipped = contract(mirror, jnp.concatenate(nears, 1), 1, 0)
    turned = [
        pltpu.roll(flipped[:, i : i + 2 * TILE], TILE + 1, 1, stride=1, stride_axis=0).astype(low_type)
        for i in range(0, 2 * n, 2 * TILE)
    ]
    top, rest = split_two(contract(table, jnp.concatenate(turned, 0), 1, 1))
    stacked = [part[:, i : i + TILE] for i in range(0, n, TILE) for part in (top, rest)]
    both = contract(jnp.concatenate(stacked, 0), mirror, 1, 0)
    rels = [
        both[i : i + BUCKETS] + both[i + BUCKETS : i + 2 * BUCKETS]
        for i in range(0, both.shape[0], 2 * BUCKETS)
    ]
    row_sums = dq[SIZE + 1 : SIZE + 2]
    own_k, own_v = own_k.astype(high_type), own_v.astype(high_type)
    own_q, own_do = q[:, T:].astype(high_type), do_high[:, T:]
    own = jnp.sum(own_q * own_k, 0, keepdims=True) + rel[0:1, T:]
    own_part = jnp.exp(own - total[:, T:])
    own_grad = own_part * (jnp.sum(own_do * own_v, 0, keepdims=True) - delta[:, T:])
    own_grad = own_grad.astype(low_type).astype(high_type)
    dq_ref[:, :T] = (dq[:SIZE, :T] * SCALE).astype(low_type)
    dq_ref[:, T:] = ((dq[:SIZE, T:] + own_grad * own_k) * SCALE).astype(low_type)
    dkv_ref[0, :, :T] = dk[:, far:]
    dkv_ref[1, :, :T] = dv[:, far:]
    dkv_ref[0, :, T:] = (own_grad * own_q).astype(low_type)
    dkv_ref[1, :, T:] = (own_part.astype(low_type).astype(high_type) * own_do).astype(low_type)
    bucket = lax.broadcasted_iota(jnp.int32, (BUCKETS, n), 0)
    drel = jnp.concatenate(rels, 1) + jnp.where(bucket == BUCKETS - 1, row_sums, 0.0)
    own_all = jnp.concatenate([jnp.zeros((1, T), high_type), own_grad], 1)
    drel_ref[...] = (drel + jnp.where(bucket == 0, own_all, 0.0)).astype(low_type)


def weight_grads_kernel(*refs, sources, terms, parts, sums):
    xs, rest = refs[: len(sources)], refs[len(sources) :]
    turned = rest[-1]
    count = max(place for step in terms for place, _ in step) + 1
    gs, out_ref = rest[:count], rest[count]
    e, c = pl.program_id(0), pl.program_id(1)

    @pl.when((e == 0) & (c == 0))
    def _():
        start = 0
        for x_ref, rows in zip(xs, sources, strict=True):
            turned[:, start : start + rows] = x_ref[...].T
            start += rows

    for step, term in enumerate(terms):

        @pl.when(c == step)
        def _():
            total = None
            for place, (low_at, high_at) in term:
                g = gs[place][...]
                piece = contract(turned[:, low_at:high_at], g, 1, 1)
                total = piece if total is None else total + piece
                if sums[step]:
                    line = contract(jnp.ones((8, high_at - low_at), low_type), g, 1, 1)
                    held = line if place == term[0][0] else held + line
            if sums[step]:
                rest[count + 1][step] = held
            total = total.astype(low_type)
            for at, row, rows, halves in parts[step]:
                if halves:
                    kept = jnp.where(e < halves, total[row : row + rows], total[row + rows : row + 2 * rows])
                else:
                    kept = total[row : row + rows]
                out_ref[at[0], at[1] : at[1] + rows, :] = kept


def back_rows_kernel(*refs, pairs, base, joined):
    gs, ws, rest = refs[:pairs], refs[pairs : 2 * pairs], refs[2 * pairs :]
    turned = rest[-pairs:]
    out_ref = rest[-pairs - 1]

    @pl.when(pl.program_id(1) == 0)
    def _():
        for g_ref, t_ref in zip(gs, turned, strict=True):
            t_ref[...] = g_ref[...].T

    total = rest[0][...] if base else None
    for t_ref, w_ref in zip(turned, ws, strict=True):
        piece = contract(t_ref[...], w_ref[...], 1, 1)
        total = piece if total is None else total + piece
    if joined:
        add = rest[1][...]
        out_ref[: add.shape[0]] = (total[: add.shape[0]] + add).astype(low_type)
        out_ref[add.shape[0] :] = total[add.shape[0] :].astype(low_type)
    else:
        out_ref[...] = total.astype(low_type)


def per_head(rows, count):
    return pl.BlockSpec((rows, count), lambda b, h: (h, b))


def per_sequence(keys):
    return pl.BlockSpec((None, 16, keys), lambda b, h: (b, 0, 0))


def per_total(count):
    return pl.BlockSpec((None, None, 1, count), lambda b, h: (b, h, 0, 0))


def like(array):
    return jax.ShapeDtypeStruct(array.shape, low_type)


def cost(B, rows, keys, products):
    return pl.CostEstimate(
        flops=2 * B * HEADS * rows * keys * 256 * products,
        bytes_accessed=B * HEADS * SIZE * (rows + keys) * 4 * products,
        transcendentals=B * HEADS * rows * keys,
    )


def cross_forward(q, k, v, mark):
    B, _, keys = mark.shape
    count = q.shape[1] // B
    return pl.pallas_call(
        cross_forward_kernel,
        grid=(B, HEADS),
        in_specs=[per_head(SIZE, count), per_head(SIZE, keys), per_head(SIZE, keys), per_sequence(keys)],
        out_specs=[per_head(SIZE, count), per_total(count)],
        out_shape=[like(q), jax.ShapeDtypeStruct((B, HEADS, 1, count), high_type)],
        cost_estimate=cost(B, count, keys, 2),
        compiler_params=pltpu.CompilerParams(vmem_limit_bytes=VMEM_LIMIT),
        name="cross_forward",
    )(q, k, v, mark)


def cross_backward(q, k, v, mark, o, total, do):
    B, _, keys = mark.shape
    count = q.shape[1] // B
    row, key = per_head(SIZE, count), per_head(SIZE, keys)
    return pl.pallas_call(
        functools.partial(cross_backward_kernel, step=count // 2),
        grid=(B, HEADS),
        in_specs=[row, key, key, per_sequence(keys), row, per_total(count), row],
        out_specs=[row, key, key],
        out_shape=[like(q), like(k), like(v)],
        scratch_shapes=[pltpu.VMEM((SIZE, keys), high_type)] * 2,
        cost_estimate=cost(B, count, keys, 5),
        compiler_params=pltpu.CompilerParams(vmem_limit_bytes=VMEM_LIMIT),
        name="cross_backward",
    )(q, k, v, mark, o, total, do)


def self_call(body, b, inputs, more, earlier, T, S, outs, out_specs, products, name):
    q, far, mark, table = inputs[0], inputs[3].shape[1], inputs[6], inputs[7]
    count = S * T
    row = pl.BlockSpec((SIZE, count), lambda h: (h, b))
    far_row = pl.BlockSpec((SIZE, far), lambda h: (h, 0))
    total = pl.BlockSpec((None, None, 1, count), lambda h: (b, h, 0, 0))
    specs = [row, row, row, far_row, far_row, pl.BlockSpec((BUCKETS, count), lambda h: (h, b))]
    specs.append(pl.BlockSpec((None, 16, far + T), lambda h: (b, 0, 0)))
    specs.append(pl.BlockSpec(table.shape, lambda h: (0, 0)))
    specs += [row, total, row][: len(more)]
    held = len(specs)
    return pl.pallas_call(
        functools.partial(body, T=T, S=S),
        grid=(HEADS,),
        in_specs=specs + [pl.BlockSpec(memory_space=pl.ANY)] * len(earlier),
        out_specs=out_specs,
        out_shape=outs,
        input_output_aliases={held + i: i for i in range(len(earlier))},
        cost_estimate=cost(1, count, far + T, products),
        compiler_params=pltpu.CompilerParams(vmem_limit_bytes=VMEM_LIMIT),
        name=name,
    )(*inputs, *more, *earlier)


def self_forward(b, inputs, earlier, T, S):
    q, mark, count = inputs[0], inputs[6], S * T
    return self_call(
        self_forward_kernel,
        b,
        inputs,
        (),
        earlier,
        T,
        S,
        [like(q), jax.ShapeDtypeStruct((mark.shape[0], HEADS, 1, count), high_type)],
        [
            pl.BlockSpec((SIZE, count), lambda h: (h, b)),
            pl.BlockSpec((None, None, 1, count), lambda h: (b, h, 0, 0)),
        ],
        2,
        "self_forward",
    )


def self_backward(b, inputs, more, earlier, T, S):
    q, rel, count, far = inputs[0], inputs[5], S * T, inputs[3].shape[1]

    def pair(columns):
        return jax.ShapeDtypeStruct((2, q.shape[0], columns), low_type)

    return self_call(
        self_backward_kernel,
        b,
        inputs,
        more,
        earlier,
        T,
        S,
        [like(q), pair(q.shape[1]), like(rel), pair(far)],
        [
            pl.BlockSpec((SIZE, count), lambda h: (h, b)),
            pl.BlockSpec((2, SIZE, count), lambda h: (0, h, b)),
            pl.BlockSpec((BUCKETS, count), lambda h: (h, b)),
            pl.BlockSpec((2, SIZE, far), lambda h: (0, h, 0)),
        ],
        5,
        "self_backward",
    )


def weight_grads(xs, gs, specs, terms, parts, sums, out, name):
    width = xs[0].shape[1]
    columns = out[2] // 4
    sources = [x.shape[0] for x in xs]
    outs = [jax.ShapeDtypeStruct(out, low_type)]
    out_specs = [pl.BlockSpec((out[0], out[1], columns), lambda e, c: (0, 0, e))]
    if any(sums):
        outs.append(jax.ShapeDtypeStruct((len(terms), 8, out[2]), high_type))
        out_specs.append(pl.BlockSpec((len(terms), 8, columns), lambda e, c: (0, 0, e)))
    flops = sum(2 * width * out[2] * (b - a) for term in terms for _, (a, b) in term)
    return pl.pallas_call(
        functools.partial(
            weight_grads_kernel, sources=sources, terms=terms, parts=parts, sums=sums
        ),
        grid=(4, len(terms)),
        in_specs=[pl.BlockSpec(x.shape, lambda e, c: (0, 0)) for x in xs] + specs,
        out_specs=out_specs,
        out_shape=outs,
        scratch_shapes=[pltpu.VMEM((width, sum(sources)), low_type)],
        cost_estimate=pl.CostEstimate(
            flops=flops, bytes_accessed=2 * width * (sum(sources) * 2 + out[2]), transcendentals=0
        ),
        compiler_params=pltpu.CompilerParams(vmem_limit_bytes=VMEM_LIMIT),
        name=name,
    )(*xs, *gs)


def back_rows(gs, ws, base, joined, tile, name):
    width, columns = 1024, 256

    def spec(entry, shape, index):
        if isinstance(entry, tuple):
            return pl.BlockSpec((None,) + shape, lambda r, d, w=entry[1]: (w,) + index(r, d))
        return pl.BlockSpec(shape, index)

    arrays = [e[0] if isinstance(e, tuple) else e for e in gs]
    weights = [e[0] if isinstance(e, tuple) else e for e in ws]
    rows = arrays[0].shape[-1]
    sizes = [a.shape[-2] for a in arrays]
    specs = [spec(e, (f, tile), lambda r, d: (0, r)) for e, f in zip(gs, sizes, strict=True)]
    specs += [spec(e, (columns, f), lambda r, d: (d, 0)) for e, f in zip(ws, sizes, strict=True)]
    extra = []
    if base is not None:
        specs.append(pl.BlockSpec((tile, columns), lambda r, d: (r, d)))
        extra.append(base)
    if joined is not None:
        specs.append(pl.BlockSpec((joined.shape[0] * tile // rows, columns), lambda r, d: (r, d)))
        extra.append(joined)
    return pl.pallas_call(
        functools.partial(
            back_rows_kernel, pairs=len(gs), base=base is not None, joined=joined is not None
        ),
        grid=(rows // tile, width // columns),
        in_specs=specs,
        out_specs=pl.BlockSpec((tile, columns), lambda r, d: (r, d)),
        out_shape=jax.ShapeDtypeStruct((rows, width), low_type),
        scratch_shapes=[pltpu.VMEM((tile, f), low_type) for f in sizes],
        cost_estimate=pl.CostEstimate(
            flops=2 * rows * width * sum(sizes),
            bytes_accessed=2 * (rows + width) * sum(sizes) + 6 * rows * width,
            transcendentals=0,
        ),
        compiler_params=pltpu.CompilerParams(vmem_limit_bytes=VMEM_LIMIT),
        name=name,
    )(*arrays, *weights, *extra)


def ffn_kernel(x_ref, w_ref, b_ref, g_ref, slope_ref):
    u = contract(x_ref[...], w_ref[...], 1, 0) + b_ref[...]
    z = jnp.abs(u) * (0.5**0.5)
    t = 1.0 / (1.0 + 0.3275911 * z)
    bell = jnp.exp(-z * z)
    poly = t * (
        0.254829592
        + t * (-0.284496736 + t * (1.421413741 + t * (-1.453152027 + t * 1.061405429)))
    )
    tail = 0.5 * poly * bell
    phi = jnp.where(u < 0.0, tail, 1.0 - tail)
    g_ref[...] = (u * phi).astype(low_type)
    slope_ref[...] = (phi + u * (bell * (2.0 * math.pi) ** -0.5)).astype(low_type)


def ffn_first(x, w, b):
    rows, width = x.shape
    hidden = w.shape[1]
    tm, tn = math.gcd(rows, 512), math.gcd(hidden, 1024)
    block = pl.BlockSpec((tm, tn), lambda j, i: (i, j))
    out = jax.ShapeDtypeStruct((rows, hidden), low_type)
    return pl.pallas_call(
        ffn_kernel,
        grid=(hidden // tn, rows // tm),
        in_specs=[
            pl.BlockSpec((tm, width), lambda j, i: (i, 0)),
            pl.BlockSpec((width, tn), lambda j, i: (0, j)),
            pl.BlockSpec((1, tn), lambda j, i: (0, j)),
        ],
        out_specs=[block, block],
        out_shape=[out, out],
        cost_estimate=pl.CostEstimate(
            flops=2 * rows * width * hidden, bytes_accessed=4 * rows * hidden, transcendentals=rows * hidden
        ),
        compiler_params=pltpu.CompilerParams(vmem_limit_bytes=VMEM_LIMIT),
        name="ffn_first",
    )(x, w, b)


def column_sum(value):
    return jnp.sum(value.astype(high_type), 0)


def row_sum(value):
    return jnp.sum(value.astype(high_type), 1)


def dot(spec, left, right):
    return jnp.einsum(spec, left, right, preferred_element_type=high_type)


def norm_parts(value):
    center = value - jnp.mean(value, -1, keepdims=True)
    inverse = lax.rsqrt(jnp.mean(center * center, -1, keepdims=True) + EPSILON)
    return center * inverse, inverse


def norm_back(value, grad, gain):
    unit, inverse = norm_parts(value)
    scaled = grad * gain
    back = inverse * (
        scaled
        - jnp.mean(scaled, -1, keepdims=True)
        - unit * jnp.mean(scaled * unit, -1, keepdims=True)
    )
    return back, jnp.sum(grad * unit, 0), jnp.sum(grad, 0)


def rounded(value):
    return lax.optimization_barrier(value.astype(jnp.bfloat16)).astype(jnp.float32)


def layer_norm(value, gain, shift):
    center = value - jnp.mean(value, -1, keepdims=True)
    spread = jnp.mean(center * center, -1, keepdims=True)
    return center * lax.rsqrt(spread + EPSILON) * gain + shift


def gelu_exact(value):
    return jax.nn.gelu(value, approximate=False)


def bucket_of(distance):
    half = BUCKETS // 2
    counted = jnp.zeros_like(distance)
    for level in range(1, half):
        bound = math.ceil(half * (MAX_DIST / half) ** (level / half))
        counted = counted + (distance >= bound).astype(jnp.int32)
    return jnp.where(distance < half, distance, half + counted)


def self_logits(query_s, key_s, rel_s, keys_s, dec_len, offset_pos):
    streams, local_len, heads, size = query_s.shape
    full_len = keys_s.shape[0]
    scale = size ** (-0.5)
    positions = offset_pos + jnp.arange(local_len, dtype=jnp.int32)
    key_positions = jnp.arange(full_len, dtype=jnp.int32)
    distance = positions[:, None] - key_positions[None, :]
    one_hot = (
        bucket_of(jnp.maximum(distance, 0))[:, :, None] == jnp.arange(BUCKETS, dtype=jnp.int32)
    ).astype(jnp.float32)
    scores = scale * jnp.einsum(
        "sqhd,khd->shqk", query_s, keys_s, preferred_element_type=jnp.float32
    )
    scores = scores + jnp.einsum("sqhb,qkb->shqk", rel_s, one_hot, precision=lax.Precision.HIGHEST)
    stream_ids = jnp.arange(streams, dtype=jnp.int32)
    allowed = (distance[None] >= jnp.minimum(stream_ids, 1)[:, None, None]) & (
        key_positions < dec_len
    )[None, None, :]
    scores = jnp.where(allowed[:, None], scores, NEGATIVE)
    own_score = (
        scale * jnp.sum(query_s.astype(jnp.float32) * key_s.astype(jnp.float32), -1) + rel_s[..., 0]
    )
    own_score = jnp.where(
        (stream_ids > 0)[:, None, None], jnp.transpose(own_score, (0, 2, 1)), NEGATIVE
    )
    return (scores, own_score, one_hot)


def plain_self_forward(items, offset_pos):
    query_s, key_s, value_s, rel_s, keys_s, values_s, dec_len = items
    scores, own_score, one_hot = self_logits(query_s, key_s, rel_s, keys_s, dec_len, offset_pos)
    peak = jnp.maximum(jnp.max(scores, -1), own_score)
    log_total = peak + jnp.log(
        jnp.sum(jnp.exp(scores - peak[..., None]), -1) + jnp.exp(own_score - peak)
    )
    weights = jnp.exp(scores - log_total[..., None]).astype(jnp.bfloat16)
    own_weight = rounded(jnp.exp(own_score - log_total))
    mixed = jnp.einsum("shqk,khd->sqhd", weights, values_s, preferred_element_type=jnp.float32)
    mixed = mixed + jnp.transpose(own_weight, (0, 2, 1))[..., None] * value_s.astype(jnp.float32)
    return (mixed.astype(jnp.bfloat16), log_total)


def plain_self_backward(items, offset_pos):
    query_s, key_s, value_s, rel_s, keys_s, values_s, dec_len, log_total, grad_s = items
    scores, own_score, one_hot = self_logits(query_s, key_s, rel_s, keys_s, dec_len, offset_pos)
    scale = query_s.shape[3] ** (-0.5)
    weights = jnp.exp(scores - log_total[..., None])
    own_weight = jnp.exp(own_score - log_total)
    grad_float = grad_s.astype(jnp.float32)
    grad_weights = jnp.einsum(
        "sqhd,khd->shqk", grad_s, values_s, preferred_element_type=jnp.float32
    )
    grad_own = jnp.transpose(jnp.sum(grad_float * value_s.astype(jnp.float32), -1), (0, 2, 1))
    delta = jnp.sum(grad_weights * weights, -1) + grad_own * own_weight
    grad_scores = (weights * (grad_weights - delta[..., None])).astype(jnp.bfloat16)
    grad_own_score = rounded(own_weight * (grad_own - delta))
    own_term = jnp.transpose(grad_own_score, (0, 2, 1))[..., None]
    grad_query = scale * (
        jnp.einsum("shqk,khd->sqhd", grad_scores, keys_s, preferred_element_type=jnp.float32)
        + own_term * key_s.astype(jnp.float32)
    )
    grad_keys = scale * jnp.einsum(
        "shqk,sqhd->khd", grad_scores, query_s, preferred_element_type=jnp.float32
    )
    grad_key_own = scale * own_term * query_s.astype(jnp.float32)
    grad_values = jnp.einsum(
        "shqk,sqhd->khd", weights.astype(jnp.bfloat16), grad_s, preferred_element_type=jnp.float32
    )
    grad_value_own = jnp.transpose(rounded(own_weight), (0, 2, 1))[..., None] * grad_float
    grad_rel = jnp.einsum(
        "shqk,qkb->sqhb", grad_scores.astype(jnp.float32), one_hot, precision=lax.Precision.HIGHEST
    )
    grad_rel = grad_rel.at[..., 0].add(jnp.transpose(grad_own_score, (0, 2, 1)))
    return (grad_query, grad_key_own, grad_value_own, grad_keys, grad_values, grad_rel)


def cross_logits(query_s, keys_s, enc_len):
    scale = query_s.shape[3] ** (-0.5)
    scores = scale * jnp.einsum(
        "sqhd,khd->shqk", query_s, keys_s, preferred_element_type=jnp.float32
    )
    key_positions = jnp.arange(keys_s.shape[0], dtype=jnp.int32)
    return jnp.where(key_positions < enc_len, scores, NEGATIVE)


def plain_cross_forward(items):
    query_s, keys_s, values_s, enc_len = items
    scores = cross_logits(query_s, keys_s, enc_len)
    peak = jnp.max(scores, -1)
    log_total = peak + jnp.log(jnp.sum(jnp.exp(scores - peak[..., None]), -1))
    weights = jnp.exp(scores - log_total[..., None]).astype(jnp.bfloat16)
    mixed = jnp.einsum("shqk,khd->sqhd", weights, values_s, preferred_element_type=jnp.float32)
    return (mixed.astype(jnp.bfloat16), log_total)


def plain_cross_backward(items):
    query_s, keys_s, values_s, enc_len, log_total, grad_s = items
    scale = query_s.shape[3] ** (-0.5)
    scores = cross_logits(query_s, keys_s, enc_len)
    weights = jnp.exp(scores - log_total[..., None])
    grad_weights = jnp.einsum(
        "sqhd,khd->shqk", grad_s, values_s, preferred_element_type=jnp.float32
    )
    delta = jnp.sum(grad_weights * weights, -1)
    grad_scores = (weights * (grad_weights - delta[..., None])).astype(jnp.bfloat16)
    grad_query = scale * jnp.einsum(
        "shqk,khd->sqhd", grad_scores, keys_s, preferred_element_type=jnp.float32
    )
    grad_keys = scale * jnp.einsum(
        "shqk,sqhd->khd", grad_scores, query_s, preferred_element_type=jnp.float32
    )
    grad_values = jnp.einsum(
        "shqk,sqhd->khd", weights.astype(jnp.bfloat16), grad_s, preferred_element_type=jnp.float32
    )
    return (grad_query, grad_keys, grad_values)


def plain_on_device(
    hidden,
    encoder_out,
    cotangent,
    dec_lengths,
    enc_lengths,
    self_qkv,
    self_qv_bias,
    self_out,
    self_out_bias,
    rel_weight,
    rel_bias,
    cross_qkv,
    cross_qv_bias,
    cross_out,
    cross_out_bias,
    ffn_in,
    ffn_in_bias,
    ffn_out,
    ffn_out_bias,
    norm_gain,
    norm_bias,
):
    seq_count, streams, local_len, width = hidden.shape
    seq_parts = lax.axis_size("seq")
    dp_parts = lax.axis_size("dp")
    full_len = local_len * seq_parts
    offset_pos = lax.axis_index("seq") * local_len
    heads = HEADS
    size = width // heads
    head_shape = (seq_count, streams, local_len, heads, size)
    all_shape = (seq_count, full_len, heads, size)
    kv_shape = (seq_count, full_len, width)
    rows = hidden.reshape(-1, width)
    row_count = rows.shape[0]
    gains = norm_gain.astype(high_type)
    shifts = norm_bias.astype(high_type)
    self_bias = self_qv_bias.astype(high_type)
    cross_bias = cross_qv_bias.astype(high_type)
    projected = jnp.einsum("rd,cde->cre", rows, self_qkv, preferred_element_type=high_type)
    query = (projected[0] + self_bias[0]).astype(low_type)
    key = projected[1].astype(low_type)
    value = (projected[2] + self_bias[1]).astype(low_type)
    rel_logits = jnp.dot(rows, rel_weight, preferred_element_type=high_type) + rel_bias.astype(
        high_type
    )
    rel_heads = rel_logits.reshape(seq_count, streams, local_len, heads, BUCKETS)
    key_main = key.reshape(seq_count, streams, local_len, width)[:, 0]
    value_main = value.reshape(seq_count, streams, local_len, width)[:, 0]
    keys_all, values_all = (
        lax.all_gather(key_main, "seq", axis=1, tiled=True),
        lax.all_gather(value_main, "seq", axis=1, tiled=True),
    )
    self_items = (
        query.reshape(head_shape),
        key.reshape(head_shape),
        value.reshape(head_shape),
        rel_heads,
        keys_all.reshape(all_shape),
        values_all.reshape(all_shape),
        dec_lengths,
    )
    attended, self_total = lax.map(lambda items: plain_self_forward(items, offset_pos), self_items)
    attended = attended.reshape(row_count, width)
    self_branch = jnp.dot(
        attended, self_out, preferred_element_type=high_type
    ) + self_out_bias.astype(high_type)
    first_sum = rows.astype(high_type) + self_branch
    first_norm = layer_norm(first_sum, gains[0], shifts[0])
    first_low = first_norm.astype(low_type)
    cross_query = (
        jnp.dot(first_low, cross_qkv[0], preferred_element_type=high_type) + cross_bias[0]
    ).astype(low_type)
    encoder_rows = encoder_out.reshape(-1, width)
    encoder_proj = jnp.einsum(
        "rd,cde->cre", encoder_rows, cross_qkv[1:], preferred_element_type=high_type
    )
    cross_key = encoder_proj[0].astype(low_type).reshape(seq_count, local_len, width)
    cross_value = (
        (encoder_proj[1] + cross_bias[1]).astype(low_type).reshape(seq_count, local_len, width)
    )
    cross_keys, cross_values = (
        lax.all_gather(cross_key, "seq", axis=1, tiled=True),
        lax.all_gather(cross_value, "seq", axis=1, tiled=True),
    )
    cross_items = (
        cross_query.reshape(head_shape),
        cross_keys.reshape(all_shape),
        cross_values.reshape(all_shape),
        enc_lengths,
    )
    cross_mixed, cross_total = lax.map(plain_cross_forward, cross_items)
    cross_mixed = cross_mixed.reshape(row_count, width)
    cross_branch = jnp.dot(
        cross_mixed, cross_out, preferred_element_type=high_type
    ) + cross_out_bias.astype(high_type)
    second_sum = first_norm + cross_branch
    second_norm = layer_norm(second_sum, gains[1], shifts[1])
    second_low = second_norm.astype(low_type)
    hidden_pre = jnp.dot(second_low, ffn_in, preferred_element_type=high_type) + ffn_in_bias.astype(
        high_type
    )
    activated = gelu_exact(hidden_pre).astype(low_type)
    ffn_branch = jnp.dot(
        activated, ffn_out, preferred_element_type=high_type
    ) + ffn_out_bias.astype(high_type)
    third_sum = second_norm + ffn_branch
    output = layer_norm(third_sum, gains[2], shifts[2]).astype(low_type).reshape(hidden.shape)
    third_value, norm_pull = jax.vjp(layer_norm, third_sum, gains[2], shifts[2])
    grad_third, grad_gain_ffn, grad_shift_ffn = norm_pull(
        cotangent.reshape(-1, width).astype(high_type)
    )
    grad_ffn = grad_third.astype(low_type)
    grad_ffn_out = jnp.einsum("rf,rd->fd", activated, grad_ffn, preferred_element_type=high_type)
    grad_ffn_out_bias = column_sum(grad_ffn)
    grad_activated = jnp.einsum("rd,fd->rf", grad_ffn, ffn_out, preferred_element_type=high_type)
    gelu_value, gelu_pull = jax.vjp(gelu_exact, hidden_pre)
    grad_pre = gelu_pull(grad_activated)[0].astype(low_type)
    grad_ffn_in = jnp.einsum("rd,rf->df", second_low, grad_pre, preferred_element_type=high_type)
    grad_ffn_in_bias = column_sum(grad_pre)
    grad_second = grad_third + jnp.einsum(
        "rf,df->rd", grad_pre, ffn_in, preferred_element_type=high_type
    )
    second_value, norm_pull = jax.vjp(layer_norm, second_sum, gains[1], shifts[1])
    grad_second_sum, grad_gain_cross, grad_shift_cross = norm_pull(grad_second)
    grad_cross = grad_second_sum.astype(low_type)
    grad_cross_out = jnp.einsum(
        "rd,re->de", cross_mixed, grad_cross, preferred_element_type=high_type
    )
    grad_cross_out_bias = column_sum(grad_cross)
    grad_cross_mixed = jnp.einsum(
        "re,de->rd", grad_cross, cross_out, preferred_element_type=high_type
    ).astype(low_type)
    cross_back_items = (
        cross_query.reshape(head_shape),
        cross_keys.reshape(all_shape),
        cross_values.reshape(all_shape),
        enc_lengths,
        cross_total,
        grad_cross_mixed.reshape(head_shape),
    )
    grad_cross_query, grad_cross_keys, grad_cross_values = lax.map(plain_cross_backward, cross_back_items)
    cross_key_sum, cross_value_sum = (
        lax.psum_scatter(
            grad_cross_keys.reshape(kv_shape).astype(jnp.bfloat16),
            "seq",
            scatter_dimension=1,
            tiled=True,
        ).astype(jnp.float32),
        lax.psum_scatter(
            grad_cross_values.reshape(kv_shape).astype(jnp.bfloat16),
            "seq",
            scatter_dimension=1,
            tiled=True,
        ).astype(jnp.float32),
    )
    query_low = grad_cross_query.reshape(row_count, width).astype(low_type)
    encoder_grads = jnp.stack(
        [cross_key_sum.reshape(-1, width), cross_value_sum.reshape(-1, width)]
    ).astype(low_type)
    grad_cross_query_weight = jnp.einsum(
        "rd,re->de", first_low, query_low, preferred_element_type=high_type
    )
    grad_cross_kv_weight = jnp.einsum(
        "rd,cre->cde", encoder_rows, encoder_grads, preferred_element_type=high_type
    )
    grad_cross_qkv = jnp.concatenate([grad_cross_query_weight[None], grad_cross_kv_weight], 0)
    grad_cross_bias = jnp.stack([column_sum(query_low), column_sum(encoder_grads[1])])
    grad_encoder = jnp.einsum(
        "cre,cde->rd", encoder_grads, cross_qkv[1:], preferred_element_type=high_type
    )
    grad_encoder = grad_encoder.astype(low_type).reshape(encoder_out.shape)
    grad_first = grad_second_sum + jnp.einsum(
        "re,de->rd", query_low, cross_qkv[0], preferred_element_type=high_type
    )
    first_value, norm_pull = jax.vjp(layer_norm, first_sum, gains[0], shifts[0])
    grad_first_sum, grad_gain_self, grad_shift_self = norm_pull(grad_first)
    grad_self = grad_first_sum.astype(low_type)
    grad_self_out = jnp.einsum("rd,re->de", attended, grad_self, preferred_element_type=high_type)
    grad_self_out_bias = column_sum(grad_self)
    grad_attended = jnp.einsum(
        "re,de->rd", grad_self, self_out, preferred_element_type=high_type
    ).astype(low_type)
    self_back_items = (
        query.reshape(head_shape),
        key.reshape(head_shape),
        value.reshape(head_shape),
        rel_heads,
        keys_all.reshape(all_shape),
        values_all.reshape(all_shape),
        dec_lengths,
        self_total,
        grad_attended.reshape(head_shape),
    )
    grad_query, grad_key_own, grad_value_own, grad_keys, grad_values, grad_rel = lax.map(
        lambda items: plain_self_backward(items, offset_pos), self_back_items
    )
    key_sum, value_sum = (
        lax.psum_scatter(
            grad_keys.reshape(kv_shape).astype(jnp.bfloat16), "seq", scatter_dimension=1, tiled=True
        ).astype(jnp.float32),
        lax.psum_scatter(
            grad_values.reshape(kv_shape).astype(jnp.bfloat16),
            "seq",
            scatter_dimension=1,
            tiled=True,
        ).astype(jnp.float32),
    )
    own_shape = (seq_count, streams, local_len, width)
    key_total = jnp.concatenate([key_sum[:, None], grad_key_own.reshape(own_shape)[:, 1:]], 1)
    value_total = jnp.concatenate([value_sum[:, None], grad_value_own.reshape(own_shape)[:, 1:]], 1)
    stacked_grad = jnp.stack(
        [
            grad_query.reshape(row_count, width),
            key_total.reshape(row_count, width),
            value_total.reshape(row_count, width),
        ]
    ).astype(low_type)
    rel_low = grad_rel.reshape(row_count, heads * BUCKETS).astype(low_type)
    grad_self_qkv = jnp.einsum("rd,cre->cde", rows, stacked_grad, preferred_element_type=high_type)
    grad_self_bias = jnp.stack([column_sum(stacked_grad[0]), column_sum(stacked_grad[2])])
    grad_rel_weight = jnp.einsum("rd,rb->db", rows, rel_low, preferred_element_type=high_type)
    grad_rel_bias = column_sum(rel_low)
    grad_rows = grad_first_sum + jnp.einsum(
        "cre,cde->rd", stacked_grad, self_qkv, preferred_element_type=high_type
    )
    grad_rows = grad_rows + jnp.einsum(
        "rb,db->rd", rel_low, rel_weight, preferred_element_type=high_type
    )
    grad_hidden = grad_rows.astype(low_type).reshape(hidden.shape)
    matrices = [
        grad_self_qkv,
        grad_self_out,
        grad_rel_weight,
        grad_cross_qkv,
        grad_cross_out,
        grad_ffn_in,
        grad_ffn_out,
    ]
    vectors = [
        grad_self_bias.reshape(-1),
        grad_self_out_bias,
        grad_rel_bias,
        grad_cross_bias.reshape(-1),
        grad_cross_out_bias,
        grad_ffn_in_bias,
        grad_ffn_out_bias,
        jnp.stack([grad_gain_self, grad_gain_cross, grad_gain_ffn]).reshape(-1),
        jnp.stack([grad_shift_self, grad_shift_cross, grad_shift_ffn]).reshape(-1),
    ]
    vec_blocks = [piece.reshape(seq_parts, -1) for piece in vectors]
    mat_blocks = [piece.reshape(dp_parts, seq_parts, -1) for piece in matrices]
    reduced = (
        lax.psum_scatter(
            mat_blocks[0].astype(jnp.bfloat16), "seq", scatter_dimension=1, tiled=True
        ).astype(jnp.float32),
        lax.psum_scatter(
            mat_blocks[1].astype(jnp.bfloat16), "seq", scatter_dimension=1, tiled=True
        ).astype(jnp.float32),
        lax.psum_scatter(
            mat_blocks[2].astype(jnp.bfloat16), "seq", scatter_dimension=1, tiled=True
        ).astype(jnp.float32),
        lax.psum_scatter(
            mat_blocks[3].astype(jnp.bfloat16), "seq", scatter_dimension=1, tiled=True
        ).astype(jnp.float32),
        lax.psum_scatter(
            mat_blocks[4].astype(jnp.bfloat16), "seq", scatter_dimension=1, tiled=True
        ).astype(jnp.float32),
        lax.psum_scatter(
            mat_blocks[5].astype(jnp.bfloat16), "seq", scatter_dimension=1, tiled=True
        ).astype(jnp.float32),
        lax.psum_scatter(
            mat_blocks[6].astype(jnp.bfloat16), "seq", scatter_dimension=1, tiled=True
        ).astype(jnp.float32),
        lax.psum_scatter(
            vec_blocks[0].astype(jnp.bfloat16), "seq", scatter_dimension=0, tiled=True
        ).astype(jnp.float32),
        lax.psum_scatter(
            vec_blocks[1].astype(jnp.bfloat16), "seq", scatter_dimension=0, tiled=True
        ).astype(jnp.float32),
        lax.psum_scatter(
            vec_blocks[2].astype(jnp.bfloat16), "seq", scatter_dimension=0, tiled=True
        ).astype(jnp.float32),
        lax.psum_scatter(
            vec_blocks[3].astype(jnp.bfloat16), "seq", scatter_dimension=0, tiled=True
        ).astype(jnp.float32),
        lax.psum_scatter(
            vec_blocks[4].astype(jnp.bfloat16), "seq", scatter_dimension=0, tiled=True
        ).astype(jnp.float32),
        lax.psum_scatter(
            vec_blocks[5].astype(jnp.bfloat16), "seq", scatter_dimension=0, tiled=True
        ).astype(jnp.float32),
        lax.psum_scatter(
            vec_blocks[6].astype(jnp.bfloat16), "seq", scatter_dimension=0, tiled=True
        ).astype(jnp.float32),
        lax.psum_scatter(
            vec_blocks[7].astype(jnp.bfloat16), "seq", scatter_dimension=0, tiled=True
        ).astype(jnp.float32),
        lax.psum_scatter(
            vec_blocks[8].astype(jnp.bfloat16), "seq", scatter_dimension=0, tiled=True
        ).astype(jnp.float32),
    )
    mat_done = (
        lax.psum_scatter(
            reduced[0].astype(jnp.bfloat16), "dp", scatter_dimension=0, tiled=True
        ).astype(jnp.float32),
        lax.psum_scatter(
            reduced[1].astype(jnp.bfloat16), "dp", scatter_dimension=0, tiled=True
        ).astype(jnp.float32),
        lax.psum_scatter(
            reduced[2].astype(jnp.bfloat16), "dp", scatter_dimension=0, tiled=True
        ).astype(jnp.float32),
        lax.psum_scatter(
            reduced[3].astype(jnp.bfloat16), "dp", scatter_dimension=0, tiled=True
        ).astype(jnp.float32),
        lax.psum_scatter(
            reduced[4].astype(jnp.bfloat16), "dp", scatter_dimension=0, tiled=True
        ).astype(jnp.float32),
        lax.psum_scatter(
            reduced[5].astype(jnp.bfloat16), "dp", scatter_dimension=0, tiled=True
        ).astype(jnp.float32),
        lax.psum_scatter(
            reduced[6].astype(jnp.bfloat16), "dp", scatter_dimension=0, tiled=True
        ).astype(jnp.float32),
    )
    vec_part = [reduced[7 + index] for index in range(9)]
    vec_done = lax.psum(
        (
            vec_part[0],
            vec_part[1],
            vec_part[2],
            vec_part[3],
            vec_part[4],
            vec_part[5],
            vec_part[6],
            vec_part[7],
            vec_part[8],
        ),
        "dp",
    )
    mats = [piece.reshape(-1) for piece in mat_done]
    vecs = [piece.reshape(-1) for piece in vec_done]
    return (
        output,
        grad_hidden,
        grad_encoder,
        mats[0],
        vecs[0],
        mats[1],
        vecs[1],
        mats[2],
        vecs[2],
        mats[3],
        vecs[3],
        mats[4],
        vecs[4],
        mats[5],
        vecs[5],
        mats[6],
        vecs[6],
        vecs[7],
        vecs[8],
    )


def on_device(
    hidden,
    encoder_out,
    cotangent,
    dec_lengths,
    enc_lengths,
    self_qkv,
    self_qv_bias,
    self_out,
    self_out_bias,
    rel_weight,
    rel_bias,
    cross_qkv,
    cross_qv_bias,
    cross_out,
    cross_out_bias,
    ffn_in,
    ffn_in_bias,
    ffn_out,
    ffn_out_bias,
    norm_gain,
    norm_bias,
):
    B, S, T, width = hidden.shape
    if T % TILE or lax.axis_size("dp") != 8 or width % (32 * 8 * lax.axis_size("seq")):
        return plain_on_device(
            hidden,
            encoder_out,
            cotangent,
            dec_lengths,
            enc_lengths,
            self_qkv,
            self_qv_bias,
            self_out,
            self_out_bias,
            rel_weight,
            rel_bias,
            cross_qkv,
            cross_qv_bias,
            cross_out,
            cross_out_bias,
            ffn_in,
            ffn_in_bias,
            ffn_out,
            ffn_out_bias,
            norm_gain,
            norm_bias,
        )
    seq_parts = lax.axis_size("seq")
    keys = T * seq_parts
    far = keys - T
    place = lax.axis_index("seq")
    up = [(i, i + 1) for i in range(seq_parts - 1)]
    down = [(i + 1, i) for i in range(seq_parts - 1)]
    gains, shifts = norm_gain.astype(high_type), norm_bias.astype(high_type)
    self_bias, cross_bias = self_qv_bias.astype(high_type), cross_qv_bias.astype(high_type)
    table = jnp.asarray(bucket_table(), low_type)

    after = lax.optimization_barrier
    x = hidden.reshape(B * S * T, width)
    rows = B * S * T
    far_rows, held = [], None
    for b in range(B):
        moving, pieces = hidden[b, 0], []
        if held is not None:
            moving, held = after((moving, held))
        for _ in range(seq_parts - 1):
            moving = lax.ppermute(moving, "seq", up)
            pieces.append(moving)
        held = moving
        far_rows.append(jnp.concatenate(pieces[::-1], 0))
    e_own, far_rows[0] = after((encoder_out, far_rows[0]))
    e_all = lax.all_gather(e_own, "seq", axis=1, tiled=True).reshape(-1, width)
    key_at = place * T - far + jnp.arange(keys, dtype=jnp.int32)
    self_mark = key_features((key_at >= 0) & (key_at < dec_lengths[:, None]))
    cross_mark = key_features(jnp.arange(keys, dtype=jnp.int32) < enc_lengths[:, None])

    q = ((dot("de,rd->er", self_qkv[0], x) + self_bias[0][:, None]) * SCALE).astype(low_type)
    rel = dot("db,rd->br", rel_weight, x) + rel_bias.astype(high_type)[:, None]
    k = dot("de,rd->er", self_qkv[1], x).astype(low_type)
    v = (dot("de,rd->er", self_qkv[2], x) + self_bias[1][:, None]).astype(low_type)
    self_inputs, results = [], ()
    for b in range(B):
        k_far = dot("de,rd->er", self_qkv[1], far_rows[b]).astype(low_type)
        v_far = (dot("de,rd->er", self_qkv[2], far_rows[b]) + self_bias[1][:, None]).astype(
            low_type
        )
        self_inputs.append((q, k, v, k_far, v_far, rel, self_mark, table))
        results = self_forward(b, self_inputs[b], results, T, S)
    attended, self_total = results
    first_sum = (
        x.astype(high_type)
        + dot("er,ed->rd", attended, self_out)
        + self_out_bias.astype(high_type)
    )
    first_unit, _ = norm_parts(first_sum)
    first_norm = first_unit * gains[0] + shifts[0]
    first_low = first_norm.astype(low_type)

    qc = ((dot("de,rd->er", cross_qkv[0], first_low) + cross_bias[0][:, None]) * SCALE).astype(
        low_type
    )
    kc = dot("de,rd->er", cross_qkv[1], e_all).astype(low_type)
    vc = (dot("de,rd->er", cross_qkv[2], e_all) + cross_bias[1][:, None]).astype(low_type)
    cross_mixed, cross_total = cross_forward(qc, kc, vc, cross_mark)
    second_sum = (
        first_norm
        + dot("er,ed->rd", cross_mixed, cross_out)
        + cross_out_bias.astype(high_type)
    )
    second_unit, _ = norm_parts(second_sum)
    second_norm = second_unit * gains[1] + shifts[1]
    second_low = second_norm.astype(low_type)

    activated, slope = ffn_first(second_low, ffn_in, ffn_in_bias.astype(high_type)[None])
    third_sum = (
        second_norm + dot("rf,fd->rd", activated, ffn_out) + ffn_out_bias.astype(high_type)
    )
    third_unit, _ = norm_parts(third_sum)
    output = (third_unit * gains[2] + shifts[2]).astype(low_type).reshape(hidden.shape)

    grad_third, grad_gain_ffn, grad_shift_ffn = norm_back(
        third_sum, cotangent.reshape(rows, width).astype(high_type), gains[2]
    )
    grad_ffn = grad_third.astype(low_type)

    def over_dp(piece):
        return lax.psum_scatter(piece, "dp", scatter_dimension=0, tiled=True)

    def over_dp_by_steps(piece, meanwhile):
        me = lax.axis_index("dp")

        def swap(pair, bit):
            mine = (me >> bit) & 1
            sent = lax.dynamic_index_in_dim(pair, 1 - mine, 0, keepdims=False)
            kept = lax.dynamic_index_in_dim(pair, mine, 0, keepdims=False)
            came = lax.ppermute(sent, "dp", [(i, i ^ (1 << bit)) for i in range(8)])
            return low(came.astype(high_type) + kept.astype(high_type))

        count = piece.shape[0] // 8
        chip = swap(jnp.swapaxes(piece.reshape(4, 2, count, width), 0, 1), 0)
        chip, meanwhile = after((chip, meanwhile))
        first, second = chip[:, : count // 2], chip[:, count // 2 :]
        first = swap(jnp.swapaxes(first.reshape(2, 2, count // 2, width), 0, 1), 1)
        second = swap(second.reshape(2, 2, count // 2, width), 2)
        return jnp.concatenate([swap(first, 2), swap(second, 1)], 0), meanwhile

    def over_seq(*pieces):
        cut = [piece.reshape(seq_parts, -1, width) for piece in pieces]
        joined = jnp.concatenate(cut, 1)

        def block(hop):
            return lax.dynamic_index_in_dim(
                joined, (place - hop) % seq_parts, 0, keepdims=False
            ).astype(high_type)

        ring = [(i, (i + 1) % seq_parts) for i in range(seq_parts)]
        held = block(1)
        for hop in range(2, seq_parts + 1):
            held = lax.ppermute(held.astype(low_type), "seq", ring).astype(high_type) + block(hop)
        ends = np.cumsum([piece.shape[1] for piece in cut])
        return [
            held[end - piece.shape[1] : end].reshape(-1)
            for piece, end in zip(cut, ends, strict=True)
        ]

    def low(value):
        return value.astype(low_type)

    part_ffn_out, grad_ffn = after((low(dot("rf,rd->fd", activated, grad_ffn)), grad_ffn))
    mat_ffn_out = over_dp(part_ffn_out)
    grad_pre = (dot("rd,fd->rf", grad_ffn, ffn_out) * slope.astype(high_type)).astype(low_type)
    part_ffn_in, grad_pre = after((low(dot("rd,rf->df", second_low, grad_pre)), grad_pre))
    mat_ffn_in = over_dp(part_ffn_in)
    grad_second = grad_third + dot("rf,df->rd", grad_pre, ffn_in)
    grad_second_sum, grad_gain_cross, grad_shift_cross = norm_back(
        second_sum, grad_second, gains[1]
    )
    grad_cross = grad_second_sum.astype(low_type)
    part_cross_out, grad_cross = after((low(dot("er,rd->ed", cross_mixed, grad_cross)), grad_cross))
    mat_cross_out = over_dp(part_cross_out)
    grad_cross_mixed = dot("ed,rd->er", cross_out, grad_cross).astype(low_type)
    dqc, dkc, dvc = cross_backward(
        qc, kc, vc, cross_mark, cross_mixed, cross_total, grad_cross_mixed
    )
    dqc, dkc, dvc, mat_ffn_out, mat_ffn_in = after((dqc, dkc, dvc, mat_ffn_out, mat_ffn_in))
    done_ffn_in, done_ffn_out = over_seq(mat_ffn_in, mat_ffn_out)
    part_encoder = back_rows(
        (dkc, dvc), ((cross_qkv, 1), (cross_qkv, 2)), None, None, keys, "encoder_rows"
    ).reshape(B, keys, width)
    third = 3 * width // 8

    def cut(step, size, blocks):
        found = []
        for block in range(blocks):
            low_at, high_at = max(size * block, width * step), min(size * (block + 1), width * (step + 1))
            if low_at < high_at:
                found.append(((block, low_at - size * block), low_at - width * step, high_at - low_at, 0))
        return found

    quarter = width // 4
    (part_cross_qkv,) = weight_grads(
        (first_low, e_all),
        (dqc, dkc, dvc),
        [
            pl.BlockSpec((quarter, rows), lambda e, c: (e, 0)),
            pl.BlockSpec((quarter, B * keys), lambda e, c: (e, 0)),
            pl.BlockSpec((quarter, B * keys), lambda e, c: (e, 0)),
        ],
        [[(0, (0, rows))], [(1, (rows, rows + B * keys))], [(2, (rows, rows + B * keys))]],
        [cut(step, third, 8) for step in range(3)],
        [False] * 3,
        (8, third, width),
        "cross_weights",
    )
    part_cross_qkv = part_cross_qkv.reshape(3 * width, width)
    part_encoder, part_cross_qkv, dqc = after((part_encoder, part_cross_qkv, dqc))
    mat_cross_qkv = over_dp(part_cross_qkv)

    def positions(hop):
        at = (place + hop) % seq_parts
        return lax.dynamic_slice_in_dim(part_encoder, at * T, T, 1)

    encoder_parts = [positions(0)] + [
        lax.ppermute(positions(hop), "seq", [(i, (i + hop) % seq_parts) for i in range(seq_parts)])
        for hop in range(1, seq_parts)
    ]
    grad_first = grad_second_sum + dot("er,de->rd", dqc, cross_qkv[0])
    grad_first_sum, grad_gain_self, grad_shift_self = norm_back(first_sum, grad_first, gains[0])
    grad_self = grad_first_sum.astype(low_type)
    part_self_out, grad_self = after((low(dot("er,rd->ed", attended, grad_self)), grad_self))
    mat_self_out = over_dp(part_self_out)
    grad_attended = dot("ed,rd->er", self_out, grad_self).astype(low_type)
    grad_attended, done_ffn_in, done_ffn_out = after((grad_attended, done_ffn_in, done_ffn_out))
    results, came = (), []
    for b in range(B):
        *results, far_grads = self_backward(
            b, self_inputs[b], (attended, self_total, grad_attended), tuple(results), T, S
        )
        if b:
            far_grads, came[b - 1] = after((far_grads, came[b - 1]))
        away = back_rows(
            ((far_grads, 0), (far_grads, 1)), ((self_qkv, 1), (self_qkv, 2)), None, None, far, "far_rows"
        )
        if b == 0:
            far_columns = [far_grads]
        else:
            far_columns.append(far_grads)
        came.append(
            [
                lax.ppermute(
                    away[(seq_parts - 1 - hop) * T : (seq_parts - hop) * T],
                    "seq",
                    [(i + hop, i) for i in range(seq_parts - hop)],
                )
                for hop in range(1, seq_parts)
            ]
        )
        if b + 1 < B:
            results[0], self_inputs[b + 1], away, encoder_parts = after(
                (results[0], self_inputs[b + 1], away, encoder_parts)
            )
            grad_encoder = functools.reduce(
                jnp.add, [piece.astype(high_type) for piece in encoder_parts]
            ).astype(low_type)
    results[0], away = after((results[0], away))
    dq, dkv, drel = results
    blocks, size, rel_size = 8 * seq_parts, 3 * width // (8 * seq_parts), width // (16 * seq_parts)
    near_at, far_at = (0, rows), [(rows + b * far, rows + (b + 1) * far) for b in range(B)]
    part_self, part_sums = weight_grads(
        (x, *far_rows),
        (dq, dkv, dkv, drel) + tuple(far_columns) * 2,
        [
            pl.BlockSpec((quarter, rows), lambda e, c: (e, 0)),
            pl.BlockSpec((None, quarter, rows), lambda e, c: (0, e, 0)),
            pl.BlockSpec((None, quarter, rows), lambda e, c: (1, e, 0)),
            pl.BlockSpec((quarter, rows), lambda e, c: (e % 2, 0)),
        ]
        + [pl.BlockSpec((None, quarter, far), lambda e, c: (0, e, 0))] * B
        + [pl.BlockSpec((None, quarter, far), lambda e, c: (1, e, 0))] * B,
        [
            [(0, near_at)],
            [(1, near_at)] + [(4 + b, far_at[b]) for b in range(B)],
            [(2, near_at)] + [(4 + B + b, far_at[b]) for b in range(B)],
            [(3, near_at)],
        ],
        [cut(step, size, blocks) for step in range(3)]
        + [[((block, size), 2 * rel_size * block, rel_size, 2) for block in range(blocks)]],
        [True, False, True, True],
        (blocks, size + rel_size, width),
        "self_weights",
    )
    part_self, came[-1] = after((part_self, came[-1]))
    mat_self, (dq, mat_cross_out, mat_cross_qkv, mat_self_out, part_sums) = over_dp_by_steps(
        part_self.reshape(-1, width), (dq, mat_cross_out, mat_cross_qkv, mat_self_out, part_sums)
    )
    moved = jnp.concatenate(
        [functools.reduce(jnp.add, [piece.astype(high_type) for piece in came[b]]) for b in range(B)], 0
    )
    grad_hidden = back_rows(
        (dq, (dkv, 0), (dkv, 1), drel),
        ((self_qkv, 0), (self_qkv, 1), (self_qkv, 2), rel_weight),
        grad_first_sum,
        moved,
        S * T,
        "near_rows",
    ).reshape(hidden.shape)
    vectors = [
        jnp.stack([part_sums[0, 0], part_sums[2, 0]]),
        column_sum(grad_self),
        part_sums[3, 0, : width // 2],
        jnp.stack([row_sum(dqc), row_sum(dvc)]),
        column_sum(grad_cross),
        column_sum(grad_pre),
        column_sum(grad_ffn),
        jnp.stack([grad_gain_self, grad_gain_cross, grad_gain_ffn]),
        jnp.stack([grad_shift_self, grad_shift_cross, grad_shift_ffn]),
    ]
    blocks = [piece.reshape(seq_parts, -1) for piece in vectors]
    ends = np.cumsum([piece.shape[1] for piece in blocks])
    summed = jnp.concatenate(blocks, 1)
    for axis, size_of in (("dp", 8), ("seq", seq_parts)):
        for bit in range(size_of.bit_length() - 1):
            summed = summed + lax.ppermute(summed, axis, [(i, i ^ (1 << bit)) for i in range(size_of)])
    mine = lax.dynamic_index_in_dim(summed, place, 0, keepdims=False)
    done_cross_out, done_cross_qkv, done_self_out = over_seq(
        mat_cross_out, mat_cross_qkv, mat_self_out
    )
    mat_self, mine, done_cross_out, grad_hidden = after((mat_self, mine, done_cross_out, grad_hidden))
    (done_self,) = over_seq(mat_self)
    done_self = done_self.reshape(size + rel_size, width)
    done_self_qkv = done_self[:size].reshape(-1)
    half = width // 2
    done_rel = jnp.concatenate([done_self[size:, :half], done_self[size:, half:]], 0).reshape(-1)

    vecs = [mine[end - piece.shape[1] : end] for piece, end in zip(blocks, ends, strict=True)]
    return (
        output,
        grad_hidden,
        grad_encoder,
        done_self_qkv,
        vecs[0],
        done_self_out,
        vecs[1],
        done_rel,
        vecs[2],
        done_cross_qkv,
        vecs[3],
        done_cross_out,
        vecs[4],
        done_ffn_in,
        vecs[5],
        done_ffn_out,
        vecs[6],
        vecs[7],
        vecs[8],
    )


def solution(mesh):
    rows, vector, matrix = P("dp", None, "seq", None), P("seq"), P(("dp", "seq"))
    return jax.shard_map(
        on_device,
        mesh=mesh,
        in_specs=(rows, P("dp", "seq", None), rows, P("dp"), P("dp")) + (P(),) * 16,
        out_specs=(rows, rows, P("dp", "seq", None))
        + (matrix, vector) * 7
        + (vector, vector),
        check_vma=False,
    )
```

```python
import functools
import math

import jax
import jax.numpy as jnp
import numpy as np
from jax import lax
from jax.experimental import pallas as pl
from jax.experimental.pallas import tpu as pltpu
from jax.sharding import PartitionSpec as P

HEADS = 16
BUCKETS = 32
MAX_DIST = 128
SIZE = 64
SCALE = 0.125
TILE = 128
NEGATIVE = -1e30
EPSILON = 1e-05
VMEM_LIMIT = 60 * 2**20
SPLIT = 2
FFN_COLS = 1024
FFN_ROWS = 768
FFN_STEP = 512
BACK_COLUMNS = 512

low_type = jnp.bfloat16
high_type = jnp.float32


def contract(left, right, left_dim, right_dim):
    return lax.dot_general(
        left, right, (((left_dim,), (right_dim,)), ((), ())), preferred_element_type=high_type
    )


def split_two(value):
    top = value.astype(low_type)
    return top, (value - top.astype(high_type)).astype(low_type)


def feature_rows(first, value):
    a = value.astype(low_type).astype(high_type)
    b = (value - a).astype(low_type).astype(high_type)
    c = value - a - b
    count = value.shape[1]
    at = lax.broadcasted_iota(jnp.int32, (16, count), 0)
    out = jnp.where(at == 0, first, 0.0)
    for index, piece in enumerate((a, b, c)):
        out = jnp.where(at == index + 1, piece, out)
    return out.astype(low_type)


def key_features(valid):
    mask = jnp.where(valid, 0.0, NEGATIVE)[:, None, :]
    ones = jnp.ones_like(mask)
    return jnp.concatenate([mask, ones, ones, ones] + [jnp.zeros_like(mask)] * 12, 1).astype(
        low_type
    )


def bucket_table():
    half = BUCKETS // 2
    distance = (TILE - np.arange(2 * TILE)) % (2 * TILE)
    counted = np.zeros_like(distance)
    for level in range(1, half):
        counted = counted + (distance >= math.ceil(half * (MAX_DIST / half) ** (level / half)))
    bucket = np.where(distance < half, distance, half + counted)
    table = (bucket[None, :] == np.arange(BUCKETS)[:, None]).astype(np.float32)
    table[BUCKETS - 1] = -(bucket < BUCKETS - 1).astype(np.float32)
    return table


def near_bias(rel, table):
    top, rest = split_two(rel)
    return contract(
        jnp.concatenate([top, rest], 0), jnp.concatenate([table, table], 0), 0, 0
    )


def cross_forward_kernel(q_ref, k_ref, v_ref, mark_ref, o_ref, total_ref):
    count, keys = q_ref.shape[1], k_ref.shape[1]
    k1 = jnp.concatenate([k_ref[...], mark_ref[...]], 0)
    v1 = jnp.concatenate([v_ref[...], jnp.ones((16, keys), low_type)], 0)
    zero = jnp.zeros((1, count), high_type)
    q1 = jnp.concatenate([q_ref[...], feature_rows(1.0, zero)], 0)
    scores = contract(k1, q1, 0, 0)
    peak = jnp.max(scores, 0, keepdims=True)
    weights = jnp.exp(scores - peak).astype(low_type)
    mixed = contract(v1, weights, 1, 0)
    total = mixed[SIZE : SIZE + 1]
    o_ref[...] = (mixed[:SIZE] * (1.0 / total)).astype(low_type)
    total_ref[...] = peak + jnp.log(total)


def cross_backward_kernel(
    q_ref, k_ref, v_ref, mark_ref, o_ref, total_ref, do_ref, dq_ref, dk_ref, dv_ref, dk_acc, dv_acc, *, step
):
    count, keys = q_ref.shape[1], k_ref.shape[1]
    k = k_ref[...]
    k1 = jnp.concatenate([k, mark_ref[...]], 0)
    v1 = jnp.concatenate([v_ref[...], mark_ref[...]], 0)
    for n in range(0, count, step):
        q, do = q_ref[:, n : n + step], do_ref[:, n : n + step]
        delta = jnp.sum(
            do.astype(high_type) * o_ref[:, n : n + step].astype(high_type), 0, keepdims=True
        )
        q1 = jnp.concatenate([q, feature_rows(1.0, -total_ref[:, n : n + step])], 0)
        do1 = jnp.concatenate([do, feature_rows(0.0, -delta)], 0)
        weights = jnp.exp(contract(q1, k1, 0, 0))
        grad_scores = (weights * contract(do1, v1, 0, 0)).astype(low_type)
        weights = weights.astype(low_type)
        dq_ref[:, n : n + step] = (contract(k, grad_scores, 1, 1) * SCALE).astype(low_type)
        dk = contract(q, grad_scores, 1, 0)
        dv = contract(do, weights, 1, 0)
        if n == 0:
            dk_acc[...] = dk
            dv_acc[...] = dv
        else:
            dk_acc[...] += dk
            dv_acc[...] += dv
    dk_ref[...] = dk_acc[...].astype(low_type)
    dv_ref[...] = dv_acc[...].astype(low_type)


def near_biases(rel, table):
    near = near_bias(rel, table)
    return [
        pltpu.roll(near[row : row + TILE], 0, 1, stride=1, stride_axis=0)
        for row in range(0, near.shape[0], TILE)
    ]


def main_and_own(far_ref, near_ref, T):
    near = near_ref[...]
    return jnp.concatenate([far_ref[...], near[:, :T]], 1), near[:, T:]


def near_window(block, bias, first, main_row):
    at = lax.broadcasted_iota(jnp.int32, (TILE, TILE), 0)
    to = lax.broadcasted_iota(jnp.int32, (TILE, TILE), 1)
    left = block[:, first : first + TILE] + bias[:, :TILE]
    right = block[:, first + TILE : first + 2 * TILE] + bias[:, TILE:]
    return left, jnp.where((to <= at) if main_row else (to < at), right, NEGATIVE)


def self_forward_kernel(*refs, T, S):
    q_ref, k_ref, v_ref, k_far_ref, v_far_ref, rel_ref, mark_ref, table_ref = refs[:8]
    o_ref, total_ref = refs[-2:]
    n, keys = S * T, k_far_ref.shape[1] + T
    q, rel = q_ref[...], rel_ref[...]
    k, own_k = main_and_own(k_far_ref, k_ref, T)
    v, own_v = main_and_own(v_far_ref, v_ref, T)
    biases = near_biases(rel, table_ref[...])
    k1 = jnp.concatenate([k, mark_ref[...]], 0)
    v1 = jnp.concatenate([v, jnp.ones((16, keys), low_type)], 0)
    q1 = jnp.concatenate([q, feature_rows(1.0, rel[BUCKETS - 1 :])], 0)
    scores = contract(q1, k1, 0, 0)
    weights, peaks = [], []
    for s in range(S):
        for r in range(T // TILE):
            row, first = s * T + r * TILE, keys - T + (r - 1) * TILE
            block = scores[row : row + TILE]
            left, right = near_window(block, biases[row // TILE], first, s == 0)
            parts = [left, right]
            peak = jnp.max(jnp.maximum(left, right), 1, keepdims=True)
            if first > 0:
                far = block[:, :first]
                peak = jnp.maximum(peak, jnp.max(far, 1, keepdims=True))
                parts = [far] + parts
            parts = [jnp.exp(part - peak).astype(low_type) for part in parts]
            if first + 2 * TILE < keys:
                parts.append(jnp.zeros((TILE, keys - first - 2 * TILE), low_type))
            weights.append(jnp.concatenate(parts, 1))
            peaks.append(jnp.broadcast_to(peak, (TILE, TILE)).T[0:1])
    mixed = contract(v1, jnp.concatenate(weights, 0), 1, 1)
    peak = jnp.concatenate(peaks, 1)
    total, mixed = mixed[SIZE : SIZE + 1], mixed[:SIZE]
    own_k, own_v = own_k.astype(high_type), own_v.astype(high_type)
    own = jnp.sum(q[:, T:].astype(high_type) * own_k, 0, keepdims=True) + rel[0:1, T:]
    top = jnp.maximum(peak[:, T:], own)
    main_part, own_part = jnp.exp(peak[:, T:] - top), jnp.exp(own - top)
    joined = total[:, T:] * main_part + own_part
    inverse = 1.0 / joined
    o_ref[:, :T] = (mixed[:, :T] * (1.0 / total[:, :T])).astype(low_type)
    o_ref[:, T:] = (mixed[:, T:] * (main_part * inverse) + own_v * (own_part * inverse)).astype(
        low_type
    )
    total_ref[:, :T] = peak[:, :T] + jnp.log(total[:, :T])
    total_ref[:, T:] = top + jnp.log(joined)


def self_backward_kernel(*refs, T, S):
    q_ref, k_ref, v_ref, k_far_ref, v_far_ref, rel_ref, mark_ref, table_ref = refs[:8]
    o_ref, total_ref, do_ref = refs[8:11]
    dq_ref, dkv_ref, drel_ref, far_ref = refs[-4:]
    n, keys = S * T, k_far_ref.shape[1] + T
    far = keys - T
    q, rel, do, total = q_ref[...], rel_ref[...], do_ref[...], total_ref[...]
    table = table_ref[...]
    k, own_k = main_and_own(k_far_ref, k_ref, T)
    v, own_v = main_and_own(v_far_ref, v_ref, T)
    biases = near_biases(rel, table)
    k1 = jnp.concatenate([k, mark_ref[...]], 0)
    v1 = jnp.concatenate([v, mark_ref[...]], 0)
    do_high = do.astype(high_type)
    delta = jnp.sum(do_high * o_ref[...].astype(high_type), 0, keepdims=True)
    q1 = jnp.concatenate([q, feature_rows(1.0, rel[BUCKETS - 1 :] - total)], 0)
    do1 = jnp.concatenate([do, feature_rows(0.0, -delta)], 0)
    scores = contract(q1, k1, 0, 0)
    slopes = contract(do1, v1, 0, 0)
    weights, grads, nears = [], [], []
    for s in range(S):
        for r in range(T // TILE):
            row, first = s * T + r * TILE, keys - T + (r - 1) * TILE
            block, slope = scores[row : row + TILE], slopes[row : row + TILE]
            part = jnp.exp(
                jnp.concatenate(near_window(block, biases[row // TILE], first, s == 0), 1)
            )
            grad = (part * slope[:, first : first + 2 * TILE]).astype(low_type)
            nears.append(grad)
            parts, pieces = [part.astype(low_type)], [grad]
            if first > 0:
                part = jnp.exp(block[:, :first])
                pieces = [(part * slope[:, :first]).astype(low_type)] + pieces
                parts = [part.astype(low_type)] + parts
            if first + 2 * TILE < keys:
                zero = jnp.zeros((TILE, keys - first - 2 * TILE), low_type)
                parts.append(zero)
                pieces.append(zero)
            weights.append(jnp.concatenate(parts, 1))
            grads.append(jnp.concatenate(pieces, 1))
    weights, grads = jnp.concatenate(weights, 0), jnp.concatenate(grads, 0)
    dq = contract(k1, grads, 1, 1)
    dk = contract(q, grads, 1, 0).astype(low_type)
    dv = contract(do, weights, 1, 0).astype(low_type)
    far_ref[0] = dk[:, :far]
    far_ref[1] = dv[:, :far]
    at = lax.broadcasted_iota(jnp.int32, (TILE, TILE), 0)
    to = lax.broadcasted_iota(jnp.int32, (TILE, TILE), 1)
    mirror = (at + to == TILE - 1).astype(high_type).astype(low_type)
    flipped = contract(mirror, jnp.concatenate(nears, 1), 1, 0)
    turned = [
        pltpu.roll(flipped[:, i : i + 2 * TILE], TILE + 1, 1, stride=1, stride_axis=0).astype(low_type)
        for i in range(0, 2 * n, 2 * TILE)
    ]
    top, rest = split_two(contract(table, jnp.concatenate(turned, 0), 1, 1))
    stacked = [part[:, i : i + TILE] for i in range(0, n, TILE) for part in (top, rest)]
    both = contract(jnp.concatenate(stacked, 0), mirror, 1, 0)
    rels = [
        both[i : i + BUCKETS] + both[i + BUCKETS : i + 2 * BUCKETS]
        for i in range(0, both.shape[0], 2 * BUCKETS)
    ]
    row_sums = dq[SIZE + 1 : SIZE + 2]
    own_k, own_v = own_k.astype(high_type), own_v.astype(high_type)
    own_q, own_do = q[:, T:].astype(high_type), do_high[:, T:]
    own = jnp.sum(own_q * own_k, 0, keepdims=True) + rel[0:1, T:]
    own_part = jnp.exp(own - total[:, T:])
    own_grad = own_part * (jnp.sum(own_do * own_v, 0, keepdims=True) - delta[:, T:])
    own_grad = own_grad.astype(low_type).astype(high_type)
    dq_ref[:, :T] = (dq[:SIZE, :T] * SCALE).astype(low_type)
    dq_ref[:, T:] = ((dq[:SIZE, T:] + own_grad * own_k) * SCALE).astype(low_type)
    dkv_ref[0, :, :T] = dk[:, far:]
    dkv_ref[1, :, :T] = dv[:, far:]
    dkv_ref[0, :, T:] = (own_grad * own_q).astype(low_type)
    dkv_ref[1, :, T:] = (own_part.astype(low_type).astype(high_type) * own_do).astype(low_type)
    bucket = lax.broadcasted_iota(jnp.int32, (BUCKETS, n), 0)
    drel = jnp.concatenate(rels, 1) + jnp.where(bucket == BUCKETS - 1, row_sums, 0.0)
    own_all = jnp.concatenate([jnp.zeros((1, T), high_type), own_grad], 1)
    drel_ref[...] = (drel + jnp.where(bucket == 0, own_all, 0.0)).astype(low_type)


def weight_grads_kernel(*refs, xs, terms, parts, sums):
    x_refs, rest = refs[:xs], refs[xs:]
    count = max(place for step in terms for _, place in step) + 1
    g_refs, out_ref = rest[:count], rest[count]
    e, c = pl.program_id(0), pl.program_id(1)

    for step, term in enumerate(terms):

        @pl.when(c == step)
        def _():
            x = jnp.concatenate([x_refs[x_at][...] for x_at, _ in term], 0)
            g = jnp.concatenate([g_refs[g_at][...] for _, g_at in term], 1)
            total = contract(x, g, 0, 1)
            if sums[step]:
                line = jnp.sum(g.astype(high_type), 1, keepdims=True)
                rest[count + 1][step] = jnp.broadcast_to(line, (line.shape[0], TILE))
            total = total.astype(low_type)
            for at, row, rows, halves in parts[step]:
                if halves:
                    kept = jnp.where(e < halves, total[row : row + rows], total[row + rows : row + 2 * rows])
                else:
                    kept = total[row : row + rows]
                out_ref[at[0], at[1] : at[1] + rows, :] = kept


def back_rows_kernel(*refs, pairs, base, joined):
    gs, ws, rest, out_ref = refs[:pairs], refs[pairs : 2 * pairs], refs[2 * pairs : -1], refs[-1]
    total = rest[0][...] if base else None
    for g_ref, w_ref in zip(gs, ws, strict=True):
        piece = contract(g_ref[...], w_ref[...], 0, 1)
        total = piece if total is None else total + piece
    if joined:
        add = rest[1][...]
        out_ref[: add.shape[0]] = (total[: add.shape[0]] + add).astype(low_type)
        out_ref[add.shape[0] :] = total[add.shape[0] :].astype(low_type)
    else:
        out_ref[...] = total.astype(low_type)


def per_head(rows, count):
    return pl.BlockSpec((rows, count), lambda b, h: (h, b))


def per_sequence(keys):
    return pl.BlockSpec((None, 16, keys), lambda b, h: (b, 0, 0))


def per_total(count):
    return pl.BlockSpec((None, None, 1, count), lambda b, h: (b, h, 0, 0))


def like(array):
    return jax.ShapeDtypeStruct(array.shape, low_type)


def cost(B, rows, keys, products):
    return pl.CostEstimate(
        flops=2 * B * HEADS * rows * keys * 256 * products,
        bytes_accessed=B * HEADS * SIZE * (rows + keys) * 4 * products,
        transcendentals=B * HEADS * rows * keys,
    )


def cross_forward(q, k, v, mark):
    B, _, keys = mark.shape
    count = q.shape[1] // B
    return pl.pallas_call(
        cross_forward_kernel,
        grid=(B, HEADS),
        in_specs=[per_head(SIZE, count), per_head(SIZE, keys), per_head(SIZE, keys), per_sequence(keys)],
        out_specs=[per_head(SIZE, count), per_total(count)],
        out_shape=[like(q), jax.ShapeDtypeStruct((B, HEADS, 1, count), high_type)],
        cost_estimate=cost(B, count, keys, 2),
        compiler_params=pltpu.CompilerParams(vmem_limit_bytes=VMEM_LIMIT),
        name="cross_forward",
    )(q, k, v, mark)


def cross_backward(q, k, v, mark, o, total, do):
    B, _, keys = mark.shape
    count = q.shape[1] // B
    row, key = per_head(SIZE, count), per_head(SIZE, keys)
    return pl.pallas_call(
        functools.partial(cross_backward_kernel, step=count // 2),
        grid=(B, HEADS),
        in_specs=[row, key, key, per_sequence(keys), row, per_total(count), row],
        out_specs=[row, key, key],
        out_shape=[like(q), like(k), like(v)],
        scratch_shapes=[pltpu.VMEM((SIZE, keys), high_type)] * 2,
        cost_estimate=cost(B, count, keys, 5),
        compiler_params=pltpu.CompilerParams(vmem_limit_bytes=VMEM_LIMIT),
        name="cross_backward",
    )(q, k, v, mark, o, total, do)


def self_call(body, b, inputs, more, earlier, T, S, outs, out_specs, products, name):
    q, far, mark, table = inputs[0], inputs[3].shape[1], inputs[6], inputs[7]
    count = S * T
    row = pl.BlockSpec((SIZE, count), lambda h: (h, b))
    far_row = pl.BlockSpec((SIZE, far), lambda h: (h, 0))
    total = pl.BlockSpec((None, None, 1, count), lambda h: (b, h, 0, 0))
    specs = [row, row, row, far_row, far_row, pl.BlockSpec((BUCKETS, count), lambda h: (h, b))]
    specs.append(pl.BlockSpec((None, 16, far + T), lambda h: (b, 0, 0)))
    specs.append(pl.BlockSpec(table.shape, lambda h: (0, 0)))
    specs += [row, total, row][: len(more)]
    held = len(specs)
    return pl.pallas_call(
        functools.partial(body, T=T, S=S),
        grid=(HEADS,),
        in_specs=specs + [pl.BlockSpec(memory_space=pl.ANY)] * len(earlier),
        out_specs=out_specs,
        out_shape=outs,
        input_output_aliases={held + i: i for i in range(len(earlier))},
        cost_estimate=cost(1, count, far + T, products),
        compiler_params=pltpu.CompilerParams(vmem_limit_bytes=VMEM_LIMIT),
        name=name,
    )(*inputs, *more, *earlier)


def self_forward(b, inputs, earlier, T, S):
    q, mark, count = inputs[0], inputs[6], S * T
    return self_call(
        self_forward_kernel,
        b,
        inputs,
        (),
        earlier,
        T,
        S,
        [like(q), jax.ShapeDtypeStruct((mark.shape[0], HEADS, 1, count), high_type)],
        [
            pl.BlockSpec((SIZE, count), lambda h: (h, b)),
            pl.BlockSpec((None, None, 1, count), lambda h: (b, h, 0, 0)),
        ],
        2,
        "self_forward",
    )


def self_backward(b, inputs, more, earlier, T, S):
    q, rel, count, far = inputs[0], inputs[5], S * T, inputs[3].shape[1]

    def pair(columns):
        return jax.ShapeDtypeStruct((2, q.shape[0], columns), low_type)

    return self_call(
        self_backward_kernel,
        b,
        inputs,
        more,
        earlier,
        T,
        S,
        [like(q), pair(q.shape[1]), like(rel), pair(far)],
        [
            pl.BlockSpec((SIZE, count), lambda h: (h, b)),
            pl.BlockSpec((2, SIZE, count), lambda h: (0, h, b)),
            pl.BlockSpec((BUCKETS, count), lambda h: (h, b)),
            pl.BlockSpec((2, SIZE, far), lambda h: (0, h, 0)),
        ],
        5,
        "self_backward",
    )


def weight_grads(xs, gs, specs, terms, parts, sums, out, name):
    width = xs[0].shape[1]
    columns = out[2] // SPLIT
    flops = sum(2 * width * out[2] * xs[x_at].shape[0] for term in terms for x_at, _ in term)
    return pl.pallas_call(
        functools.partial(weight_grads_kernel, xs=len(xs), terms=terms, parts=parts, sums=sums),
        grid=(SPLIT, len(terms)),
        in_specs=[pl.BlockSpec(x.shape, lambda e, c: (0, 0)) for x in xs] + specs,
        out_specs=[
            pl.BlockSpec((out[0], out[1], columns), lambda e, c: (0, 0, e)),
            pl.BlockSpec((len(terms), columns, TILE), lambda e, c: (0, e, 0)),
        ],
        out_shape=[
            jax.ShapeDtypeStruct(out, low_type),
            jax.ShapeDtypeStruct((len(terms), out[2], TILE), high_type),
        ],
        cost_estimate=pl.CostEstimate(
            flops=flops, bytes_accessed=flops // 256, transcendentals=0
        ),
        compiler_params=pltpu.CompilerParams(vmem_limit_bytes=VMEM_LIMIT),
        name=name,
    )(*xs, *gs)


def back_rows(gs, ws, base, joined, tile, name):
    width, columns = 1024, BACK_COLUMNS

    def spec(entry, shape, index):
        if isinstance(entry, tuple):
            return pl.BlockSpec((None,) + shape, lambda r, d, w=entry[1]: (w,) + index(r, d))
        return pl.BlockSpec(shape, index)

    arrays = [e[0] if isinstance(e, tuple) else e for e in gs]
    weights = [e[0] if isinstance(e, tuple) else e for e in ws]
    rows = arrays[0].shape[-1]
    sizes = [a.shape[-2] for a in arrays]
    specs = [spec(e, (f, tile), lambda r, d: (0, r)) for e, f in zip(gs, sizes, strict=True)]
    specs += [spec(e, (columns, f), lambda r, d: (d, 0)) for e, f in zip(ws, sizes, strict=True)]
    extra = []
    if base is not None:
        specs.append(pl.BlockSpec((tile, columns), lambda r, d: (r, d)))
        extra.append(base)
    if joined is not None:
        specs.append(pl.BlockSpec((joined.shape[0] * tile // rows, columns), lambda r, d: (r, d)))
        extra.append(joined)
    return pl.pallas_call(
        functools.partial(
            back_rows_kernel, pairs=len(gs), base=base is not None, joined=joined is not None
        ),
        grid=(rows // tile, width // columns),
        in_specs=specs,
        out_specs=pl.BlockSpec((tile, columns), lambda r, d: (r, d)),
        out_shape=jax.ShapeDtypeStruct((rows, width), low_type),
        cost_estimate=pl.CostEstimate(
            flops=2 * rows * width * sum(sizes),
            bytes_accessed=2 * (rows + width) * sum(sizes) + 6 * rows * width,
            transcendentals=0,
        ),
        compiler_params=pltpu.CompilerParams(vmem_limit_bytes=VMEM_LIMIT),
        name=name,
    )(*arrays, *weights, *extra)


def ffn_kernel(x_ref, w_ref, b_ref, g_ref, slope_ref, *, step):
    x = x_ref[...]
    for at in range(0, w_ref.shape[1], step):
        u = contract(x, w_ref[:, at : at + step], 1, 0) + b_ref[:, at : at + step]
        t = 1.0 / (1.0 + (0.3275911 * 0.5**0.5) * jnp.abs(u))
        bell = jnp.exp2(u * u * (-0.5 / math.log(2.0)))
        poly = 0.7107068705 + t * (-0.7265760135 + t * 0.5307027145)
        tail = bell * (t * (0.127414796 + t * (-0.142248368 + t * poly)))
        phi = jnp.where(u < 0.0, tail, 1.0 - tail)
        g_ref[:, at : at + step] = (u * phi).astype(low_type)
        slope_ref[:, at : at + step] = (phi + u * (bell * (2.0 * math.pi) ** -0.5)).astype(low_type)


def ffn_first(x, w, b):
    rows, width = x.shape
    hidden = w.shape[1]
    tm, tn = math.gcd(rows, FFN_ROWS), math.gcd(hidden, FFN_COLS)
    block = pl.BlockSpec((tm, tn), lambda j, i: (i, j))
    out = jax.ShapeDtypeStruct((rows, hidden), low_type)
    return pl.pallas_call(
        functools.partial(ffn_kernel, step=FFN_STEP),
        grid=(hidden // tn, rows // tm),
        in_specs=[
            pl.BlockSpec((tm, width), lambda j, i: (i, 0)),
            pl.BlockSpec((width, tn), lambda j, i: (0, j)),
            pl.BlockSpec((1, tn), lambda j, i: (0, j)),
        ],
        out_specs=[block, block],
        out_shape=[out, out],
        cost_estimate=pl.CostEstimate(
            flops=2 * rows * width * hidden, bytes_accessed=4 * rows * hidden, transcendentals=rows * hidden
        ),
        compiler_params=pltpu.CompilerParams(vmem_limit_bytes=VMEM_LIMIT),
        name="ffn_first",
    )(x, w, b)


def column_sum(value):
    return jnp.sum(value.astype(high_type), 0)


def row_sum(value):
    return jnp.sum(value.astype(high_type), 1)


def dot(spec, left, right):
    return jnp.einsum(spec, left, right, preferred_element_type=high_type)


def norm_parts(value):
    center = value - jnp.mean(value, -1, keepdims=True)
    inverse = lax.rsqrt(jnp.mean(center * center, -1, keepdims=True) + EPSILON)
    return center * inverse, inverse


def norm_back(value, grad, gain):
    unit, inverse = norm_parts(value)
    scaled = grad * gain
    back = inverse * (
        scaled
        - jnp.mean(scaled, -1, keepdims=True)
        - unit * jnp.mean(scaled * unit, -1, keepdims=True)
    )
    return back, jnp.sum(grad * unit, 0), jnp.sum(grad, 0)


def rounded(value):
    return lax.optimization_barrier(value.astype(jnp.bfloat16)).astype(jnp.float32)


def layer_norm(value, gain, shift):
    center = value - jnp.mean(value, -1, keepdims=True)
    spread = jnp.mean(center * center, -1, keepdims=True)
    return center * lax.rsqrt(spread + EPSILON) * gain + shift


def gelu_exact(value):
    return jax.nn.gelu(value, approximate=False)


def bucket_of(distance):
    half = BUCKETS // 2
    counted = jnp.zeros_like(distance)
    for level in range(1, half):
        bound = math.ceil(half * (MAX_DIST / half) ** (level / half))
        counted = counted + (distance >= bound).astype(jnp.int32)
    return jnp.where(distance < half, distance, half + counted)


def self_logits(query_s, key_s, rel_s, keys_s, dec_len, offset_pos):
    streams, local_len, heads, size = query_s.shape
    full_len = keys_s.shape[0]
    scale = size ** (-0.5)
    positions = offset_pos + jnp.arange(local_len, dtype=jnp.int32)
    key_positions = jnp.arange(full_len, dtype=jnp.int32)
    distance = positions[:, None] - key_positions[None, :]
    one_hot = (
        bucket_of(jnp.maximum(distance, 0))[:, :, None] == jnp.arange(BUCKETS, dtype=jnp.int32)
    ).astype(jnp.float32)
    scores = scale * jnp.einsum(
        "sqhd,khd->shqk", query_s, keys_s, preferred_element_type=jnp.float32
    )
    scores = scores + jnp.einsum("sqhb,qkb->shqk", rel_s, one_hot, precision=lax.Precision.HIGHEST)
    stream_ids = jnp.arange(streams, dtype=jnp.int32)
    allowed = (distance[None] >= jnp.minimum(stream_ids, 1)[:, None, None]) & (
        key_positions < dec_len
    )[None, None, :]
    scores = jnp.where(allowed[:, None], scores, NEGATIVE)
    own_score = (
        scale * jnp.sum(query_s.astype(jnp.float32) * key_s.astype(jnp.float32), -1) + rel_s[..., 0]
    )
    own_score = jnp.where(
        (stream_ids > 0)[:, None, None], jnp.transpose(own_score, (0, 2, 1)), NEGATIVE
    )
    return (scores, own_score, one_hot)


def plain_self_forward(items, offset_pos):
    query_s, key_s, value_s, rel_s, keys_s, values_s, dec_len = items
    scores, own_score, one_hot = self_logits(query_s, key_s, rel_s, keys_s, dec_len, offset_pos)
    peak = jnp.maximum(jnp.max(scores, -1), own_score)
    log_total = peak + jnp.log(
        jnp.sum(jnp.exp(scores - peak[..., None]), -1) + jnp.exp(own_score - peak)
    )
    weights = jnp.exp(scores - log_total[..., None]).astype(jnp.bfloat16)
    own_weight = rounded(jnp.exp(own_score - log_total))
    mixed = jnp.einsum("shqk,khd->sqhd", weights, values_s, preferred_element_type=jnp.float32)
    mixed = mixed + jnp.transpose(own_weight, (0, 2, 1))[..., None] * value_s.astype(jnp.float32)
    return (mixed.astype(jnp.bfloat16), log_total)


def plain_self_backward(items, offset_pos):
    query_s, key_s, value_s, rel_s, keys_s, values_s, dec_len, log_total, grad_s = items
    scores, own_score, one_hot = self_logits(query_s, key_s, rel_s, keys_s, dec_len, offset_pos)
    scale = query_s.shape[3] ** (-0.5)
    weights = jnp.exp(scores - log_total[..., None])
    own_weight = jnp.exp(own_score - log_total)
    grad_float = grad_s.astype(jnp.float32)
    grad_weights = jnp.einsum(
        "sqhd,khd->shqk", grad_s, values_s, preferred_element_type=jnp.float32
    )
    grad_own = jnp.transpose(jnp.sum(grad_float * value_s.astype(jnp.float32), -1), (0, 2, 1))
    delta = jnp.sum(grad_weights * weights, -1) + grad_own * own_weight
    grad_scores = (weights * (grad_weights - delta[..., None])).astype(jnp.bfloat16)
    grad_own_score = rounded(own_weight * (grad_own - delta))
    own_term = jnp.transpose(grad_own_score, (0, 2, 1))[..., None]
    grad_query = scale * (
        jnp.einsum("shqk,khd->sqhd", grad_scores, keys_s, preferred_element_type=jnp.float32)
        + own_term * key_s.astype(jnp.float32)
    )
    grad_keys = scale * jnp.einsum(
        "shqk,sqhd->khd", grad_scores, query_s, preferred_element_type=jnp.float32
    )
    grad_key_own = scale * own_term * query_s.astype(jnp.float32)
    grad_values = jnp.einsum(
        "shqk,sqhd->khd", weights.astype(jnp.bfloat16), grad_s, preferred_element_type=jnp.float32
    )
    grad_value_own = jnp.transpose(rounded(own_weight), (0, 2, 1))[..., None] * grad_float
    grad_rel = jnp.einsum(
        "shqk,qkb->sqhb", grad_scores.astype(jnp.float32), one_hot, precision=lax.Precision.HIGHEST
    )
    grad_rel = grad_rel.at[..., 0].add(jnp.transpose(grad_own_score, (0, 2, 1)))
    return (grad_query, grad_key_own, grad_value_own, grad_keys, grad_values, grad_rel)


def cross_logits(query_s, keys_s, enc_len):
    scale = query_s.shape[3] ** (-0.5)
    scores = scale * jnp.einsum(
        "sqhd,khd->shqk", query_s, keys_s, preferred_element_type=jnp.float32
    )
    key_positions = jnp.arange(keys_s.shape[0], dtype=jnp.int32)
    return jnp.where(key_positions < enc_len, scores, NEGATIVE)


def plain_cross_forward(items):
    query_s, keys_s, values_s, enc_len = items
    scores = cross_logits(query_s, keys_s, enc_len)
    peak = jnp.max(scores, -1)
    log_total = peak + jnp.log(jnp.sum(jnp.exp(scores - peak[..., None]), -1))
    weights = jnp.exp(scores - log_total[..., None]).astype(jnp.bfloat16)
    mixed = jnp.einsum("shqk,khd->sqhd", weights, values_s, preferred_element_type=jnp.float32)
    return (mixed.astype(jnp.bfloat16), log_total)


def plain_cross_backward(items):
    query_s, keys_s, values_s, enc_len, log_total, grad_s = items
    scale = query_s.shape[3] ** (-0.5)
    scores = cross_logits(query_s, keys_s, enc_len)
    weights = jnp.exp(scores - log_total[..., None])
    grad_weights = jnp.einsum(
        "sqhd,khd->shqk", grad_s, values_s, preferred_element_type=jnp.float32
    )
    delta = jnp.sum(grad_weights * weights, -1)
    grad_scores = (weights * (grad_weights - delta[..., None])).astype(jnp.bfloat16)
    grad_query = scale * jnp.einsum(
        "shqk,khd->sqhd", grad_scores, keys_s, preferred_element_type=jnp.float32
    )
    grad_keys = scale * jnp.einsum(
        "shqk,sqhd->khd", grad_scores, query_s, preferred_element_type=jnp.float32
    )
    grad_values = jnp.einsum(
        "shqk,sqhd->khd", weights.astype(jnp.bfloat16), grad_s, preferred_element_type=jnp.float32
    )
    return (grad_query, grad_keys, grad_values)


def plain_on_device(
    hidden,
    encoder_out,
    cotangent,
    dec_lengths,
    enc_lengths,
    self_qkv,
    self_qv_bias,
    self_out,
    self_out_bias,
    rel_weight,
    rel_bias,
    cross_qkv,
    cross_qv_bias,
    cross_out,
    cross_out_bias,
    ffn_in,
    ffn_in_bias,
    ffn_out,
    ffn_out_bias,
    norm_gain,
    norm_bias,
):
    seq_count, streams, local_len, width = hidden.shape
    seq_parts = lax.axis_size("seq")
    dp_parts = lax.axis_size("dp")
    full_len = local_len * seq_parts
    offset_pos = lax.axis_index("seq") * local_len
    heads = HEADS
    size = width // heads
    head_shape = (seq_count, streams, local_len, heads, size)
    all_shape = (seq_count, full_len, heads, size)
    kv_shape = (seq_count, full_len, width)
    rows = hidden.reshape(-1, width)
    row_count = rows.shape[0]
    gains = norm_gain.astype(high_type)
    shifts = norm_bias.astype(high_type)
    self_bias = self_qv_bias.astype(high_type)
    cross_bias = cross_qv_bias.astype(high_type)
    projected = jnp.einsum("rd,cde->cre", rows, self_qkv, preferred_element_type=high_type)
    query = (projected[0] + self_bias[0]).astype(low_type)
    key = projected[1].astype(low_type)
    value = (projected[2] + self_bias[1]).astype(low_type)
    rel_logits = jnp.dot(rows, rel_weight, preferred_element_type=high_type) + rel_bias.astype(
        high_type
    )
    rel_heads = rel_logits.reshape(seq_count, streams, local_len, heads, BUCKETS)
    key_main = key.reshape(seq_count, streams, local_len, width)[:, 0]
    value_main = value.reshape(seq_count, streams, local_len, width)[:, 0]
    keys_all, values_all = (
        lax.all_gather(key_main, "seq", axis=1, tiled=True),
        lax.all_gather(value_main, "seq", axis=1, tiled=True),
    )
    self_items = (
        query.reshape(head_shape),
        key.reshape(head_shape),
        value.reshape(head_shape),
        rel_heads,
        keys_all.reshape(all_shape),
        values_all.reshape(all_shape),
        dec_lengths,
    )
    attended, self_total = lax.map(lambda items: plain_self_forward(items, offset_pos), self_items)
    attended = attended.reshape(row_count, width)
    self_branch = jnp.dot(
        attended, self_out, preferred_element_type=high_type
    ) + self_out_bias.astype(high_type)
    first_sum = rows.astype(high_type) + self_branch
    first_norm = layer_norm(first_sum, gains[0], shifts[0])
    first_low = first_norm.astype(low_type)
    cross_query = (
        jnp.dot(first_low, cross_qkv[0], preferred_element_type=high_type) + cross_bias[0]
    ).astype(low_type)
    encoder_rows = encoder_out.reshape(-1, width)
    encoder_proj = jnp.einsum(
        "rd,cde->cre", encoder_rows, cross_qkv[1:], preferred_element_type=high_type
    )
    cross_key = encoder_proj[0].astype(low_type).reshape(seq_count, local_len, width)
    cross_value = (
        (encoder_proj[1] + cross_bias[1]).astype(low_type).reshape(seq_count, local_len, width)
    )
    cross_keys, cross_values = (
        lax.all_gather(cross_key, "seq", axis=1, tiled=True),
        lax.all_gather(cross_value, "seq", axis=1, tiled=True),
    )
    cross_items = (
        cross_query.reshape(head_shape),
        cross_keys.reshape(all_shape),
        cross_values.reshape(all_shape),
        enc_lengths,
    )
    cross_mixed, cross_total = lax.map(plain_cross_forward, cross_items)
    cross_mixed = cross_mixed.reshape(row_count, width)
    cross_branch = jnp.dot(
        cross_mixed, cross_out, preferred_element_type=high_type
    ) + cross_out_bias.astype(high_type)
    second_sum = first_norm + cross_branch
    second_norm = layer_norm(second_sum, gains[1], shifts[1])
    second_low = second_norm.astype(low_type)
    hidden_pre = jnp.dot(second_low, ffn_in, preferred_element_type=high_type) + ffn_in_bias.astype(
        high_type
    )
    activated = gelu_exact(hidden_pre).astype(low_type)
    ffn_branch = jnp.dot(
        activated, ffn_out, preferred_element_type=high_type
    ) + ffn_out_bias.astype(high_type)
    third_sum = second_norm + ffn_branch
    output = layer_norm(third_sum, gains[2], shifts[2]).astype(low_type).reshape(hidden.shape)
    third_value, norm_pull = jax.vjp(layer_norm, third_sum, gains[2], shifts[2])
    grad_third, grad_gain_ffn, grad_shift_ffn = norm_pull(
        cotangent.reshape(-1, width).astype(high_type)
    )
    grad_ffn = grad_third.astype(low_type)
    grad_ffn_out = jnp.einsum("rf,rd->fd", activated, grad_ffn, preferred_element_type=high_type)
    grad_ffn_out_bias = column_sum(grad_ffn)
    grad_activated = jnp.einsum("rd,fd->rf", grad_ffn, ffn_out, preferred_element_type=high_type)
    gelu_value, gelu_pull = jax.vjp(gelu_exact, hidden_pre)
    grad_pre = gelu_pull(grad_activated)[0].astype(low_type)
    grad_ffn_in = jnp.einsum("rd,rf->df", second_low, grad_pre, preferred_element_type=high_type)
    grad_ffn_in_bias = column_sum(grad_pre)
    grad_second = grad_third + jnp.einsum(
        "rf,df->rd", grad_pre, ffn_in, preferred_element_type=high_type
    )
    second_value, norm_pull = jax.vjp(layer_norm, second_sum, gains[1], shifts[1])
    grad_second_sum, grad_gain_cross, grad_shift_cross = norm_pull(grad_second)
    grad_cross = grad_second_sum.astype(low_type)
    grad_cross_out = jnp.einsum(
        "rd,re->de", cross_mixed, grad_cross, preferred_element_type=high_type
    )
    grad_cross_out_bias = column_sum(grad_cross)
    grad_cross_mixed = jnp.einsum(
        "re,de->rd", grad_cross, cross_out, preferred_element_type=high_type
    ).astype(low_type)
    cross_back_items = (
        cross_query.reshape(head_shape),
        cross_keys.reshape(all_shape),
        cross_values.reshape(all_shape),
        enc_lengths,
        cross_total,
        grad_cross_mixed.reshape(head_shape),
    )
    grad_cross_query, grad_cross_keys, grad_cross_values = lax.map(plain_cross_backward, cross_back_items)
    cross_key_sum, cross_value_sum = (
        lax.psum_scatter(
            grad_cross_keys.reshape(kv_shape).astype(jnp.bfloat16),
            "seq",
            scatter_dimension=1,
            tiled=True,
        ).astype(jnp.float32),
        lax.psum_scatter(
            grad_cross_values.reshape(kv_shape).astype(jnp.bfloat16),
            "seq",
            scatter_dimension=1,
            tiled=True,
        ).astype(jnp.float32),
    )
    query_low = grad_cross_query.reshape(row_count, width).astype(low_type)
    encoder_grads = jnp.stack(
        [cross_key_sum.reshape(-1, width), cross_value_sum.reshape(-1, width)]
    ).astype(low_type)
    grad_cross_query_weight = jnp.einsum(
        "rd,re->de", first_low, query_low, preferred_element_type=high_type
    )
    grad_cross_kv_weight = jnp.einsum(
        "rd,cre->cde", encoder_rows, encoder_grads, preferred_element_type=high_type
    )
    grad_cross_qkv = jnp.concatenate([grad_cross_query_weight[None], grad_cross_kv_weight], 0)
    grad_cross_bias = jnp.stack([column_sum(query_low), column_sum(encoder_grads[1])])
    grad_encoder = jnp.einsum(
        "cre,cde->rd", encoder_grads, cross_qkv[1:], preferred_element_type=high_type
    )
    grad_encoder = grad_encoder.astype(low_type).reshape(encoder_out.shape)
    grad_first = grad_second_sum + jnp.einsum(
        "re,de->rd", query_low, cross_qkv[0], preferred_element_type=high_type
    )
    first_value, norm_pull = jax.vjp(layer_norm, first_sum, gains[0], shifts[0])
    grad_first_sum, grad_gain_self, grad_shift_self = norm_pull(grad_first)
    grad_self = grad_first_sum.astype(low_type)
    grad_self_out = jnp.einsum("rd,re->de", attended, grad_self, preferred_element_type=high_type)
    grad_self_out_bias = column_sum(grad_self)
    grad_attended = jnp.einsum(
        "re,de->rd", grad_self, self_out, preferred_element_type=high_type
    ).astype(low_type)
    self_back_items = (
        query.reshape(head_shape),
        key.reshape(head_shape),
        value.reshape(head_shape),
        rel_heads,
        keys_all.reshape(all_shape),
        values_all.reshape(all_shape),
        dec_lengths,
        self_total,
        grad_attended.reshape(head_shape),
    )
    grad_query, grad_key_own, grad_value_own, grad_keys, grad_values, grad_rel = lax.map(
        lambda items: plain_self_backward(items, offset_pos), self_back_items
    )
    key_sum, value_sum = (
        lax.psum_scatter(
            grad_keys.reshape(kv_shape).astype(jnp.bfloat16), "seq", scatter_dimension=1, tiled=True
        ).astype(jnp.float32),
        lax.psum_scatter(
            grad_values.reshape(kv_shape).astype(jnp.bfloat16),
            "seq",
            scatter_dimension=1,
            tiled=True,
        ).astype(jnp.float32),
    )
    own_shape = (seq_count, streams, local_len, width)
    key_total = jnp.concatenate([key_sum[:, None], grad_key_own.reshape(own_shape)[:, 1:]], 1)
    value_total = jnp.concatenate([value_sum[:, None], grad_value_own.reshape(own_shape)[:, 1:]], 1)
    stacked_grad = jnp.stack(
        [
            grad_query.reshape(row_count, width),
            key_total.reshape(row_count, width),
            value_total.reshape(row_count, width),
        ]
    ).astype(low_type)
    rel_low = grad_rel.reshape(row_count, heads * BUCKETS).astype(low_type)
    grad_self_qkv = jnp.einsum("rd,cre->cde", rows, stacked_grad, preferred_element_type=high_type)
    grad_self_bias = jnp.stack([column_sum(stacked_grad[0]), column_sum(stacked_grad[2])])
    grad_rel_weight = jnp.einsum("rd,rb->db", rows, rel_low, preferred_element_type=high_type)
    grad_rel_bias = column_sum(rel_low)
    grad_rows = grad_first_sum + jnp.einsum(
        "cre,cde->rd", stacked_grad, self_qkv, preferred_element_type=high_type
    )
    grad_rows = grad_rows + jnp.einsum(
        "rb,db->rd", rel_low, rel_weight, preferred_element_type=high_type
    )
    grad_hidden = grad_rows.astype(low_type).reshape(hidden.shape)
    matrices = [
        grad_self_qkv,
        grad_self_out,
        grad_rel_weight,
        grad_cross_qkv,
        grad_cross_out,
        grad_ffn_in,
        grad_ffn_out,
    ]
    vectors = [
        grad_self_bias.reshape(-1),
        grad_self_out_bias,
        grad_rel_bias,
        grad_cross_bias.reshape(-1),
        grad_cross_out_bias,
        grad_ffn_in_bias,
        grad_ffn_out_bias,
        jnp.stack([grad_gain_self, grad_gain_cross, grad_gain_ffn]).reshape(-1),
        jnp.stack([grad_shift_self, grad_shift_cross, grad_shift_ffn]).reshape(-1),
    ]
    vec_blocks = [piece.reshape(seq_parts, -1) for piece in vectors]
    mat_blocks = [piece.reshape(dp_parts, seq_parts, -1) for piece in matrices]
    reduced = (
        lax.psum_scatter(
            mat_blocks[0].astype(jnp.bfloat16), "seq", scatter_dimension=1, tiled=True
        ).astype(jnp.float32),
        lax.psum_scatter(
            mat_blocks[1].astype(jnp.bfloat16), "seq", scatter_dimension=1, tiled=True
        ).astype(jnp.float32),
        lax.psum_scatter(
            mat_blocks[2].astype(jnp.bfloat16), "seq", scatter_dimension=1, tiled=True
        ).astype(jnp.float32),
        lax.psum_scatter(
            mat_blocks[3].astype(jnp.bfloat16), "seq", scatter_dimension=1, tiled=True
        ).astype(jnp.float32),
        lax.psum_scatter(
            mat_blocks[4].astype(jnp.bfloat16), "seq", scatter_dimension=1, tiled=True
        ).astype(jnp.float32),
        lax.psum_scatter(
            mat_blocks[5].astype(jnp.bfloat16), "seq", scatter_dimension=1, tiled=True
        ).astype(jnp.float32),
        lax.psum_scatter(
            mat_blocks[6].astype(jnp.bfloat16), "seq", scatter_dimension=1, tiled=True
        ).astype(jnp.float32),
        lax.psum_scatter(
            vec_blocks[0].astype(jnp.bfloat16), "seq", scatter_dimension=0, tiled=True
        ).astype(jnp.float32),
        lax.psum_scatter(
            vec_blocks[1].astype(jnp.bfloat16), "seq", scatter_dimension=0, tiled=True
        ).astype(jnp.float32),
        lax.psum_scatter(
            vec_blocks[2].astype(jnp.bfloat16), "seq", scatter_dimension=0, tiled=True
        ).astype(jnp.float32),
        lax.psum_scatter(
            vec_blocks[3].astype(jnp.bfloat16), "seq", scatter_dimension=0, tiled=True
        ).astype(jnp.float32),
        lax.psum_scatter(
            vec_blocks[4].astype(jnp.bfloat16), "seq", scatter_dimension=0, tiled=True
        ).astype(jnp.float32),
        lax.psum_scatter(
            vec_blocks[5].astype(jnp.bfloat16), "seq", scatter_dimension=0, tiled=True
        ).astype(jnp.float32),
        lax.psum_scatter(
            vec_blocks[6].astype(jnp.bfloat16), "seq", scatter_dimension=0, tiled=True
        ).astype(jnp.float32),
        lax.psum_scatter(
            vec_blocks[7].astype(jnp.bfloat16), "seq", scatter_dimension=0, tiled=True
        ).astype(jnp.float32),
        lax.psum_scatter(
            vec_blocks[8].astype(jnp.bfloat16), "seq", scatter_dimension=0, tiled=True
        ).astype(jnp.float32),
    )
    mat_done = (
        lax.psum_scatter(
            reduced[0].astype(jnp.bfloat16), "dp", scatter_dimension=0, tiled=True
        ).astype(jnp.float32),
        lax.psum_scatter(
            reduced[1].astype(jnp.bfloat16), "dp", scatter_dimension=0, tiled=True
        ).astype(jnp.float32),
        lax.psum_scatter(
            reduced[2].astype(jnp.bfloat16), "dp", scatter_dimension=0, tiled=True
        ).astype(jnp.float32),
        lax.psum_scatter(
            reduced[3].astype(jnp.bfloat16), "dp", scatter_dimension=0, tiled=True
        ).astype(jnp.float32),
        lax.psum_scatter(
            reduced[4].astype(jnp.bfloat16), "dp", scatter_dimension=0, tiled=True
        ).astype(jnp.float32),
        lax.psum_scatter(
            reduced[5].astype(jnp.bfloat16), "dp", scatter_dimension=0, tiled=True
        ).astype(jnp.float32),
        lax.psum_scatter(
            reduced[6].astype(jnp.bfloat16), "dp", scatter_dimension=0, tiled=True
        ).astype(jnp.float32),
    )
    vec_part = [reduced[7 + index] for index in range(9)]
    vec_done = lax.psum(
        (
            vec_part[0],
            vec_part[1],
            vec_part[2],
            vec_part[3],
            vec_part[4],
            vec_part[5],
            vec_part[6],
            vec_part[7],
            vec_part[8],
        ),
        "dp",
    )
    mats = [piece.reshape(-1) for piece in mat_done]
    vecs = [piece.reshape(-1) for piece in vec_done]
    return (
        output,
        grad_hidden,
        grad_encoder,
        mats[0],
        vecs[0],
        mats[1],
        vecs[1],
        mats[2],
        vecs[2],
        mats[3],
        vecs[3],
        mats[4],
        vecs[4],
        mats[5],
        vecs[5],
        mats[6],
        vecs[6],
        vecs[7],
        vecs[8],
    )


def on_device(
    hidden,
    encoder_out,
    cotangent,
    dec_lengths,
    enc_lengths,
    self_qkv,
    self_qv_bias,
    self_out,
    self_out_bias,
    rel_weight,
    rel_bias,
    cross_qkv,
    cross_qv_bias,
    cross_out,
    cross_out_bias,
    ffn_in,
    ffn_in_bias,
    ffn_out,
    ffn_out_bias,
    norm_gain,
    norm_bias,
):
    B, S, T, width = hidden.shape
    if T % TILE or lax.axis_size("dp") != 8 or width % (32 * 8 * lax.axis_size("seq")):
        return plain_on_device(
            hidden,
            encoder_out,
            cotangent,
            dec_lengths,
            enc_lengths,
            self_qkv,
            self_qv_bias,
            self_out,
            self_out_bias,
            rel_weight,
            rel_bias,
            cross_qkv,
            cross_qv_bias,
            cross_out,
            cross_out_bias,
            ffn_in,
            ffn_in_bias,
            ffn_out,
            ffn_out_bias,
            norm_gain,
            norm_bias,
        )
    seq_parts = lax.axis_size("seq")
    keys = T * seq_parts
    far = keys - T
    place = lax.axis_index("seq")
    gains, shifts = norm_gain.astype(high_type), norm_bias.astype(high_type)
    self_bias, cross_bias = self_qv_bias.astype(high_type), cross_qv_bias.astype(high_type)
    table = jnp.asarray(bucket_table(), low_type)

    after = lax.optimization_barrier
    x = hidden.reshape(B * S * T, width)
    rows = B * S * T
    far_rows = []
    for b in range(B):
        sent = hidden[b, 0]
        if b:
            sent, far_rows[b - 1] = after((sent, far_rows[b - 1]))
        pieces = [
            lax.ppermute(sent, "seq", [(i, i + hop) for i in range(seq_parts - hop)])
            for hop in range(seq_parts - 1, 0, -1)
        ]
        far_rows.append(jnp.concatenate(pieces, 0))
        if b == 0:
            e_own, far_rows[0] = after((encoder_out, far_rows[0]))
    e_all = lax.all_gather(e_own, "seq", axis=1, tiled=True).reshape(-1, width)
    key_at = place * T - far + jnp.arange(keys, dtype=jnp.int32)
    self_mark = key_features((key_at >= 0) & (key_at < dec_lengths[:, None]))
    cross_mark = key_features(jnp.arange(keys, dtype=jnp.int32) < enc_lengths[:, None])

    q = ((dot("de,rd->er", self_qkv[0], x) + self_bias[0][:, None]) * SCALE).astype(low_type)
    rel = dot("db,rd->br", rel_weight, x) + rel_bias.astype(high_type)[:, None]
    k = dot("de,rd->er", self_qkv[1], x).astype(low_type)
    v = (dot("de,rd->er", self_qkv[2], x) + self_bias[1][:, None]).astype(low_type)
    self_inputs, results = [], ()
    for b in range(B):
        k_far = dot("de,rd->er", self_qkv[1], far_rows[b]).astype(low_type)
        v_far = (dot("de,rd->er", self_qkv[2], far_rows[b]) + self_bias[1][:, None]).astype(
            low_type
        )
        self_inputs.append((q, k, v, k_far, v_far, rel, self_mark, table))
        results = self_forward(b, self_inputs[b], results, T, S)
        if b + 1 < B:
            far_rows[b + 1], results = after((far_rows[b + 1], results))
    attended, self_total = results
    first_sum = (
        x.astype(high_type)
        + dot("er,ed->rd", attended, self_out)
        + self_out_bias.astype(high_type)
    )
    first_unit, _ = norm_parts(first_sum)
    first_norm = first_unit * gains[0] + shifts[0]
    first_low = first_norm.astype(low_type)

    qc = ((dot("de,rd->er", cross_qkv[0], first_low) + cross_bias[0][:, None]) * SCALE).astype(
        low_type
    )
    kc = dot("de,rd->er", cross_qkv[1], e_all).astype(low_type)
    vc = (dot("de,rd->er", cross_qkv[2], e_all) + cross_bias[1][:, None]).astype(low_type)
    cross_mixed, cross_total = cross_forward(qc, kc, vc, cross_mark)
    second_sum = (
        first_norm
        + dot("er,ed->rd", cross_mixed, cross_out)
        + cross_out_bias.astype(high_type)
    )
    second_unit, _ = norm_parts(second_sum)
    second_norm = second_unit * gains[1] + shifts[1]
    second_low = second_norm.astype(low_type)

    activated, slope = ffn_first(second_low, ffn_in, ffn_in_bias.astype(high_type)[None])
    third_sum = (
        second_norm + dot("rf,fd->rd", activated, ffn_out) + ffn_out_bias.astype(high_type)
    )
    third_unit, _ = norm_parts(third_sum)
    output = (third_unit * gains[2] + shifts[2]).astype(low_type).reshape(hidden.shape)

    grad_third, grad_gain_ffn, grad_shift_ffn = norm_back(
        third_sum, cotangent.reshape(rows, width).astype(high_type), gains[2]
    )
    grad_ffn = grad_third.astype(low_type)

    def over_dp(piece):
        return lax.psum_scatter(piece, "dp", scatter_dimension=0, tiled=True)

    def over_dp_by_steps(piece, meanwhile, beside, later):
        me = lax.axis_index("dp")

        def swap(pair, bit):
            mine = (me >> bit) & 1
            sent = lax.dynamic_index_in_dim(pair, 1 - mine, 0, keepdims=False)
            kept = lax.dynamic_index_in_dim(pair, mine, 0, keepdims=False)
            came = lax.ppermute(sent, "dp", [(i, i ^ (1 << bit)) for i in range(8)])
            return low(came.astype(high_type) + kept.astype(high_type))

        count = piece.shape[0] // 8
        chip = swap(jnp.swapaxes(piece.reshape(4, 2, count, width), 0, 1), 0)
        chip, meanwhile = after((chip, meanwhile))
        first, second = chip[:, : count // 2], chip[:, count // 2 :]
        first = swap(jnp.swapaxes(first.reshape(2, 2, count // 2, width), 0, 1), 1)
        second = swap(second.reshape(2, 2, count // 2, width), 2)
        first, second, done, later = after((first, second, beside(meanwhile), later))
        return jnp.concatenate([swap(first, 2), swap(second, 1)], 0), done, later

    def over_seq(*pieces):
        cut = [piece.reshape(seq_parts, -1, width) for piece in pieces]
        joined = jnp.concatenate(cut, 1)

        def block(hop):
            return lax.dynamic_index_in_dim(
                joined, (place - hop) % seq_parts, 0, keepdims=False
            ).astype(high_type)

        ring = [(i, (i + 1) % seq_parts) for i in range(seq_parts)]
        held = block(1)
        for hop in range(2, seq_parts + 1):
            came = yield lax.ppermute(held.astype(low_type), "seq", ring)
            held = came.astype(high_type) + block(hop)
        ends = np.cumsum([piece.shape[1] for piece in cut])
        yield [
            held[end - piece.shape[1] : end].reshape(-1)
            for piece, end in zip(cut, ends, strict=True)
        ]

    def finish(steps, item):
        for _ in range(seq_parts - 2):
            item = steps.send(item)
        return steps.send(item)

    def low(value):
        return value.astype(low_type)

    part_ffn_out, grad_ffn = after((low(dot("rf,rd->fd", activated, grad_ffn)), grad_ffn))
    mat_ffn_out = over_dp(part_ffn_out)
    grad_pre = (dot("rd,fd->rf", grad_ffn, ffn_out) * slope.astype(high_type)).astype(low_type)
    part_ffn_in, grad_pre = after((low(dot("rd,rf->df", second_low, grad_pre)), grad_pre))
    mat_ffn_in = over_dp(part_ffn_in)
    grad_second = grad_third + dot("rf,df->rd", grad_pre, ffn_in)
    grad_second_sum, grad_gain_cross, grad_shift_cross = norm_back(
        second_sum, grad_second, gains[1]
    )
    grad_cross = grad_second_sum.astype(low_type)
    part_cross_out, grad_cross = after((low(dot("er,rd->ed", cross_mixed, grad_cross)), grad_cross))
    grad_cross_mixed = dot("ed,rd->er", cross_out, grad_cross).astype(low_type)
    dqc, dkc, dvc = cross_backward(
        qc, kc, vc, cross_mark, cross_mixed, cross_total, grad_cross_mixed
    )
    dqc, dkc, dvc, mat_ffn_out, mat_ffn_in = after((dqc, dkc, dvc, mat_ffn_out, mat_ffn_in))
    ffn_steps = over_seq(mat_ffn_in, mat_ffn_out)
    ffn_item = next(ffn_steps)
    part_encoder = back_rows(
        (dkc, dvc), ((cross_qkv, 1), (cross_qkv, 2)), None, None, keys, "encoder_rows"
    ).reshape(B, keys, width)
    grad_encoder = lax.psum_scatter(part_encoder, "seq", scatter_dimension=1, tiled=True)
    e_all, part_encoder, part_cross_out = after((e_all, part_encoder, part_cross_out))
    mat_cross_out = over_dp(part_cross_out)
    third = 3 * width // 8

    def cut(step, size, blocks):
        found = []
        for block in range(blocks):
            low_at, high_at = max(size * block, width * step), min(size * (block + 1), width * (step + 1))
            if low_at < high_at:
                found.append(((block, low_at - size * block), low_at - width * step, high_at - low_at, 0))
        return found

    columns = width // SPLIT
    part_cross_qkv, cross_sums = weight_grads(
        (first_low, e_all),
        (dqc, dkc, dvc),
        [
            pl.BlockSpec((columns, rows), lambda e, c: (e, 0)),
            pl.BlockSpec((columns, B * keys), lambda e, c: (e, 0)),
            pl.BlockSpec((columns, B * keys), lambda e, c: (e, 0)),
        ],
        [[(0, 0)], [(1, 1)], [(1, 2)]],
        [cut(step, third, 8) for step in range(3)],
        [True, False, True],
        (8, third, width),
        "cross_weights",
    )
    part_cross_qkv = part_cross_qkv.reshape(3 * width, width)
    part_encoder, part_cross_qkv, dqc, ffn_item = after(
        (part_encoder, part_cross_qkv, dqc, ffn_item)
    )
    ffn_item = ffn_steps.send(ffn_item)
    mat_cross_qkv = over_dp(part_cross_qkv)

    grad_first = grad_second_sum + dot("er,de->rd", dqc, cross_qkv[0])
    grad_first_sum, grad_gain_self, grad_shift_self = norm_back(first_sum, grad_first, gains[0])
    grad_self = grad_first_sum.astype(low_type)
    part_self_out, grad_self = after((low(dot("er,rd->ed", attended, grad_self)), grad_self))
    mat_self_out = over_dp(part_self_out)
    grad_attended = dot("ed,rd->er", self_out, grad_self).astype(low_type)
    def give_back(far_grads):
        away = back_rows(
            ((far_grads, 0), (far_grads, 1)), ((self_qkv, 1), (self_qkv, 2)), None, None, far, "far_rows"
        )
        return away, [
            lax.ppermute(
                away[(seq_parts - 1 - hop) * T : (seq_parts - hop) * T],
                "seq",
                [(i + hop, i) for i in range(seq_parts - hop)],
            )
            for hop in range(1, seq_parts)
        ]

    results, came, far_columns = (), [], []
    for b in range(B):
        *results, far_grads = self_backward(
            b, self_inputs[b], (attended, self_total, grad_attended), tuple(results), T, S
        )
        if b:
            far_grads, came[b - 1], grad_encoder, ffn_item = after(
                (far_grads, came[b - 1], grad_encoder, ffn_item)
            )
        far_columns.append(far_grads)
        away, pieces = give_back(far_grads)
        came.append(pieces)
        if b + 1 < B:
            results[0], self_inputs[b + 1], away, ffn_item = after(
                (results[0], self_inputs[b + 1], away, ffn_item)
            )
            for _ in range(seq_parts - 3):
                ffn_item = ffn_steps.send(ffn_item)
    results[0], away = after((results[0], away))
    done_ffn_in, done_ffn_out = ffn_steps.send(ffn_item)
    dq, dkv, drel = results
    blocks, size, rel_size = 8 * seq_parts, 3 * width // (8 * seq_parts), width // (16 * seq_parts)
    part_self, part_sums = weight_grads(
        (x, *far_rows),
        (dq, dkv, dkv, drel) + tuple(far_columns) * 2,
        [
            pl.BlockSpec((columns, rows), lambda e, c: (e, 0)),
            pl.BlockSpec((None, columns, rows), lambda e, c: (0, e, 0)),
            pl.BlockSpec((None, columns, rows), lambda e, c: (1, e, 0)),
            pl.BlockSpec((width // 2, rows), lambda e, c: (0, 0)),
        ]
        + [pl.BlockSpec((None, columns, far), lambda e, c: (0, e, 0))] * B
        + [pl.BlockSpec((None, columns, far), lambda e, c: (1, e, 0))] * B,
        [
            [(0, 0)],
            [(0, 1)] + [(1 + b, 4 + b) for b in range(B)],
            [(0, 2)] + [(1 + b, 4 + B + b) for b in range(B)],
            [(0, 3)],
        ],
        [cut(step, size, blocks) for step in range(3)]
        + [[((block, size), 2 * rel_size * block, rel_size, 1) for block in range(blocks)]],
        [True, False, True, True],
        (blocks, size + rel_size, width),
        "self_weights",
    )
    part_self, came[-1] = after((part_self, came[-1]))
    summands = (grad_self, grad_cross, grad_pre, grad_ffn, part_sums, cross_sums)

    def near_rows(arrays):
        dq, came = arrays
        moved = jnp.concatenate(
            [functools.reduce(jnp.add, [piece.astype(high_type) for piece in came[b]]) for b in range(B)], 0
        )
        return back_rows(
            (dq, (dkv, 0), (dkv, 1), drel),
            ((self_qkv, 0), (self_qkv, 1), (self_qkv, 2), rel_weight),
            grad_first_sum,
            moved,
            S * T,
            "near_rows",
        )

    mat_self, grad_hidden, (mat_cross_out, mat_cross_qkv, mat_self_out, summands) = over_dp_by_steps(
        part_self.reshape(-1, width),
        (dq, came),
        near_rows,
        (mat_cross_out, mat_cross_qkv, mat_self_out, summands),
    )
    grad_hidden = grad_hidden.reshape(hidden.shape)
    grad_self, grad_cross, grad_pre, grad_ffn, part_sums, cross_sums = summands
    vectors = [
        jnp.stack([part_sums[0, :, 0], part_sums[2, :, 0]]),
        column_sum(grad_self),
        part_sums[3, : width // 2, 0],
        jnp.stack([cross_sums[0, :, 0], cross_sums[2, :, 0]]),
        column_sum(grad_cross),
        column_sum(grad_pre),
        column_sum(grad_ffn),
        jnp.stack([grad_gain_self, grad_gain_cross, grad_gain_ffn]),
        jnp.stack([grad_shift_self, grad_shift_cross, grad_shift_ffn]),
    ]
    blocks = [piece.reshape(seq_parts, -1) for piece in vectors]
    ends = np.cumsum([piece.shape[1] for piece in blocks])
    summed = jnp.concatenate(blocks, 1)
    for axis, size_of in (("dp", 8), ("seq", seq_parts)):
        for bit in range(size_of.bit_length() - 1):
            summed = summed + lax.ppermute(summed, axis, [(i, i ^ (1 << bit)) for i in range(size_of)])
    mine = lax.dynamic_index_in_dim(summed, place, 0, keepdims=False)
    cross_steps = over_seq(mat_cross_out, mat_cross_qkv, mat_self_out)
    done_cross_out, done_cross_qkv, done_self_out = finish(cross_steps, next(cross_steps))
    self_steps = over_seq(mat_self)
    (done_self,) = finish(self_steps, next(self_steps))
    done_self = done_self.reshape(size + rel_size, width)
    done_self_qkv = done_self[:size].reshape(-1)
    half = width // 2
    done_rel = jnp.concatenate([done_self[size:, :half], done_self[size:, half:]], 0).reshape(-1)

    vecs = [mine[end - piece.shape[1] : end] for piece, end in zip(blocks, ends, strict=True)]
    return (
        output,
        grad_hidden,
        grad_encoder,
        done_self_qkv,
        vecs[0],
        done_self_out,
        vecs[1],
        done_rel,
        vecs[2],
        done_cross_qkv,
        vecs[3],
        done_cross_out,
        vecs[4],
        done_ffn_in,
        vecs[5],
        done_ffn_out,
        vecs[6],
        vecs[7],
        vecs[8],
    )


def solution(mesh):
    rows, vector, matrix = P("dp", None, "seq", None), P("seq"), P(("dp", "seq"))
    return jax.shard_map(
        on_device,
        mesh=mesh,
        in_specs=(rows, P("dp", "seq", None), rows, P("dp"), P("dp")) + (P(),) * 16,
        out_specs=(rows, rows, P("dp", "seq", None))
        + (matrix, vector) * 7
        + (vector, vector),
        check_vma=False,
    )
```

```python
import functools
import math

import jax
import jax.numpy as jnp
import numpy as np
from jax import lax
from jax.experimental import pallas as pl
from jax.experimental.pallas import tpu as pltpu
from jax.sharding import PartitionSpec as P

HEADS = 16
BUCKETS = 32
MAX_DIST = 128
SIZE = 64
SCALE = 0.125
TILE = 128
NEGATIVE = -1e30
EPSILON = 1e-05
VMEM_LIMIT = 60 * 2**20
GROUPS = {"cross_forward": 4, "cross_backward": 2, "self_forward": 1, "self_backward": 2}
SPLIT = 2
FFN_COLS = 1024
FFN_ROWS = 768
FFN_STEP = 512
BACK_COLUMNS = 512

low_type = jnp.bfloat16
high_type = jnp.float32


def contract(left, right, left_dim, right_dim):
    return lax.dot_general(
        left, right, (((left_dim,), (right_dim,)), ((), ())), preferred_element_type=high_type
    )


def split_two(value):
    top = value.astype(low_type)
    return top, (value - top.astype(high_type)).astype(low_type)


def feature_rows(first, value):
    a = value.astype(low_type).astype(high_type)
    b = (value - a).astype(low_type).astype(high_type)
    c = value - a - b
    count = value.shape[1]
    at = lax.broadcasted_iota(jnp.int32, (16, count), 0)
    out = jnp.where(at == 0, first, 0.0)
    for index, piece in enumerate((a, b, c)):
        out = jnp.where(at == index + 1, piece, out)
    return out.astype(low_type)


def key_features(valid):
    mask = jnp.where(valid, 0.0, NEGATIVE)[:, None, :]
    ones = jnp.ones_like(mask)
    return jnp.concatenate([mask, ones, ones, ones] + [jnp.zeros_like(mask)] * 12, 1).astype(
        low_type
    )


def bucket_table():
    half = BUCKETS // 2
    distance = (TILE - np.arange(2 * TILE)) % (2 * TILE)
    counted = np.zeros_like(distance)
    for level in range(1, half):
        counted = counted + (distance >= math.ceil(half * (MAX_DIST / half) ** (level / half)))
    bucket = np.where(distance < half, distance, half + counted)
    table = (bucket[None, :] == np.arange(BUCKETS)[:, None]).astype(np.float32)
    table[BUCKETS - 1] = -(bucket < BUCKETS - 1).astype(np.float32)
    return table


def near_bias(rel, table):
    top, rest = split_two(rel)
    return contract(
        jnp.concatenate([top, rest], 0), jnp.concatenate([table, table], 0), 0, 0
    )


def cross_forward_kernel(q_ref, k_ref, v_ref, mark_ref, o_ref, total_ref):
    count, keys = q_ref.shape[1], k_ref.shape[1]
    k1 = jnp.concatenate([k_ref[...], mark_ref[...]], 0)
    v1 = jnp.concatenate([v_ref[...], jnp.ones((16, keys), low_type)], 0)
    zero = jnp.zeros((1, count), high_type)
    q1 = jnp.concatenate([q_ref[...], feature_rows(1.0, zero)], 0)
    scores = contract(k1, q1, 0, 0)
    peak = jnp.max(scores, 0, keepdims=True)
    weights = jnp.exp(scores - peak).astype(low_type)
    mixed = contract(v1, weights, 1, 0)
    total = mixed[SIZE : SIZE + 1]
    o_ref[...] = (mixed[:SIZE] * (1.0 / total)).astype(low_type)
    total_ref[...] = peak + jnp.log(total)


def cross_backward_kernel(
    q_ref, k_ref, v_ref, mark_ref, o_ref, total_ref, do_ref, dq_ref, dk_ref, dv_ref, dk_acc, dv_acc, *, step
):
    count, keys = q_ref.shape[1], k_ref.shape[1]
    k = k_ref[...]
    k1 = jnp.concatenate([k, mark_ref[...]], 0)
    v1 = jnp.concatenate([v_ref[...], mark_ref[...]], 0)
    for n in range(0, count, step):
        q, do = q_ref[:, n : n + step], do_ref[:, n : n + step]
        delta = jnp.sum(
            do.astype(high_type) * o_ref[:, n : n + step].astype(high_type), 0, keepdims=True
        )
        q1 = jnp.concatenate([q, feature_rows(1.0, -total_ref[:, n : n + step])], 0)
        do1 = jnp.concatenate([do, feature_rows(0.0, -delta)], 0)
        weights = jnp.exp(contract(q1, k1, 0, 0))
        grad_scores = (weights * contract(do1, v1, 0, 0)).astype(low_type)
        weights = weights.astype(low_type)
        dq_ref[:, n : n + step] = (contract(k, grad_scores, 1, 1) * SCALE).astype(low_type)
        dk = contract(q, grad_scores, 1, 0)
        dv = contract(do, weights, 1, 0)
        if n == 0:
            dk_acc[...] = dk
            dv_acc[...] = dv
        else:
            dk_acc[...] += dk
            dv_acc[...] += dv
    dk_ref[...] = dk_acc[...].astype(low_type)
    dv_ref[...] = dv_acc[...].astype(low_type)


def near_biases(rel, table):
    near = near_bias(rel, table)
    return [
        pltpu.roll(near[row : row + TILE], 0, 1, stride=1, stride_axis=0)
        for row in range(0, near.shape[0], TILE)
    ]


def main_and_own(far_ref, near_ref, T):
    near = near_ref[...]
    return jnp.concatenate([far_ref[...], near[:, :T]], 1), near[:, T:]


def near_window(block, bias, first, main_row):
    at = lax.broadcasted_iota(jnp.int32, (TILE, TILE), 0)
    to = lax.broadcasted_iota(jnp.int32, (TILE, TILE), 1)
    left = block[:, first : first + TILE] + bias[:, :TILE]
    right = block[:, first + TILE : first + 2 * TILE] + bias[:, TILE:]
    return left, jnp.where((to <= at) if main_row else (to < at), right, NEGATIVE)


def self_forward_kernel(*refs, T, S):
    q_ref, k_ref, v_ref, k_far_ref, v_far_ref, rel_ref, mark_ref, table_ref = refs[:8]
    o_ref, total_ref = refs[-2:]
    n, keys = S * T, k_far_ref.shape[1] + T
    q, rel = q_ref[...], rel_ref[...]
    k, own_k = main_and_own(k_far_ref, k_ref, T)
    v, own_v = main_and_own(v_far_ref, v_ref, T)
    biases = near_biases(rel, table_ref[...])
    k1 = jnp.concatenate([k, mark_ref[...]], 0)
    v1 = jnp.concatenate([v, jnp.ones((16, keys), low_type)], 0)
    q1 = jnp.concatenate([q, feature_rows(1.0, rel[BUCKETS - 1 :])], 0)
    scores = contract(q1, k1, 0, 0)
    weights, peaks = [], []
    for s in range(S):
        for r in range(T // TILE):
            row, first = s * T + r * TILE, keys - T + (r - 1) * TILE
            block = scores[row : row + TILE]
            left, right = near_window(block, biases[row // TILE], first, s == 0)
            parts = [left, right]
            peak = jnp.max(jnp.maximum(left, right), 1, keepdims=True)
            if first > 0:
                far = block[:, :first]
                peak = jnp.maximum(peak, jnp.max(far, 1, keepdims=True))
                parts = [far] + parts
            parts = [jnp.exp(part - peak).astype(low_type) for part in parts]
            if first + 2 * TILE < keys:
                parts.append(jnp.zeros((TILE, keys - first - 2 * TILE), low_type))
            weights.append(jnp.concatenate(parts, 1))
            peaks.append(jnp.broadcast_to(peak, (TILE, TILE)).T[0:1])
    mixed = contract(v1, jnp.concatenate(weights, 0), 1, 1)
    peak = jnp.concatenate(peaks, 1)
    total, mixed = mixed[SIZE : SIZE + 1], mixed[:SIZE]
    own_k, own_v = own_k.astype(high_type), own_v.astype(high_type)
    own = jnp.sum(q[:, T:].astype(high_type) * own_k, 0, keepdims=True) + rel[0:1, T:]
    top = jnp.maximum(peak[:, T:], own)
    main_part, own_part = jnp.exp(peak[:, T:] - top), jnp.exp(own - top)
    joined = total[:, T:] * main_part + own_part
    inverse = 1.0 / joined
    o_ref[:, :T] = (mixed[:, :T] * (1.0 / total[:, :T])).astype(low_type)
    o_ref[:, T:] = (mixed[:, T:] * (main_part * inverse) + own_v * (own_part * inverse)).astype(
        low_type
    )
    total_ref[:, :T] = peak[:, :T] + jnp.log(total[:, :T])
    total_ref[:, T:] = top + jnp.log(joined)


def self_backward_kernel(*refs, T, S):
    q_ref, k_ref, v_ref, k_far_ref, v_far_ref, rel_ref, mark_ref, table_ref = refs[:8]
    o_ref, total_ref, do_ref = refs[8:11]
    dq_ref, dkv_ref, drel_ref, far_ref = refs[-4:]
    n, keys = S * T, k_far_ref.shape[1] + T
    far = keys - T
    q, rel, do, total = q_ref[...], rel_ref[...], do_ref[...], total_ref[...]
    table = table_ref[...]
    k, own_k = main_and_own(k_far_ref, k_ref, T)
    v, own_v = main_and_own(v_far_ref, v_ref, T)
    biases = near_biases(rel, table)
    k1 = jnp.concatenate([k, mark_ref[...]], 0)
    v1 = jnp.concatenate([v, mark_ref[...]], 0)
    do_high = do.astype(high_type)
    delta = jnp.sum(do_high * o_ref[...].astype(high_type), 0, keepdims=True)
    q1 = jnp.concatenate([q, feature_rows(1.0, rel[BUCKETS - 1 :] - total)], 0)
    do1 = jnp.concatenate([do, feature_rows(0.0, -delta)], 0)
    scores = contract(q1, k1, 0, 0)
    slopes = contract(do1, v1, 0, 0)
    weights, grads, nears = [], [], []
    for s in range(S):
        for r in range(T // TILE):
            row, first = s * T + r * TILE, keys - T + (r - 1) * TILE
            block, slope = scores[row : row + TILE], slopes[row : row + TILE]
            part = jnp.exp(
                jnp.concatenate(near_window(block, biases[row // TILE], first, s == 0), 1)
            )
            grad = (part * slope[:, first : first + 2 * TILE]).astype(low_type)
            nears.append(grad)
            parts, pieces = [part.astype(low_type)], [grad]
            if first > 0:
                part = jnp.exp(block[:, :first])
                pieces = [(part * slope[:, :first]).astype(low_type)] + pieces
                parts = [part.astype(low_type)] + parts
            if first + 2 * TILE < keys:
                zero = jnp.zeros((TILE, keys - first - 2 * TILE), low_type)
                parts.append(zero)
                pieces.append(zero)
            weights.append(jnp.concatenate(parts, 1))
            grads.append(jnp.concatenate(pieces, 1))
    weights, grads = jnp.concatenate(weights, 0), jnp.concatenate(grads, 0)
    dq = contract(k1, grads, 1, 1)
    dk = contract(q, grads, 1, 0).astype(low_type)
    dv = contract(do, weights, 1, 0).astype(low_type)
    far_ref[0] = dk[:, :far]
    far_ref[1] = dv[:, :far]
    at = lax.broadcasted_iota(jnp.int32, (TILE, TILE), 0)
    to = lax.broadcasted_iota(jnp.int32, (TILE, TILE), 1)
    mirror = (at + to == TILE - 1).astype(high_type).astype(low_type)
    flipped = contract(mirror, jnp.concatenate(nears, 1), 1, 0)
    turned = [
        pltpu.roll(flipped[:, i : i + 2 * TILE], TILE + 1, 1, stride=1, stride_axis=0).astype(low_type)
        for i in range(0, 2 * n, 2 * TILE)
    ]
    top, rest = split_two(contract(table, jnp.concatenate(turned, 0), 1, 1))
    stacked = [part[:, i : i + TILE] for i in range(0, n, TILE) for part in (top, rest)]
    both = contract(jnp.concatenate(stacked, 0), mirror, 1, 0)
    rels = [
        both[i : i + BUCKETS] + both[i + BUCKETS : i + 2 * BUCKETS]
        for i in range(0, both.shape[0], 2 * BUCKETS)
    ]
    row_sums = dq[SIZE + 1 : SIZE + 2]
    own_k, own_v = own_k.astype(high_type), own_v.astype(high_type)
    own_q, own_do = q[:, T:].astype(high_type), do_high[:, T:]
    own = jnp.sum(own_q * own_k, 0, keepdims=True) + rel[0:1, T:]
    own_part = jnp.exp(own - total[:, T:])
    own_grad = own_part * (jnp.sum(own_do * own_v, 0, keepdims=True) - delta[:, T:])
    own_grad = own_grad.astype(low_type).astype(high_type)
    dq_ref[:, :T] = (dq[:SIZE, :T] * SCALE).astype(low_type)
    dq_ref[:, T:] = ((dq[:SIZE, T:] + own_grad * own_k) * SCALE).astype(low_type)
    dkv_ref[0, :, :T] = dk[:, far:]
    dkv_ref[1, :, :T] = dv[:, far:]
    dkv_ref[0, :, T:] = (own_grad * own_q).astype(low_type)
    dkv_ref[1, :, T:] = (own_part.astype(low_type).astype(high_type) * own_do).astype(low_type)
    bucket = lax.broadcasted_iota(jnp.int32, (BUCKETS, n), 0)
    drel = jnp.concatenate(rels, 1) + jnp.where(bucket == BUCKETS - 1, row_sums, 0.0)
    own_all = jnp.concatenate([jnp.zeros((1, T), high_type), own_grad], 1)
    drel_ref[...] = (drel + jnp.where(bucket == 0, own_all, 0.0)).astype(low_type)


def weight_grads_kernel(*refs, xs, terms, parts, sums):
    x_refs, rest = refs[:xs], refs[xs:]
    count = max(place for step in terms for _, place in step) + 1
    g_refs, out_ref = rest[:count], rest[count]
    e, c = pl.program_id(0), pl.program_id(1)

    for step, term in enumerate(terms):

        @pl.when(c == step)
        def _():
            x = jnp.concatenate([x_refs[x_at][...] for x_at, _ in term], 0)
            g = jnp.concatenate([g_refs[g_at][...] for _, g_at in term], 1)
            total = contract(x, g, 0, 1)
            if sums[step]:
                line = jnp.sum(g.astype(high_type), 1, keepdims=True)
                rest[count + 1][step] = jnp.broadcast_to(line, (line.shape[0], TILE))
            total = total.astype(low_type)
            for at, row, rows, halves in parts[step]:
                if halves:
                    kept = jnp.where(e < halves, total[row : row + rows], total[row + rows : row + 2 * rows])
                else:
                    kept = total[row : row + rows]
                out_ref[at[0], at[1] : at[1] + rows, :] = kept


def back_rows_kernel(*refs, pairs, base, joined):
    gs, ws, rest, out_ref = refs[:pairs], refs[pairs : 2 * pairs], refs[2 * pairs : -1], refs[-1]
    total = rest[0][...] if base else None
    for g_ref, w_ref in zip(gs, ws, strict=True):
        piece = contract(g_ref[...], w_ref[...], 0, 1)
        total = piece if total is None else total + piece
    if joined:
        add = rest[1][...]
        out_ref[: add.shape[0]] = (total[: add.shape[0]] + add).astype(low_type)
        out_ref[add.shape[0] :] = total[add.shape[0] :].astype(low_type)
    else:
        out_ref[...] = total.astype(low_type)


def by_head(body, group, split, **static):
    def kernel(*refs):
        for head in range(group):
            views = []
            for ref, how in zip(refs, split, strict=True):
                if how is None:
                    views.append(ref)
                elif how == 0:
                    views.append(ref.at[head])
                elif isinstance(how, tuple):
                    views.append(ref.at[:, pl.ds(head * how[1], how[1]), :])
                else:
                    views.append(ref.at[pl.ds(head * how, how), :])
            body(*views, **static)

    return kernel


def per_head(rows, count):
    return pl.BlockSpec((rows, count), lambda b, h: (h, b))


def per_sequence(keys):
    return pl.BlockSpec((None, 16, keys), lambda b, h: (b, 0, 0))


def per_total(group, count):
    return pl.BlockSpec((None, group, 1, count), lambda b, h: (b, h, 0, 0))


def like(array):
    return jax.ShapeDtypeStruct(array.shape, low_type)


def cost(B, rows, keys, products):
    return pl.CostEstimate(
        flops=2 * B * HEADS * rows * keys * 256 * products,
        bytes_accessed=B * HEADS * SIZE * (rows + keys) * 4 * products,
        transcendentals=B * HEADS * rows * keys,
    )


def cross_forward(q, k, v, mark):
    B, _, keys = mark.shape
    count, group = q.shape[1] // B, GROUPS["cross_forward"]
    size = group * SIZE
    return pl.pallas_call(
        by_head(cross_forward_kernel, group, [SIZE, SIZE, SIZE, None, SIZE, 0]),
        grid=(B, HEADS // group),
        in_specs=[per_head(size, count), per_head(size, keys), per_head(size, keys), per_sequence(keys)],
        out_specs=[per_head(size, count), per_total(group, count)],
        out_shape=[like(q), jax.ShapeDtypeStruct((B, HEADS, 1, count), high_type)],
        cost_estimate=cost(B, count, keys, 2),
        compiler_params=pltpu.CompilerParams(vmem_limit_bytes=VMEM_LIMIT),
        name="cross_forward",
    )(q, k, v, mark)


def cross_backward(q, k, v, mark, o, total, do):
    B, _, keys = mark.shape
    count, group = q.shape[1] // B, GROUPS["cross_backward"]
    size = group * SIZE
    row, key = per_head(size, count), per_head(size, keys)
    return pl.pallas_call(
        by_head(
            cross_backward_kernel,
            group,
            [SIZE, SIZE, SIZE, None, SIZE, 0, SIZE, SIZE, SIZE, SIZE, None, None],
            step=count // 2,
        ),
        grid=(B, HEADS // group),
        in_specs=[row, key, key, per_sequence(keys), row, per_total(group, count), row],
        out_specs=[row, key, key],
        out_shape=[like(q), like(k), like(v)],
        scratch_shapes=[pltpu.VMEM((SIZE, keys), high_type)] * 2,
        cost_estimate=cost(B, count, keys, 5),
        compiler_params=pltpu.CompilerParams(vmem_limit_bytes=VMEM_LIMIT),
        name="cross_backward",
    )(q, k, v, mark, o, total, do)


def self_call(body, b, inputs, more, earlier, T, S, outs, out_specs, out_split, products, name):
    q, far, mark, table = inputs[0], inputs[3].shape[1], inputs[6], inputs[7]
    count, group = S * T, GROUPS[name]
    row = pl.BlockSpec((group * SIZE, count), lambda h: (h, b))
    far_row = pl.BlockSpec((group * SIZE, far), lambda h: (h, 0))
    total = pl.BlockSpec((None, group, 1, count), lambda h: (b, h, 0, 0))
    specs = [row, row, row, far_row, far_row, pl.BlockSpec((group * BUCKETS, count), lambda h: (h, b))]
    specs.append(pl.BlockSpec((None, 16, far + T), lambda h: (b, 0, 0)))
    specs.append(pl.BlockSpec(table.shape, lambda h: (0, 0)))
    specs += [row, total, row][: len(more)]
    held = len(specs)
    return pl.pallas_call(
        by_head(
            body,
            group,
            [SIZE] * 5
            + [BUCKETS, None, None]
            + [SIZE, 0, SIZE][: len(more)]
            + [None] * len(earlier)
            + out_split,
            T=T,
            S=S,
        ),
        grid=(HEADS // group,),
        in_specs=specs + [pl.BlockSpec(memory_space=pl.ANY)] * len(earlier),
        out_specs=out_specs,
        out_shape=outs,
        input_output_aliases={held + i: i for i in range(len(earlier))},
        cost_estimate=cost(1, count, far + T, products),
        compiler_params=pltpu.CompilerParams(vmem_limit_bytes=VMEM_LIMIT),
        name=name,
    )(*inputs, *more, *earlier)


def self_forward(b, inputs, earlier, T, S):
    q, mark, count, group = inputs[0], inputs[6], S * T, GROUPS["self_forward"]
    return self_call(
        self_forward_kernel,
        b,
        inputs,
        (),
        earlier,
        T,
        S,
        [like(q), jax.ShapeDtypeStruct((mark.shape[0], HEADS, 1, count), high_type)],
        [
            pl.BlockSpec((group * SIZE, count), lambda h: (h, b)),
            pl.BlockSpec((None, group, 1, count), lambda h: (b, h, 0, 0)),
        ],
        [SIZE, 0],
        2,
        "self_forward",
    )


def self_backward(b, inputs, more, earlier, T, S):
    q, rel, count, far = inputs[0], inputs[5], S * T, inputs[3].shape[1]
    group = GROUPS["self_backward"]

    def pair(columns):
        return jax.ShapeDtypeStruct((2, q.shape[0], columns), low_type)

    return self_call(
        self_backward_kernel,
        b,
        inputs,
        more,
        earlier,
        T,
        S,
        [like(q), pair(q.shape[1]), like(rel), pair(far)],
        [
            pl.BlockSpec((group * SIZE, count), lambda h: (h, b)),
            pl.BlockSpec((2, group * SIZE, count), lambda h: (0, h, b)),
            pl.BlockSpec((group * BUCKETS, count), lambda h: (h, b)),
            pl.BlockSpec((2, group * SIZE, far), lambda h: (0, h, 0)),
        ],
        [SIZE, (2, SIZE), BUCKETS, (2, SIZE)],
        5,
        "self_backward",
    )


def weight_grads(xs, gs, specs, terms, parts, sums, out, name):
    width = xs[0].shape[1]
    columns = out[2] // SPLIT
    flops = sum(2 * width * out[2] * xs[x_at].shape[0] for term in terms for x_at, _ in term)
    return pl.pallas_call(
        functools.partial(weight_grads_kernel, xs=len(xs), terms=terms, parts=parts, sums=sums),
        grid=(SPLIT, len(terms)),
        in_specs=[pl.BlockSpec(x.shape, lambda e, c: (0, 0)) for x in xs] + specs,
        out_specs=[
            pl.BlockSpec((out[0], out[1], columns), lambda e, c: (0, 0, e)),
            pl.BlockSpec((len(terms), columns, TILE), lambda e, c: (0, e, 0)),
        ],
        out_shape=[
            jax.ShapeDtypeStruct(out, low_type),
            jax.ShapeDtypeStruct((len(terms), out[2], TILE), high_type),
        ],
        cost_estimate=pl.CostEstimate(
            flops=flops, bytes_accessed=flops // 256, transcendentals=0
        ),
        compiler_params=pltpu.CompilerParams(vmem_limit_bytes=VMEM_LIMIT),
        name=name,
    )(*xs, *gs)


def back_rows(gs, ws, base, joined, tile, name):
    width, columns = 1024, BACK_COLUMNS

    def spec(entry, shape, index):
        if isinstance(entry, tuple):
            return pl.BlockSpec((None,) + shape, lambda r, d, w=entry[1]: (w,) + index(r, d))
        return pl.BlockSpec(shape, index)

    arrays = [e[0] if isinstance(e, tuple) else e for e in gs]
    weights = [e[0] if isinstance(e, tuple) else e for e in ws]
    rows = arrays[0].shape[-1]
    sizes = [a.shape[-2] for a in arrays]
    specs = [spec(e, (f, tile), lambda r, d: (0, r)) for e, f in zip(gs, sizes, strict=True)]
    specs += [spec(e, (columns, f), lambda r, d: (d, 0)) for e, f in zip(ws, sizes, strict=True)]
    extra = []
    if base is not None:
        specs.append(pl.BlockSpec((tile, columns), lambda r, d: (r, d)))
        extra.append(base)
    if joined is not None:
        specs.append(pl.BlockSpec((joined.shape[0] * tile // rows, columns), lambda r, d: (r, d)))
        extra.append(joined)
    return pl.pallas_call(
        functools.partial(
            back_rows_kernel, pairs=len(gs), base=base is not None, joined=joined is not None
        ),
        grid=(rows // tile, width // columns),
        in_specs=specs,
        out_specs=pl.BlockSpec((tile, columns), lambda r, d: (r, d)),
        out_shape=jax.ShapeDtypeStruct((rows, width), low_type),
        cost_estimate=pl.CostEstimate(
            flops=2 * rows * width * sum(sizes),
            bytes_accessed=2 * (rows + width) * sum(sizes) + 6 * rows * width,
            transcendentals=0,
        ),
        compiler_params=pltpu.CompilerParams(vmem_limit_bytes=VMEM_LIMIT),
        name=name,
    )(*arrays, *weights, *extra)


def keys_and_values_kernel(x_ref, wk_ref, wv_ref, b_ref, k_ref, v_ref):
    x = x_ref[...]
    k_ref[...] = contract(wk_ref[...], x, 0, 1).astype(low_type)
    v_ref[...] = (contract(wv_ref[...], x, 0, 1) + b_ref[...]).astype(low_type)


def keys_and_values(x, weights, bias):
    rows, width = x.shape
    columns = width // SPLIT
    out = jax.ShapeDtypeStruct((width, rows), low_type)
    return pl.pallas_call(
        keys_and_values_kernel,
        grid=(SPLIT,),
        in_specs=[
            pl.BlockSpec((rows, width), lambda e: (0, 0)),
            pl.BlockSpec((None, width, columns), lambda e: (1, 0, e)),
            pl.BlockSpec((None, width, columns), lambda e: (2, 0, e)),
            pl.BlockSpec((columns, 1), lambda e: (e, 0)),
        ],
        out_specs=[pl.BlockSpec((columns, rows), lambda e: (e, 0))] * 2,
        out_shape=[out, out],
        cost_estimate=pl.CostEstimate(
            flops=4 * rows * width * width,
            bytes_accessed=2 * (3 * rows * width + 2 * width * width),
            transcendentals=0,
        ),
        compiler_params=pltpu.CompilerParams(vmem_limit_bytes=VMEM_LIMIT),
        name="keys_and_values",
    )(x, weights, weights, bias[:, None])


def ffn_kernel(x_ref, w_ref, b_ref, g_ref, slope_ref, *, step):
    x = x_ref[...]
    for at in range(0, w_ref.shape[1], step):
        u = contract(x, w_ref[:, at : at + step], 1, 0) + b_ref[:, at : at + step]
        t = 1.0 / (1.0 + (0.3275911 * 0.5**0.5) * jnp.abs(u))
        bell = jnp.exp2(u * u * (-0.5 / math.log(2.0)))
        poly = 0.7107068705 + t * (-0.7265760135 + t * 0.5307027145)
        tail = bell * (t * (0.127414796 + t * (-0.142248368 + t * poly)))
        phi = jnp.where(u < 0.0, tail, 1.0 - tail)
        g_ref[:, at : at + step] = (u * phi).astype(low_type)
        slope_ref[:, at : at + step] = (phi + u * (bell * (2.0 * math.pi) ** -0.5)).astype(low_type)


def ffn_first(x, w, b):
    rows, width = x.shape
    hidden = w.shape[1]
    tm, tn = math.gcd(rows, FFN_ROWS), math.gcd(hidden, FFN_COLS)
    block = pl.BlockSpec((tm, tn), lambda j, i: (i, j))
    out = jax.ShapeDtypeStruct((rows, hidden), low_type)
    return pl.pallas_call(
        functools.partial(ffn_kernel, step=FFN_STEP),
        grid=(hidden // tn, rows // tm),
        in_specs=[
            pl.BlockSpec((tm, width), lambda j, i: (i, 0)),
            pl.BlockSpec((width, tn), lambda j, i: (0, j)),
            pl.BlockSpec((1, tn), lambda j, i: (0, j)),
        ],
        out_specs=[block, block],
        out_shape=[out, out],
        cost_estimate=pl.CostEstimate(
            flops=2 * rows * width * hidden, bytes_accessed=4 * rows * hidden, transcendentals=rows * hidden
        ),
        compiler_params=pltpu.CompilerParams(vmem_limit_bytes=VMEM_LIMIT),
        name="ffn_first",
    )(x, w, b)


def column_sum(value):
    return jnp.sum(value.astype(high_type), 0)


def row_sum(value):
    return jnp.sum(value.astype(high_type), 1)


def dot(spec, left, right):
    return jnp.einsum(spec, left, right, preferred_element_type=high_type)


def norm_parts(value):
    center = value - jnp.mean(value, -1, keepdims=True)
    inverse = lax.rsqrt(jnp.mean(center * center, -1, keepdims=True) + EPSILON)
    return center * inverse, inverse


def norm_back(value, grad, gain):
    unit, inverse = norm_parts(value)
    scaled = grad * gain
    back = inverse * (
        scaled
        - jnp.mean(scaled, -1, keepdims=True)
        - unit * jnp.mean(scaled * unit, -1, keepdims=True)
    )
    return back, jnp.sum(grad * unit, 0), jnp.sum(grad, 0)


def rounded(value):
    return lax.optimization_barrier(value.astype(jnp.bfloat16)).astype(jnp.float32)


def layer_norm(value, gain, shift):
    center = value - jnp.mean(value, -1, keepdims=True)
    spread = jnp.mean(center * center, -1, keepdims=True)
    return center * lax.rsqrt(spread + EPSILON) * gain + shift


def gelu_exact(value):
    return jax.nn.gelu(value, approximate=False)


def bucket_of(distance):
    half = BUCKETS // 2
    counted = jnp.zeros_like(distance)
    for level in range(1, half):
        bound = math.ceil(half * (MAX_DIST / half) ** (level / half))
        counted = counted + (distance >= bound).astype(jnp.int32)
    return jnp.where(distance < half, distance, half + counted)


def self_logits(query_s, key_s, rel_s, keys_s, dec_len, offset_pos):
    streams, local_len, heads, size = query_s.shape
    full_len = keys_s.shape[0]
    scale = size ** (-0.5)
    positions = offset_pos + jnp.arange(local_len, dtype=jnp.int32)
    key_positions = jnp.arange(full_len, dtype=jnp.int32)
    distance = positions[:, None] - key_positions[None, :]
    one_hot = (
        bucket_of(jnp.maximum(distance, 0))[:, :, None] == jnp.arange(BUCKETS, dtype=jnp.int32)
    ).astype(jnp.float32)
    scores = scale * jnp.einsum(
        "sqhd,khd->shqk", query_s, keys_s, preferred_element_type=jnp.float32
    )
    scores = scores + jnp.einsum("sqhb,qkb->shqk", rel_s, one_hot, precision=lax.Precision.HIGHEST)
    stream_ids = jnp.arange(streams, dtype=jnp.int32)
    allowed = (distance[None] >= jnp.minimum(stream_ids, 1)[:, None, None]) & (
        key_positions < dec_len
    )[None, None, :]
    scores = jnp.where(allowed[:, None], scores, NEGATIVE)
    own_score = (
        scale * jnp.sum(query_s.astype(jnp.float32) * key_s.astype(jnp.float32), -1) + rel_s[..., 0]
    )
    own_score = jnp.where(
        (stream_ids > 0)[:, None, None], jnp.transpose(own_score, (0, 2, 1)), NEGATIVE
    )
    return (scores, own_score, one_hot)


def plain_self_forward(items, offset_pos):
    query_s, key_s, value_s, rel_s, keys_s, values_s, dec_len = items
    scores, own_score, one_hot = self_logits(query_s, key_s, rel_s, keys_s, dec_len, offset_pos)
    peak = jnp.maximum(jnp.max(scores, -1), own_score)
    log_total = peak + jnp.log(
        jnp.sum(jnp.exp(scores - peak[..., None]), -1) + jnp.exp(own_score - peak)
    )
    weights = jnp.exp(scores - log_total[..., None]).astype(jnp.bfloat16)
    own_weight = rounded(jnp.exp(own_score - log_total))
    mixed = jnp.einsum("shqk,khd->sqhd", weights, values_s, preferred_element_type=jnp.float32)
    mixed = mixed + jnp.transpose(own_weight, (0, 2, 1))[..., None] * value_s.astype(jnp.float32)
    return (mixed.astype(jnp.bfloat16), log_total)


def plain_self_backward(items, offset_pos):
    query_s, key_s, value_s, rel_s, keys_s, values_s, dec_len, log_total, grad_s = items
    scores, own_score, one_hot = self_logits(query_s, key_s, rel_s, keys_s, dec_len, offset_pos)
    scale = query_s.shape[3] ** (-0.5)
    weights = jnp.exp(scores - log_total[..., None])
    own_weight = jnp.exp(own_score - log_total)
    grad_float = grad_s.astype(jnp.float32)
    grad_weights = jnp.einsum(
        "sqhd,khd->shqk", grad_s, values_s, preferred_element_type=jnp.float32
    )
    grad_own = jnp.transpose(jnp.sum(grad_float * value_s.astype(jnp.float32), -1), (0, 2, 1))
    delta = jnp.sum(grad_weights * weights, -1) + grad_own * own_weight
    grad_scores = (weights * (grad_weights - delta[..., None])).astype(jnp.bfloat16)
    grad_own_score = rounded(own_weight * (grad_own - delta))
    own_term = jnp.transpose(grad_own_score, (0, 2, 1))[..., None]
    grad_query = scale * (
        jnp.einsum("shqk,khd->sqhd", grad_scores, keys_s, preferred_element_type=jnp.float32)
        + own_term * key_s.astype(jnp.float32)
    )
    grad_keys = scale * jnp.einsum(
        "shqk,sqhd->khd", grad_scores, query_s, preferred_element_type=jnp.float32
    )
    grad_key_own = scale * own_term * query_s.astype(jnp.float32)
    grad_values = jnp.einsum(
        "shqk,sqhd->khd", weights.astype(jnp.bfloat16), grad_s, preferred_element_type=jnp.float32
    )
    grad_value_own = jnp.transpose(rounded(own_weight), (0, 2, 1))[..., None] * grad_float
    grad_rel = jnp.einsum(
        "shqk,qkb->sqhb", grad_scores.astype(jnp.float32), one_hot, precision=lax.Precision.HIGHEST
    )
    grad_rel = grad_rel.at[..., 0].add(jnp.transpose(grad_own_score, (0, 2, 1)))
    return (grad_query, grad_key_own, grad_value_own, grad_keys, grad_values, grad_rel)


def cross_logits(query_s, keys_s, enc_len):
    scale = query_s.shape[3] ** (-0.5)
    scores = scale * jnp.einsum(
        "sqhd,khd->shqk", query_s, keys_s, preferred_element_type=jnp.float32
    )
    key_positions = jnp.arange(keys_s.shape[0], dtype=jnp.int32)
    return jnp.where(key_positions < enc_len, scores, NEGATIVE)


def plain_cross_forward(items):
    query_s, keys_s, values_s, enc_len = items
    scores = cross_logits(query_s, keys_s, enc_len)
    peak = jnp.max(scores, -1)
    log_total = peak + jnp.log(jnp.sum(jnp.exp(scores - peak[..., None]), -1))
    weights = jnp.exp(scores - log_total[..., None]).astype(jnp.bfloat16)
    mixed = jnp.einsum("shqk,khd->sqhd", weights, values_s, preferred_element_type=jnp.float32)
    return (mixed.astype(jnp.bfloat16), log_total)


def plain_cross_backward(items):
    query_s, keys_s, values_s, enc_len, log_total, grad_s = items
    scale = query_s.shape[3] ** (-0.5)
    scores = cross_logits(query_s, keys_s, enc_len)
    weights = jnp.exp(scores - log_total[..., None])
    grad_weights = jnp.einsum(
        "sqhd,khd->shqk", grad_s, values_s, preferred_element_type=jnp.float32
    )
    delta = jnp.sum(grad_weights * weights, -1)
    grad_scores = (weights * (grad_weights - delta[..., None])).astype(jnp.bfloat16)
    grad_query = scale * jnp.einsum(
        "shqk,khd->sqhd", grad_scores, keys_s, preferred_element_type=jnp.float32
    )
    grad_keys = scale * jnp.einsum(
        "shqk,sqhd->khd", grad_scores, query_s, preferred_element_type=jnp.float32
    )
    grad_values = jnp.einsum(
        "shqk,sqhd->khd", weights.astype(jnp.bfloat16), grad_s, preferred_element_type=jnp.float32
    )
    return (grad_query, grad_keys, grad_values)


def plain_on_device(
    hidden,
    encoder_out,
    cotangent,
    dec_lengths,
    enc_lengths,
    self_qkv,
    self_qv_bias,
    self_out,
    self_out_bias,
    rel_weight,
    rel_bias,
    cross_qkv,
    cross_qv_bias,
    cross_out,
    cross_out_bias,
    ffn_in,
    ffn_in_bias,
    ffn_out,
    ffn_out_bias,
    norm_gain,
    norm_bias,
):
    seq_count, streams, local_len, width = hidden.shape
    seq_parts = lax.axis_size("seq")
    dp_parts = lax.axis_size("dp")
    full_len = local_len * seq_parts
    offset_pos = lax.axis_index("seq") * local_len
    heads = HEADS
    size = width // heads
    head_shape = (seq_count, streams, local_len, heads, size)
    all_shape = (seq_count, full_len, heads, size)
    kv_shape = (seq_count, full_len, width)
    rows = hidden.reshape(-1, width)
    row_count = rows.shape[0]
    gains = norm_gain.astype(high_type)
    shifts = norm_bias.astype(high_type)
    self_bias = self_qv_bias.astype(high_type)
    cross_bias = cross_qv_bias.astype(high_type)
    projected = jnp.einsum("rd,cde->cre", rows, self_qkv, preferred_element_type=high_type)
    query = (projected[0] + self_bias[0]).astype(low_type)
    key = projected[1].astype(low_type)
    value = (projected[2] + self_bias[1]).astype(low_type)
    rel_logits = jnp.dot(rows, rel_weight, preferred_element_type=high_type) + rel_bias.astype(
        high_type
    )
    rel_heads = rel_logits.reshape(seq_count, streams, local_len, heads, BUCKETS)
    key_main = key.reshape(seq_count, streams, local_len, width)[:, 0]
    value_main = value.reshape(seq_count, streams, local_len, width)[:, 0]
    keys_all, values_all = (
        lax.all_gather(key_main, "seq", axis=1, tiled=True),
        lax.all_gather(value_main, "seq", axis=1, tiled=True),
    )
    self_items = (
        query.reshape(head_shape),
        key.reshape(head_shape),
        value.reshape(head_shape),
        rel_heads,
        keys_all.reshape(all_shape),
        values_all.reshape(all_shape),
        dec_lengths,
    )
    attended, self_total = lax.map(lambda items: plain_self_forward(items, offset_pos), self_items)
    attended = attended.reshape(row_count, width)
    self_branch = jnp.dot(
        attended, self_out, preferred_element_type=high_type
    ) + self_out_bias.astype(high_type)
    first_sum = rows.astype(high_type) + self_branch
    first_norm = layer_norm(first_sum, gains[0], shifts[0])
    first_low = first_norm.astype(low_type)
    cross_query = (
        jnp.dot(first_low, cross_qkv[0], preferred_element_type=high_type) + cross_bias[0]
    ).astype(low_type)
    encoder_rows = encoder_out.reshape(-1, width)
    encoder_proj = jnp.einsum(
        "rd,cde->cre", encoder_rows, cross_qkv[1:], preferred_element_type=high_type
    )
    cross_key = encoder_proj[0].astype(low_type).reshape(seq_count, local_len, width)
    cross_value = (
        (encoder_proj[1] + cross_bias[1]).astype(low_type).reshape(seq_count, local_len, width)
    )
    cross_keys, cross_values = (
        lax.all_gather(cross_key, "seq", axis=1, tiled=True),
        lax.all_gather(cross_value, "seq", axis=1, tiled=True),
    )
    cross_items = (
        cross_query.reshape(head_shape),
        cross_keys.reshape(all_shape),
        cross_values.reshape(all_shape),
        enc_lengths,
    )
    cross_mixed, cross_total = lax.map(plain_cross_forward, cross_items)
    cross_mixed = cross_mixed.reshape(row_count, width)
    cross_branch = jnp.dot(
        cross_mixed, cross_out, preferred_element_type=high_type
    ) + cross_out_bias.astype(high_type)
    second_sum = first_norm + cross_branch
    second_norm = layer_norm(second_sum, gains[1], shifts[1])
    second_low = second_norm.astype(low_type)
    hidden_pre = jnp.dot(second_low, ffn_in, preferred_element_type=high_type) + ffn_in_bias.astype(
        high_type
    )
    activated = gelu_exact(hidden_pre).astype(low_type)
    ffn_branch = jnp.dot(
        activated, ffn_out, preferred_element_type=high_type
    ) + ffn_out_bias.astype(high_type)
    third_sum = second_norm + ffn_branch
    output = layer_norm(third_sum, gains[2], shifts[2]).astype(low_type).reshape(hidden.shape)
    third_value, norm_pull = jax.vjp(layer_norm, third_sum, gains[2], shifts[2])
    grad_third, grad_gain_ffn, grad_shift_ffn = norm_pull(
        cotangent.reshape(-1, width).astype(high_type)
    )
    grad_ffn = grad_third.astype(low_type)
    grad_ffn_out = jnp.einsum("rf,rd->fd", activated, grad_ffn, preferred_element_type=high_type)
    grad_ffn_out_bias = column_sum(grad_ffn)
    grad_activated = jnp.einsum("rd,fd->rf", grad_ffn, ffn_out, preferred_element_type=high_type)
    gelu_value, gelu_pull = jax.vjp(gelu_exact, hidden_pre)
    grad_pre = gelu_pull(grad_activated)[0].astype(low_type)
    grad_ffn_in = jnp.einsum("rd,rf->df", second_low, grad_pre, preferred_element_type=high_type)
    grad_ffn_in_bias = column_sum(grad_pre)
    grad_second = grad_third + jnp.einsum(
        "rf,df->rd", grad_pre, ffn_in, preferred_element_type=high_type
    )
    second_value, norm_pull = jax.vjp(layer_norm, second_sum, gains[1], shifts[1])
    grad_second_sum, grad_gain_cross, grad_shift_cross = norm_pull(grad_second)
    grad_cross = grad_second_sum.astype(low_type)
    grad_cross_out = jnp.einsum(
        "rd,re->de", cross_mixed, grad_cross, preferred_element_type=high_type
    )
    grad_cross_out_bias = column_sum(grad_cross)
    grad_cross_mixed = jnp.einsum(
        "re,de->rd", grad_cross, cross_out, preferred_element_type=high_type
    ).astype(low_type)
    cross_back_items = (
        cross_query.reshape(head_shape),
        cross_keys.reshape(all_shape),
        cross_values.reshape(all_shape),
        enc_lengths,
        cross_total,
        grad_cross_mixed.reshape(head_shape),
    )
    grad_cross_query, grad_cross_keys, grad_cross_values = lax.map(plain_cross_backward, cross_back_items)
    cross_key_sum, cross_value_sum = (
        lax.psum_scatter(
            grad_cross_keys.reshape(kv_shape).astype(jnp.bfloat16),
            "seq",
            scatter_dimension=1,
            tiled=True,
        ).astype(jnp.float32),
        lax.psum_scatter(
            grad_cross_values.reshape(kv_shape).astype(jnp.bfloat16),
            "seq",
            scatter_dimension=1,
            tiled=True,
        ).astype(jnp.float32),
    )
    query_low = grad_cross_query.reshape(row_count, width).astype(low_type)
    encoder_grads = jnp.stack(
        [cross_key_sum.reshape(-1, width), cross_value_sum.reshape(-1, width)]
    ).astype(low_type)
    grad_cross_query_weight = jnp.einsum(
        "rd,re->de", first_low, query_low, preferred_element_type=high_type
    )
    grad_cross_kv_weight = jnp.einsum(
        "rd,cre->cde", encoder_rows, encoder_grads, preferred_element_type=high_type
    )
    grad_cross_qkv = jnp.concatenate([grad_cross_query_weight[None], grad_cross_kv_weight], 0)
    grad_cross_bias = jnp.stack([column_sum(query_low), column_sum(encoder_grads[1])])
    grad_encoder = jnp.einsum(
        "cre,cde->rd", encoder_grads, cross_qkv[1:], preferred_element_type=high_type
    )
    grad_encoder = grad_encoder.astype(low_type).reshape(encoder_out.shape)
    grad_first = grad_second_sum + jnp.einsum(
        "re,de->rd", query_low, cross_qkv[0], preferred_element_type=high_type
    )
    first_value, norm_pull = jax.vjp(layer_norm, first_sum, gains[0], shifts[0])
    grad_first_sum, grad_gain_self, grad_shift_self = norm_pull(grad_first)
    grad_self = grad_first_sum.astype(low_type)
    grad_self_out = jnp.einsum("rd,re->de", attended, grad_self, preferred_element_type=high_type)
    grad_self_out_bias = column_sum(grad_self)
    grad_attended = jnp.einsum(
        "re,de->rd", grad_self, self_out, preferred_element_type=high_type
    ).astype(low_type)
    self_back_items = (
        query.reshape(head_shape),
        key.reshape(head_shape),
        value.reshape(head_shape),
        rel_heads,
        keys_all.reshape(all_shape),
        values_all.reshape(all_shape),
        dec_lengths,
        self_total,
        grad_attended.reshape(head_shape),
    )
    grad_query, grad_key_own, grad_value_own, grad_keys, grad_values, grad_rel = lax.map(
        lambda items: plain_self_backward(items, offset_pos), self_back_items
    )
    key_sum, value_sum = (
        lax.psum_scatter(
            grad_keys.reshape(kv_shape).astype(jnp.bfloat16), "seq", scatter_dimension=1, tiled=True
        ).astype(jnp.float32),
        lax.psum_scatter(
            grad_values.reshape(kv_shape).astype(jnp.bfloat16),
            "seq",
            scatter_dimension=1,
            tiled=True,
        ).astype(jnp.float32),
    )
    own_shape = (seq_count, streams, local_len, width)
    key_total = jnp.concatenate([key_sum[:, None], grad_key_own.reshape(own_shape)[:, 1:]], 1)
    value_total = jnp.concatenate([value_sum[:, None], grad_value_own.reshape(own_shape)[:, 1:]], 1)
    stacked_grad = jnp.stack(
        [
            grad_query.reshape(row_count, width),
            key_total.reshape(row_count, width),
            value_total.reshape(row_count, width),
        ]
    ).astype(low_type)
    rel_low = grad_rel.reshape(row_count, heads * BUCKETS).astype(low_type)
    grad_self_qkv = jnp.einsum("rd,cre->cde", rows, stacked_grad, preferred_element_type=high_type)
    grad_self_bias = jnp.stack([column_sum(stacked_grad[0]), column_sum(stacked_grad[2])])
    grad_rel_weight = jnp.einsum("rd,rb->db", rows, rel_low, preferred_element_type=high_type)
    grad_rel_bias = column_sum(rel_low)
    grad_rows = grad_first_sum + jnp.einsum(
        "cre,cde->rd", stacked_grad, self_qkv, preferred_element_type=high_type
    )
    grad_rows = grad_rows + jnp.einsum(
        "rb,db->rd", rel_low, rel_weight, preferred_element_type=high_type
    )
    grad_hidden = grad_rows.astype(low_type).reshape(hidden.shape)
    matrices = [
        grad_self_qkv,
        grad_self_out,
        grad_rel_weight,
        grad_cross_qkv,
        grad_cross_out,
        grad_ffn_in,
        grad_ffn_out,
    ]
    vectors = [
        grad_self_bias.reshape(-1),
        grad_self_out_bias,
        grad_rel_bias,
        grad_cross_bias.reshape(-1),
        grad_cross_out_bias,
        grad_ffn_in_bias,
        grad_ffn_out_bias,
        jnp.stack([grad_gain_self, grad_gain_cross, grad_gain_ffn]).reshape(-1),
        jnp.stack([grad_shift_self, grad_shift_cross, grad_shift_ffn]).reshape(-1),
    ]
    vec_blocks = [piece.reshape(seq_parts, -1) for piece in vectors]
    mat_blocks = [piece.reshape(dp_parts, seq_parts, -1) for piece in matrices]
    reduced = (
        lax.psum_scatter(
            mat_blocks[0].astype(jnp.bfloat16), "seq", scatter_dimension=1, tiled=True
        ).astype(jnp.float32),
        lax.psum_scatter(
            mat_blocks[1].astype(jnp.bfloat16), "seq", scatter_dimension=1, tiled=True
        ).astype(jnp.float32),
        lax.psum_scatter(
            mat_blocks[2].astype(jnp.bfloat16), "seq", scatter_dimension=1, tiled=True
        ).astype(jnp.float32),
        lax.psum_scatter(
            mat_blocks[3].astype(jnp.bfloat16), "seq", scatter_dimension=1, tiled=True
        ).astype(jnp.float32),
        lax.psum_scatter(
            mat_blocks[4].astype(jnp.bfloat16), "seq", scatter_dimension=1, tiled=True
        ).astype(jnp.float32),
        lax.psum_scatter(
            mat_blocks[5].astype(jnp.bfloat16), "seq", scatter_dimension=1, tiled=True
        ).astype(jnp.float32),
        lax.psum_scatter(
            mat_blocks[6].astype(jnp.bfloat16), "seq", scatter_dimension=1, tiled=True
        ).astype(jnp.float32),
        lax.psum_scatter(
            vec_blocks[0].astype(jnp.bfloat16), "seq", scatter_dimension=0, tiled=True
        ).astype(jnp.float32),
        lax.psum_scatter(
            vec_blocks[1].astype(jnp.bfloat16), "seq", scatter_dimension=0, tiled=True
        ).astype(jnp.float32),
        lax.psum_scatter(
            vec_blocks[2].astype(jnp.bfloat16), "seq", scatter_dimension=0, tiled=True
        ).astype(jnp.float32),
        lax.psum_scatter(
            vec_blocks[3].astype(jnp.bfloat16), "seq", scatter_dimension=0, tiled=True
        ).astype(jnp.float32),
        lax.psum_scatter(
            vec_blocks[4].astype(jnp.bfloat16), "seq", scatter_dimension=0, tiled=True
        ).astype(jnp.float32),
        lax.psum_scatter(
            vec_blocks[5].astype(jnp.bfloat16), "seq", scatter_dimension=0, tiled=True
        ).astype(jnp.float32),
        lax.psum_scatter(
            vec_blocks[6].astype(jnp.bfloat16), "seq", scatter_dimension=0, tiled=True
        ).astype(jnp.float32),
        lax.psum_scatter(
            vec_blocks[7].astype(jnp.bfloat16), "seq", scatter_dimension=0, tiled=True
        ).astype(jnp.float32),
        lax.psum_scatter(
            vec_blocks[8].astype(jnp.bfloat16), "seq", scatter_dimension=0, tiled=True
        ).astype(jnp.float32),
    )
    mat_done = (
        lax.psum_scatter(
            reduced[0].astype(jnp.bfloat16), "dp", scatter_dimension=0, tiled=True
        ).astype(jnp.float32),
        lax.psum_scatter(
            reduced[1].astype(jnp.bfloat16), "dp", scatter_dimension=0, tiled=True
        ).astype(jnp.float32),
        lax.psum_scatter(
            reduced[2].astype(jnp.bfloat16), "dp", scatter_dimension=0, tiled=True
        ).astype(jnp.float32),
        lax.psum_scatter(
            reduced[3].astype(jnp.bfloat16), "dp", scatter_dimension=0, tiled=True
        ).astype(jnp.float32),
        lax.psum_scatter(
            reduced[4].astype(jnp.bfloat16), "dp", scatter_dimension=0, tiled=True
        ).astype(jnp.float32),
        lax.psum_scatter(
            reduced[5].astype(jnp.bfloat16), "dp", scatter_dimension=0, tiled=True
        ).astype(jnp.float32),
        lax.psum_scatter(
            reduced[6].astype(jnp.bfloat16), "dp", scatter_dimension=0, tiled=True
        ).astype(jnp.float32),
    )
    vec_part = [reduced[7 + index] for index in range(9)]
    vec_done = lax.psum(
        (
            vec_part[0],
            vec_part[1],
            vec_part[2],
            vec_part[3],
            vec_part[4],
            vec_part[5],
            vec_part[6],
            vec_part[7],
            vec_part[8],
        ),
        "dp",
    )
    mats = [piece.reshape(-1) for piece in mat_done]
    vecs = [piece.reshape(-1) for piece in vec_done]
    return (
        output,
        grad_hidden,
        grad_encoder,
        mats[0],
        vecs[0],
        mats[1],
        vecs[1],
        mats[2],
        vecs[2],
        mats[3],
        vecs[3],
        mats[4],
        vecs[4],
        mats[5],
        vecs[5],
        mats[6],
        vecs[6],
        vecs[7],
        vecs[8],
    )


def on_device(
    hidden,
    encoder_out,
    cotangent,
    dec_lengths,
    enc_lengths,
    self_qkv,
    self_qv_bias,
    self_out,
    self_out_bias,
    rel_weight,
    rel_bias,
    cross_qkv,
    cross_qv_bias,
    cross_out,
    cross_out_bias,
    ffn_in,
    ffn_in_bias,
    ffn_out,
    ffn_out_bias,
    norm_gain,
    norm_bias,
):
    B, S, T, width = hidden.shape
    if T % TILE or lax.axis_size("dp") != 8 or width % (32 * 8 * lax.axis_size("seq")):
        return plain_on_device(
            hidden,
            encoder_out,
            cotangent,
            dec_lengths,
            enc_lengths,
            self_qkv,
            self_qv_bias,
            self_out,
            self_out_bias,
            rel_weight,
            rel_bias,
            cross_qkv,
            cross_qv_bias,
            cross_out,
            cross_out_bias,
            ffn_in,
            ffn_in_bias,
            ffn_out,
            ffn_out_bias,
            norm_gain,
            norm_bias,
        )
    seq_parts = lax.axis_size("seq")
    keys = T * seq_parts
    far = keys - T
    place = lax.axis_index("seq")
    gains, shifts = norm_gain.astype(high_type), norm_bias.astype(high_type)
    self_bias, cross_bias = self_qv_bias.astype(high_type), cross_qv_bias.astype(high_type)
    table = jnp.asarray(bucket_table(), low_type)

    after = lax.optimization_barrier
    x = hidden.reshape(B * S * T, width)
    rows = B * S * T
    far_rows = []
    for b in range(B):
        sent = hidden[b, 0]
        if b:
            sent, far_rows[b - 1] = after((sent, far_rows[b - 1]))
        pieces = [
            lax.ppermute(sent, "seq", [(i, i + hop) for i in range(seq_parts - hop)])
            for hop in range(seq_parts - 1, 0, -1)
        ]
        far_rows.append(jnp.concatenate(pieces, 0))
    key_at = place * T - far + jnp.arange(keys, dtype=jnp.int32)
    self_mark = key_features((key_at >= 0) & (key_at < dec_lengths[:, None]))
    cross_mark = key_features(jnp.arange(keys, dtype=jnp.int32) < enc_lengths[:, None])

    q = ((dot("de,rd->er", self_qkv[0], x) + self_bias[0][:, None]) * SCALE).astype(low_type)
    rel = dot("db,rd->br", rel_weight, x) + rel_bias.astype(high_type)[:, None]
    k = dot("de,rd->er", self_qkv[1], x).astype(low_type)
    v = (dot("de,rd->er", self_qkv[2], x) + self_bias[1][:, None]).astype(low_type)
    self_inputs, results = [], ()
    for b in range(B):
        k_far, v_far = keys_and_values(far_rows[b], self_qkv, self_bias[1])
        if b == 0:
            e_own, k_far = after((encoder_out, k_far))
            e_all = lax.all_gather(e_own, "seq", axis=1, tiled=True).reshape(-1, width)
        self_inputs.append((q, k, v, k_far, v_far, rel, self_mark, table))
        results = self_forward(b, self_inputs[b], results, T, S)
        if b + 1 < B:
            far_rows[b + 1], results = after((far_rows[b + 1], results))
    attended, self_total = results
    first_sum = (
        x.astype(high_type)
        + dot("er,ed->rd", attended, self_out)
        + self_out_bias.astype(high_type)
    )
    first_unit, _ = norm_parts(first_sum)
    first_norm = first_unit * gains[0] + shifts[0]
    first_low = first_norm.astype(low_type)

    qc = ((dot("de,rd->er", cross_qkv[0], first_low) + cross_bias[0][:, None]) * SCALE).astype(
        low_type
    )
    kc, vc = keys_and_values(e_all, cross_qkv, cross_bias[1])
    cross_mixed, cross_total = cross_forward(qc, kc, vc, cross_mark)
    second_sum = (
        first_norm
        + dot("er,ed->rd", cross_mixed, cross_out)
        + cross_out_bias.astype(high_type)
    )
    second_unit, _ = norm_parts(second_sum)
    second_norm = second_unit * gains[1] + shifts[1]
    second_low = second_norm.astype(low_type)

    activated, slope = ffn_first(second_low, ffn_in, ffn_in_bias.astype(high_type)[None])
    third_sum = (
        second_norm + dot("rf,fd->rd", activated, ffn_out) + ffn_out_bias.astype(high_type)
    )
    third_unit, _ = norm_parts(third_sum)
    output = (third_unit * gains[2] + shifts[2]).astype(low_type).reshape(hidden.shape)

    grad_third, grad_gain_ffn, grad_shift_ffn = norm_back(
        third_sum, cotangent.reshape(rows, width).astype(high_type), gains[2]
    )
    grad_ffn = grad_third.astype(low_type)

    def over_dp(piece):
        return lax.psum_scatter(piece, "dp", scatter_dimension=0, tiled=True)

    def over_dp_by_steps(piece, beside_first, first_inputs, beside_second, second_inputs):
        me = lax.axis_index("dp")

        def swap(pair, bit):
            mine = (me >> bit) & 1
            sent = lax.dynamic_index_in_dim(pair, 1 - mine, 0, keepdims=False)
            kept = lax.dynamic_index_in_dim(pair, mine, 0, keepdims=False)
            came = lax.ppermute(sent, "dp", [(i, i ^ (1 << bit)) for i in range(8)])
            return low(came.astype(high_type) + kept.astype(high_type))

        count = piece.shape[0] // 8
        chip = swap(jnp.swapaxes(piece.reshape(4, 2, count, width), 0, 1), 0)
        chip, first_inputs = after((chip, first_inputs))
        first, second = chip[:, : count // 2], chip[:, count // 2 :]
        first = swap(jnp.swapaxes(first.reshape(2, 2, count // 2, width), 0, 1), 1)
        second = swap(second.reshape(2, 2, count // 2, width), 2)
        first, second, done_first, second_inputs = after(
            (first, second, beside_first(first_inputs), second_inputs)
        )
        first, second, done_second = after(
            (swap(first, 2), swap(second, 1), beside_second((done_first[1], *second_inputs)))
        )
        return jnp.concatenate([first, second], 0), done_first, done_second

    def over_seq(*pieces):
        cut = [piece.reshape(seq_parts, -1, width) for piece in pieces]
        joined = jnp.concatenate(cut, 1)

        def block(hop):
            return lax.dynamic_index_in_dim(
                joined, (place - hop) % seq_parts, 0, keepdims=False
            ).astype(high_type)

        ring = [(i, (i + 1) % seq_parts) for i in range(seq_parts)]
        held = block(1)
        for hop in range(2, seq_parts + 1):
            came = yield lax.ppermute(held.astype(low_type), "seq", ring)
            held = came.astype(high_type) + block(hop)
        ends = np.cumsum([piece.shape[1] for piece in cut])
        yield [
            held[end - piece.shape[1] : end].reshape(-1)
            for piece, end in zip(cut, ends, strict=True)
        ]

    def finish(steps, item):
        for _ in range(seq_parts - 2):
            item = steps.send(item)
        return steps.send(item)

    def low(value):
        return value.astype(low_type)

    part_ffn_out, grad_ffn = after((low(dot("rf,rd->fd", activated, grad_ffn)), grad_ffn))
    mat_ffn_out = over_dp(part_ffn_out)
    grad_pre = (dot("rd,fd->rf", grad_ffn, ffn_out) * slope.astype(high_type)).astype(low_type)
    part_ffn_in, grad_pre = after((low(dot("rd,rf->df", second_low, grad_pre)), grad_pre))
    mat_ffn_in = over_dp(part_ffn_in)
    grad_second = grad_third + dot("rf,df->rd", grad_pre, ffn_in)
    grad_second_sum, grad_gain_cross, grad_shift_cross = norm_back(
        second_sum, grad_second, gains[1]
    )
    grad_cross = grad_second_sum.astype(low_type)
    part_cross_out, grad_cross = after((low(dot("er,rd->ed", cross_mixed, grad_cross)), grad_cross))
    grad_cross_mixed = dot("ed,rd->er", cross_out, grad_cross).astype(low_type)
    dqc, dkc, dvc = cross_backward(
        qc, kc, vc, cross_mark, cross_mixed, cross_total, grad_cross_mixed
    )
    dqc, dkc, dvc, mat_ffn_out, mat_ffn_in = after((dqc, dkc, dvc, mat_ffn_out, mat_ffn_in))
    ffn_steps = over_seq(mat_ffn_in, mat_ffn_out)
    ffn_item = next(ffn_steps)
    part_encoder = back_rows(
        (dkc, dvc), ((cross_qkv, 1), (cross_qkv, 2)), None, None, keys, "encoder_rows"
    ).reshape(B, keys, width)
    grad_encoder = lax.psum_scatter(part_encoder, "seq", scatter_dimension=1, tiled=True)
    e_all, part_encoder, part_cross_out = after((e_all, part_encoder, part_cross_out))
    mat_cross_out = over_dp(part_cross_out)
    third = 3 * width // 8

    def cut(step, size, blocks):
        found = []
        for block in range(blocks):
            low_at, high_at = max(size * block, width * step), min(size * (block + 1), width * (step + 1))
            if low_at < high_at:
                found.append(((block, low_at - size * block), low_at - width * step, high_at - low_at, 0))
        return found

    columns = width // SPLIT
    part_cross_qkv, cross_sums = weight_grads(
        (first_low, e_all),
        (dqc, dkc, dvc),
        [
            pl.BlockSpec((columns, rows), lambda e, c: (e, 0)),
            pl.BlockSpec((columns, B * keys), lambda e, c: (e, 0)),
            pl.BlockSpec((columns, B * keys), lambda e, c: (e, 0)),
        ],
        [[(0, 0)], [(1, 1)], [(1, 2)]],
        [cut(step, third, 8) for step in range(3)],
        [True, False, True],
        (8, third, width),
        "cross_weights",
    )
    part_cross_qkv = part_cross_qkv.reshape(3 * width, width)
    part_encoder, part_cross_qkv, dqc, ffn_item = after(
        (part_encoder, part_cross_qkv, dqc, ffn_item)
    )
    ffn_item = ffn_steps.send(ffn_item)
    mat_cross_qkv = over_dp(part_cross_qkv)

    grad_first = grad_second_sum + dot("er,de->rd", dqc, cross_qkv[0])
    grad_first_sum, grad_gain_self, grad_shift_self = norm_back(first_sum, grad_first, gains[0])
    grad_self = grad_first_sum.astype(low_type)
    part_self_out, grad_self = after((low(dot("er,rd->ed", attended, grad_self)), grad_self))
    mat_self_out = over_dp(part_self_out)
    grad_attended = dot("ed,rd->er", self_out, grad_self).astype(low_type)
    def give_back(far_grads):
        away = back_rows(
            ((far_grads, 0), (far_grads, 1)), ((self_qkv, 1), (self_qkv, 2)), None, None, far, "far_rows"
        )
        return away, [
            lax.ppermute(
                away[(seq_parts - 1 - hop) * T : (seq_parts - hop) * T],
                "seq",
                [(i + hop, i) for i in range(seq_parts - hop)],
            )
            for hop in range(1, seq_parts)
        ]

    results, came, far_columns = (), [], []
    for b in range(B):
        *results, far_grads = self_backward(
            b, self_inputs[b], (attended, self_total, grad_attended), tuple(results), T, S
        )
        if b:
            far_grads, came[b - 1], grad_encoder, ffn_item = after(
                (far_grads, came[b - 1], grad_encoder, ffn_item)
            )
            done_ffn_in, done_ffn_out = ffn_steps.send(ffn_item)
        far_columns.append(far_grads)
        away, pieces = give_back(far_grads)
        came.append(pieces)
        if b + 1 < B:
            results[0], self_inputs[b + 1], away, ffn_item = after(
                (results[0], self_inputs[b + 1], away, ffn_item)
            )
            for _ in range(seq_parts - 3):
                ffn_item = ffn_steps.send(ffn_item)
    results[0], away = after((results[0], away))
    dq, dkv, drel = results
    blocks, size, rel_size = 8 * seq_parts, 3 * width // (8 * seq_parts), width // (16 * seq_parts)
    part_self, part_sums = weight_grads(
        (x, *far_rows),
        (dq, dkv, dkv, drel) + tuple(far_columns) * 2,
        [
            pl.BlockSpec((columns, rows), lambda e, c: (e, 0)),
            pl.BlockSpec((None, columns, rows), lambda e, c: (0, e, 0)),
            pl.BlockSpec((None, columns, rows), lambda e, c: (1, e, 0)),
            pl.BlockSpec((width // 2, rows), lambda e, c: (0, 0)),
        ]
        + [pl.BlockSpec((None, columns, far), lambda e, c: (0, e, 0))] * B
        + [pl.BlockSpec((None, columns, far), lambda e, c: (1, e, 0))] * B,
        [
            [(0, 0)],
            [(0, 1)] + [(1 + b, 4 + b) for b in range(B)],
            [(0, 2)] + [(1 + b, 4 + B + b) for b in range(B)],
            [(0, 3)],
        ],
        [cut(step, size, blocks) for step in range(3)]
        + [[((block, size), 2 * rel_size * block, rel_size, 1) for block in range(blocks)]],
        [True, False, True, True],
        (blocks, size + rel_size, width),
        "self_weights",
    )
    part_self, came[-1] = after((part_self, came[-1]))

    def near_rows(arrays):
        dq, came, sums = arrays
        moved = jnp.concatenate(
            [functools.reduce(jnp.add, [piece.astype(high_type) for piece in came[b]]) for b in range(B)], 0
        )
        return back_rows(
            (dq, (dkv, 0), (dkv, 1), drel),
            ((self_qkv, 0), (self_qkv, 1), (self_qkv, 2), rel_weight),
            grad_first_sum,
            moved,
            S * T,
            "near_rows",
        ), sums

    def vector_sums(arrays):
        sums, part_sums, cross_sums = arrays
        vectors = [
            jnp.stack([part_sums[0, :, 0], part_sums[2, :, 0]]),
            sums[0],
            part_sums[3, : width // 2, 0],
            jnp.stack([cross_sums[0, :, 0], cross_sums[2, :, 0]]),
            sums[1],
            sums[2],
            sums[3],
            jnp.stack([grad_gain_self, grad_gain_cross, grad_gain_ffn]),
            jnp.stack([grad_shift_self, grad_shift_cross, grad_shift_ffn]),
        ]
        blocks = [piece.reshape(seq_parts, -1) for piece in vectors]
        summed = jnp.concatenate(blocks, 1)
        for bit in range(3):
            summed = summed + lax.ppermute(summed, "dp", [(i, i ^ (1 << bit)) for i in range(8)])
        return summed, [piece.shape[1] for piece in blocks]

    lengths = []

    cross_steps = None

    def second_window(arrays):
        nonlocal cross_steps
        cross_steps = over_seq(*arrays[3:])
        summed, found = vector_sums(arrays[:3])
        lengths.extend(found)
        return summed, next(cross_steps)

    part_self, summands = after((part_self, (grad_self, grad_cross, grad_pre, grad_ffn)))
    sums = [column_sum(summand) for summand in summands]
    mat_self, (grad_hidden, sums), (summed, cross_item) = over_dp_by_steps(
        part_self.reshape(-1, width),
        near_rows,
        (dq, came, sums),
        second_window,
        (part_sums, cross_sums, mat_cross_out, mat_cross_qkv, mat_self_out),
    )
    grad_hidden = grad_hidden.reshape(hidden.shape)
    done_cross_out, done_cross_qkv, done_self_out = finish(cross_steps, cross_item)
    ends = np.cumsum(lengths)
    lines = -(-int(ends[-1]) // (16 * width)) * 16
    summed = jnp.pad(summed, ((0, 0), (0, lines * width - int(ends[-1]))))
    self_steps = over_seq(mat_self, low(summed))
    done_self, mine = finish(self_steps, next(self_steps))
    done_self = done_self.reshape(size + rel_size, width)
    done_self_qkv = done_self[:size].reshape(-1)
    half = width // 2
    done_rel = jnp.concatenate([done_self[size:, :half], done_self[size:, half:]], 0).reshape(-1)
    vecs = [mine[end - count : end] for count, end in zip(lengths, ends, strict=True)]
    return (
        output,
        grad_hidden,
        grad_encoder,
        done_self_qkv,
        vecs[0],
        done_self_out,
        vecs[1],
        done_rel,
        vecs[2],
        done_cross_qkv,
        vecs[3],
        done_cross_out,
        vecs[4],
        done_ffn_in,
        vecs[5],
        done_ffn_out,
        vecs[6],
        vecs[7],
        vecs[8],
    )


def solution(mesh):
    rows, vector, matrix = P("dp", None, "seq", None), P("seq"), P(("dp", "seq"))
    return jax.shard_map(
        on_device,
        mesh=mesh,
        in_specs=(rows, P("dp", "seq", None), rows, P("dp"), P("dp")) + (P(),) * 16,
        out_specs=(rows, rows, P("dp", "seq", None))
        + (matrix, vector) * 7
        + (vector, vector),
        check_vma=False,
    )
```

```python
import functools
import math

import jax
import jax.numpy as jnp
import numpy as np
from jax import lax
from jax.experimental import pallas as pl
from jax.experimental.pallas import tpu as pltpu
from jax.sharding import PartitionSpec as P

HEADS = 16
BUCKETS = 32
MAX_DIST = 128
SIZE = 64
SCALE = 0.125
TILE = 128
NEGATIVE = -1e30
EPSILON = 1e-05
VMEM_LIMIT = 60 * 2**20
GROUPS = {"cross_forward": 4, "cross_backward": 2, "self_forward": 1, "self_backward": 2}
SPLIT = 2
FFN_COLS = 1024
FFN_ROWS = 768
FFN_STEP = 512
BACK_COLUMNS = 512

low_type = jnp.bfloat16
high_type = jnp.float32


def contract(left, right, left_dim, right_dim):
    return lax.dot_general(
        left, right, (((left_dim,), (right_dim,)), ((), ())), preferred_element_type=high_type
    )


def split_two(value):
    top = value.astype(low_type)
    return top, (value - top.astype(high_type)).astype(low_type)


def feature_rows(first, value):
    a = value.astype(low_type).astype(high_type)
    b = (value - a).astype(low_type).astype(high_type)
    c = value - a - b
    count = value.shape[1]
    at = lax.broadcasted_iota(jnp.int32, (16, count), 0)
    out = jnp.where(at == 0, first, 0.0)
    for index, piece in enumerate((a, b, c)):
        out = jnp.where(at == index + 1, piece, out)
    return out.astype(low_type)


def key_features(valid):
    mask = jnp.where(valid, 0.0, NEGATIVE)[:, None, :]
    ones = jnp.ones_like(mask)
    return jnp.concatenate([mask, ones, ones, ones] + [jnp.zeros_like(mask)] * 12, 1).astype(
        low_type
    )


def bucket_table():
    half = BUCKETS // 2
    distance = (TILE - np.arange(2 * TILE)) % (2 * TILE)
    counted = np.zeros_like(distance)
    for level in range(1, half):
        counted = counted + (distance >= math.ceil(half * (MAX_DIST / half) ** (level / half)))
    bucket = np.where(distance < half, distance, half + counted)
    table = (bucket[None, :] == np.arange(BUCKETS)[:, None]).astype(np.float32)
    table[BUCKETS - 1] = -(bucket < BUCKETS - 1).astype(np.float32)
    return table


def near_bias(rel, table):
    top, rest = split_two(rel)
    return contract(
        jnp.concatenate([top, rest], 0), jnp.concatenate([table, table], 0), 0, 0
    )


def cross_forward_kernel(q_ref, k_ref, v_ref, mark_ref, o_ref, total_ref):
    count, keys = q_ref.shape[1], k_ref.shape[1]
    k1 = jnp.concatenate([k_ref[...], mark_ref[...]], 0)
    v1 = jnp.concatenate([v_ref[...], jnp.ones((16, keys), low_type)], 0)
    zero = jnp.zeros((1, count), high_type)
    q1 = jnp.concatenate([q_ref[...], feature_rows(1.0, zero)], 0)
    scores = contract(k1, q1, 0, 0)
    peak = jnp.max(scores, 0, keepdims=True)
    weights = jnp.exp(scores - peak).astype(low_type)
    mixed = contract(v1, weights, 1, 0)
    total = mixed[SIZE : SIZE + 1]
    o_ref[...] = (mixed[:SIZE] * (1.0 / total)).astype(low_type)
    total_ref[...] = peak + jnp.log(total)


def cross_backward_kernel(
    q_ref, k_ref, v_ref, mark_ref, o_ref, total_ref, do_ref, dq_ref, dk_ref, dv_ref, dk_acc, dv_acc, *, step
):
    count, keys = q_ref.shape[1], k_ref.shape[1]
    k = k_ref[...]
    k1 = jnp.concatenate([k, mark_ref[...]], 0)
    v1 = jnp.concatenate([v_ref[...], mark_ref[...]], 0)
    for n in range(0, count, step):
        q, do = q_ref[:, n : n + step], do_ref[:, n : n + step]
        delta = jnp.sum(
            do.astype(high_type) * o_ref[:, n : n + step].astype(high_type), 0, keepdims=True
        )
        q1 = jnp.concatenate([q, feature_rows(1.0, -total_ref[:, n : n + step])], 0)
        do1 = jnp.concatenate([do, feature_rows(0.0, -delta)], 0)
        weights = jnp.exp(contract(q1, k1, 0, 0))
        grad_scores = (weights * contract(do1, v1, 0, 0)).astype(low_type)
        weights = weights.astype(low_type)
        dq_ref[:, n : n + step] = (contract(k, grad_scores, 1, 1) * SCALE).astype(low_type)
        dk = contract(q, grad_scores, 1, 0)
        dv = contract(do, weights, 1, 0)
        if n == 0:
            dk_acc[...] = dk
            dv_acc[...] = dv
        else:
            dk_acc[...] += dk
            dv_acc[...] += dv
    dk_ref[...] = dk_acc[...].astype(low_type)
    dv_ref[...] = dv_acc[...].astype(low_type)


def near_biases(rel, table):
    near = near_bias(rel, table)
    return [
        pltpu.roll(near[row : row + TILE], 0, 1, stride=1, stride_axis=0)
        for row in range(0, near.shape[0], TILE)
    ]


def main_and_own(far_ref, near_ref, T):
    near = near_ref[...]
    return jnp.concatenate([far_ref[...], near[:, :T]], 1), near[:, T:]


def near_window(block, bias, first, main_row):
    at = lax.broadcasted_iota(jnp.int32, (TILE, TILE), 0)
    to = lax.broadcasted_iota(jnp.int32, (TILE, TILE), 1)
    left = block[:, first : first + TILE] + bias[:, :TILE]
    right = block[:, first + TILE : first + 2 * TILE] + bias[:, TILE:]
    return left, jnp.where((to <= at) if main_row else (to < at), right, NEGATIVE)


def self_forward_kernel(*refs, T, S):
    q_ref, k_ref, v_ref, k_far_ref, v_far_ref, rel_ref, mark_ref, table_ref = refs[:8]
    o_ref, total_ref = refs[-2:]
    n, keys = S * T, k_far_ref.shape[1] + T
    q, rel = q_ref[...], rel_ref[...]
    k, own_k = main_and_own(k_far_ref, k_ref, T)
    v, own_v = main_and_own(v_far_ref, v_ref, T)
    biases = near_biases(rel, table_ref[...])
    k1 = jnp.concatenate([k, mark_ref[...]], 0)
    v1 = jnp.concatenate([v, jnp.ones((16, keys), low_type)], 0)
    q1 = jnp.concatenate([q, feature_rows(1.0, rel[BUCKETS - 1 :])], 0)
    scores = contract(q1, k1, 0, 0)
    weights, peaks = [], []
    for s in range(S):
        for r in range(T // TILE):
            row, first = s * T + r * TILE, keys - T + (r - 1) * TILE
            block = scores[row : row + TILE]
            left, right = near_window(block, biases[row // TILE], first, s == 0)
            parts = [left, right]
            peak = jnp.max(jnp.maximum(left, right), 1, keepdims=True)
            if first > 0:
                far = block[:, :first]
                peak = jnp.maximum(peak, jnp.max(far, 1, keepdims=True))
                parts = [far] + parts
            parts = [jnp.exp(part - peak).astype(low_type) for part in parts]
            if first + 2 * TILE < keys:
                parts.append(jnp.zeros((TILE, keys - first - 2 * TILE), low_type))
            weights.append(jnp.concatenate(parts, 1))
            peaks.append(jnp.broadcast_to(peak, (TILE, TILE)).T[0:1])
    mixed = contract(v1, jnp.concatenate(weights, 0), 1, 1)
    peak = jnp.concatenate(peaks, 1)
    total, mixed = mixed[SIZE : SIZE + 1], mixed[:SIZE]
    own_k, own_v = own_k.astype(high_type), own_v.astype(high_type)
    own = jnp.sum(q[:, T:].astype(high_type) * own_k, 0, keepdims=True) + rel[0:1, T:]
    top = jnp.maximum(peak[:, T:], own)
    main_part, own_part = jnp.exp(peak[:, T:] - top), jnp.exp(own - top)
    joined = total[:, T:] * main_part + own_part
    inverse = 1.0 / joined
    o_ref[:, :T] = (mixed[:, :T] * (1.0 / total[:, :T])).astype(low_type)
    o_ref[:, T:] = (mixed[:, T:] * (main_part * inverse) + own_v * (own_part * inverse)).astype(
        low_type
    )
    total_ref[:, :T] = peak[:, :T] + jnp.log(total[:, :T])
    total_ref[:, T:] = top + jnp.log(joined)


def self_backward_kernel(*refs, T, S):
    q_ref, k_ref, v_ref, k_far_ref, v_far_ref, rel_ref, mark_ref, table_ref = refs[:8]
    o_ref, total_ref, do_ref = refs[8:11]
    dq_ref, dkv_ref, drel_ref, far_ref = refs[-4:]
    n, keys = S * T, k_far_ref.shape[1] + T
    far = keys - T
    q, rel, do, total = q_ref[...], rel_ref[...], do_ref[...], total_ref[...]
    table = table_ref[...]
    k, own_k = main_and_own(k_far_ref, k_ref, T)
    v, own_v = main_and_own(v_far_ref, v_ref, T)
    biases = near_biases(rel, table)
    k1 = jnp.concatenate([k, mark_ref[...]], 0)
    v1 = jnp.concatenate([v, mark_ref[...]], 0)
    do_high = do.astype(high_type)
    delta = jnp.sum(do_high * o_ref[...].astype(high_type), 0, keepdims=True)
    q1 = jnp.concatenate([q, feature_rows(1.0, rel[BUCKETS - 1 :] - total)], 0)
    do1 = jnp.concatenate([do, feature_rows(0.0, -delta)], 0)
    scores = contract(q1, k1, 0, 0)
    slopes = contract(do1, v1, 0, 0)
    weights, grads, nears = [], [], []
    for s in range(S):
        for r in range(T // TILE):
            row, first = s * T + r * TILE, keys - T + (r - 1) * TILE
            block, slope = scores[row : row + TILE], slopes[row : row + TILE]
            part = jnp.exp(
                jnp.concatenate(near_window(block, biases[row // TILE], first, s == 0), 1)
            )
            grad = (part * slope[:, first : first + 2 * TILE]).astype(low_type)
            nears.append(grad)
            parts, pieces = [part.astype(low_type)], [grad]
            if first > 0:
                part = jnp.exp(block[:, :first])
                pieces = [(part * slope[:, :first]).astype(low_type)] + pieces
                parts = [part.astype(low_type)] + parts
            if first + 2 * TILE < keys:
                zero = jnp.zeros((TILE, keys - first - 2 * TILE), low_type)
                parts.append(zero)
                pieces.append(zero)
            weights.append(jnp.concatenate(parts, 1))
            grads.append(jnp.concatenate(pieces, 1))
    weights, grads = jnp.concatenate(weights, 0), jnp.concatenate(grads, 0)
    dq = contract(k1, grads, 1, 1)
    dk = contract(q, grads, 1, 0).astype(low_type)
    dv = contract(do, weights, 1, 0).astype(low_type)
    far_ref[0] = dk[:, :far]
    far_ref[1] = dv[:, :far]
    at = lax.broadcasted_iota(jnp.int32, (TILE, TILE), 0)
    to = lax.broadcasted_iota(jnp.int32, (TILE, TILE), 1)
    mirror = (at + to == TILE - 1).astype(high_type).astype(low_type)
    flipped = contract(mirror, jnp.concatenate(nears, 1), 1, 0)
    turned = [
        pltpu.roll(flipped[:, i : i + 2 * TILE], TILE + 1, 1, stride=1, stride_axis=0).astype(low_type)
        for i in range(0, 2 * n, 2 * TILE)
    ]
    top, rest = split_two(contract(table, jnp.concatenate(turned, 0), 1, 1))
    stacked = [part[:, i : i + TILE] for i in range(0, n, TILE) for part in (top, rest)]
    both = contract(jnp.concatenate(stacked, 0), mirror, 1, 0)
    rels = [
        both[i : i + BUCKETS] + both[i + BUCKETS : i + 2 * BUCKETS]
        for i in range(0, both.shape[0], 2 * BUCKETS)
    ]
    row_sums = dq[SIZE + 1 : SIZE + 2]
    own_k, own_v = own_k.astype(high_type), own_v.astype(high_type)
    own_q, own_do = q[:, T:].astype(high_type), do_high[:, T:]
    own = jnp.sum(own_q * own_k, 0, keepdims=True) + rel[0:1, T:]
    own_part = jnp.exp(own - total[:, T:])
    own_grad = own_part * (jnp.sum(own_do * own_v, 0, keepdims=True) - delta[:, T:])
    own_grad = own_grad.astype(low_type).astype(high_type)
    dq_ref[:, :T] = (dq[:SIZE, :T] * SCALE).astype(low_type)
    dq_ref[:, T:] = ((dq[:SIZE, T:] + own_grad * own_k) * SCALE).astype(low_type)
    dkv_ref[0, :, :T] = dk[:, far:]
    dkv_ref[1, :, :T] = dv[:, far:]
    dkv_ref[0, :, T:] = (own_grad * own_q).astype(low_type)
    dkv_ref[1, :, T:] = (own_part.astype(low_type).astype(high_type) * own_do).astype(low_type)
    bucket = lax.broadcasted_iota(jnp.int32, (BUCKETS, n), 0)
    drel = jnp.concatenate(rels, 1) + jnp.where(bucket == BUCKETS - 1, row_sums, 0.0)
    own_all = jnp.concatenate([jnp.zeros((1, T), high_type), own_grad], 1)
    drel_ref[...] = (drel + jnp.where(bucket == 0, own_all, 0.0)).astype(low_type)


def weight_grads_kernel(*refs, xs, terms, parts, sums):
    x_refs, rest = refs[:xs], refs[xs:]
    count = max(place for step in terms for _, place in step) + 1
    g_refs, out_ref = rest[:count], rest[count]
    e, c = pl.program_id(0), pl.program_id(1)

    for step, term in enumerate(terms):

        @pl.when(c == step)
        def _():
            x = jnp.concatenate([x_refs[x_at][...] for x_at, _ in term], 0)
            g = jnp.concatenate([g_refs[g_at][...] for _, g_at in term], 1)
            total = contract(x, g, 0, 1)
            if sums[step]:
                line = jnp.sum(g.astype(high_type), 1, keepdims=True)
                rest[count + 1][step] = jnp.broadcast_to(line, (line.shape[0], TILE))
            total = total.astype(low_type)
            for at, row, rows, halves in parts[step]:
                if halves:
                    kept = jnp.where(e < halves, total[row : row + rows], total[row + rows : row + 2 * rows])
                else:
                    kept = total[row : row + rows]
                out_ref[at[0], at[1] : at[1] + rows, :] = kept


def back_rows_kernel(*refs, pairs, base, joined):
    gs, ws, rest, out_ref = refs[:pairs], refs[pairs : 2 * pairs], refs[2 * pairs : -1], refs[-1]
    total = rest[0][...] if base else None
    for g_ref, w_ref in zip(gs, ws, strict=True):
        piece = contract(g_ref[...], w_ref[...], 0, 1)
        total = piece if total is None else total + piece
    if joined:
        add = rest[1][...]
        out_ref[: add.shape[0]] = (total[: add.shape[0]] + add).astype(low_type)
        out_ref[add.shape[0] :] = total[add.shape[0] :].astype(low_type)
    else:
        out_ref[...] = total.astype(low_type)


def by_head(body, group, split, **static):
    def kernel(*refs):
        for head in range(group):
            views = []
            for ref, how in zip(refs, split, strict=True):
                if how is None:
                    views.append(ref)
                elif how == 0:
                    views.append(ref.at[head])
                elif isinstance(how, tuple):
                    views.append(ref.at[:, pl.ds(head * how[1], how[1]), :])
                else:
                    views.append(ref.at[pl.ds(head * how, how), :])
            body(*views, **static)

    return kernel


def per_head(rows, count):
    return pl.BlockSpec((rows, count), lambda b, h: (h, b))


def per_sequence(keys):
    return pl.BlockSpec((None, 16, keys), lambda b, h: (b, 0, 0))


def per_total(group, count):
    return pl.BlockSpec((None, group, 1, count), lambda b, h: (b, h, 0, 0))


def like(array):
    return jax.ShapeDtypeStruct(array.shape, low_type)


def cost(B, rows, keys, products):
    return pl.CostEstimate(
        flops=2 * B * HEADS * rows * keys * 256 * products,
        bytes_accessed=B * HEADS * SIZE * (rows + keys) * 4 * products,
        transcendentals=B * HEADS * rows * keys,
    )


def cross_forward(q, k, v, mark):
    B, _, keys = mark.shape
    count, group = q.shape[1] // B, GROUPS["cross_forward"]
    size = group * SIZE
    return pl.pallas_call(
        by_head(cross_forward_kernel, group, [SIZE, SIZE, SIZE, None, SIZE, 0]),
        grid=(B, HEADS // group),
        in_specs=[per_head(size, count), per_head(size, keys), per_head(size, keys), per_sequence(keys)],
        out_specs=[per_head(size, count), per_total(group, count)],
        out_shape=[like(q), jax.ShapeDtypeStruct((B, HEADS, 1, count), high_type)],
        cost_estimate=cost(B, count, keys, 2),
        compiler_params=pltpu.CompilerParams(vmem_limit_bytes=VMEM_LIMIT),
        name="cross_forward",
    )(q, k, v, mark)


def cross_backward(q, k, v, mark, o, total, do):
    B, _, keys = mark.shape
    count, group = q.shape[1] // B, GROUPS["cross_backward"]
    size = group * SIZE
    row, key = per_head(size, count), per_head(size, keys)
    return pl.pallas_call(
        by_head(
            cross_backward_kernel,
            group,
            [SIZE, SIZE, SIZE, None, SIZE, 0, SIZE, SIZE, SIZE, SIZE, None, None],
            step=count // 2,
        ),
        grid=(B, HEADS // group),
        in_specs=[row, key, key, per_sequence(keys), row, per_total(group, count), row],
        out_specs=[row, key, key],
        out_shape=[like(q), like(k), like(v)],
        scratch_shapes=[pltpu.VMEM((SIZE, keys), high_type)] * 2,
        cost_estimate=cost(B, count, keys, 5),
        compiler_params=pltpu.CompilerParams(vmem_limit_bytes=VMEM_LIMIT),
        name="cross_backward",
    )(q, k, v, mark, o, total, do)


def self_call(body, b, inputs, more, earlier, T, S, outs, out_specs, out_split, products, name):
    q, far, mark, table = inputs[0], inputs[3].shape[1], inputs[6], inputs[7]
    count, group = S * T, GROUPS[name]
    row = pl.BlockSpec((group * SIZE, count), lambda h: (h, b))
    far_row = pl.BlockSpec((group * SIZE, far), lambda h: (h, 0))
    total = pl.BlockSpec((None, group, 1, count), lambda h: (b, h, 0, 0))
    specs = [row, row, row, far_row, far_row, pl.BlockSpec((group * BUCKETS, count), lambda h: (h, b))]
    specs.append(pl.BlockSpec((None, 16, far + T), lambda h: (b, 0, 0)))
    specs.append(pl.BlockSpec(table.shape, lambda h: (0, 0)))
    specs += [row, total, row][: len(more)]
    held = len(specs)
    return pl.pallas_call(
        by_head(
            body,
            group,
            [SIZE] * 5
            + [BUCKETS, None, None]
            + [SIZE, 0, SIZE][: len(more)]
            + [None] * len(earlier)
            + out_split,
            T=T,
            S=S,
        ),
        grid=(HEADS // group,),
        in_specs=specs + [pl.BlockSpec(memory_space=pl.ANY)] * len(earlier),
        out_specs=out_specs,
        out_shape=outs,
        input_output_aliases={held + i: i for i in range(len(earlier))},
        cost_estimate=cost(1, count, far + T, products),
        compiler_params=pltpu.CompilerParams(vmem_limit_bytes=VMEM_LIMIT),
        name=name,
    )(*inputs, *more, *earlier)


def self_forward(b, inputs, earlier, T, S):
    q, mark, count, group = inputs[0], inputs[6], S * T, GROUPS["self_forward"]
    return self_call(
        self_forward_kernel,
        b,
        inputs,
        (),
        earlier,
        T,
        S,
        [like(q), jax.ShapeDtypeStruct((mark.shape[0], HEADS, 1, count), high_type)],
        [
            pl.BlockSpec((group * SIZE, count), lambda h: (h, b)),
            pl.BlockSpec((None, group, 1, count), lambda h: (b, h, 0, 0)),
        ],
        [SIZE, 0],
        2,
        "self_forward",
    )


def self_backward(b, inputs, more, earlier, T, S):
    q, rel, count, far = inputs[0], inputs[5], S * T, inputs[3].shape[1]
    group = GROUPS["self_backward"]

    def pair(columns):
        return jax.ShapeDtypeStruct((2, q.shape[0], columns), low_type)

    return self_call(
        self_backward_kernel,
        b,
        inputs,
        more,
        earlier,
        T,
        S,
        [like(q), pair(q.shape[1]), like(rel), pair(far)],
        [
            pl.BlockSpec((group * SIZE, count), lambda h: (h, b)),
            pl.BlockSpec((2, group * SIZE, count), lambda h: (0, h, b)),
            pl.BlockSpec((group * BUCKETS, count), lambda h: (h, b)),
            pl.BlockSpec((2, group * SIZE, far), lambda h: (0, h, 0)),
        ],
        [SIZE, (2, SIZE), BUCKETS, (2, SIZE)],
        5,
        "self_backward",
    )


def weight_grads(xs, gs, specs, terms, parts, sums, out, name):
    width = xs[0].shape[1]
    columns = out[2] // SPLIT
    flops = sum(2 * width * out[2] * xs[x_at].shape[0] for term in terms for x_at, _ in term)
    return pl.pallas_call(
        functools.partial(weight_grads_kernel, xs=len(xs), terms=terms, parts=parts, sums=sums),
        grid=(SPLIT, len(terms)),
        in_specs=[pl.BlockSpec(x.shape, lambda e, c: (0, 0)) for x in xs] + specs,
        out_specs=[
            pl.BlockSpec((out[0], out[1], columns), lambda e, c: (0, 0, e)),
            pl.BlockSpec((len(terms), columns, TILE), lambda e, c: (0, e, 0)),
        ],
        out_shape=[
            jax.ShapeDtypeStruct(out, low_type),
            jax.ShapeDtypeStruct((len(terms), out[2], TILE), high_type),
        ],
        cost_estimate=pl.CostEstimate(
            flops=flops, bytes_accessed=flops // 256, transcendentals=0
        ),
        compiler_params=pltpu.CompilerParams(vmem_limit_bytes=VMEM_LIMIT),
        name=name,
    )(*xs, *gs)


def back_rows(gs, ws, base, joined, tile, name):
    width, columns = 1024, BACK_COLUMNS

    def spec(entry, shape, index):
        if isinstance(entry, tuple):
            return pl.BlockSpec((None,) + shape, lambda r, d, w=entry[1]: (w,) + index(r, d))
        return pl.BlockSpec(shape, index)

    arrays = [e[0] if isinstance(e, tuple) else e for e in gs]
    weights = [e[0] if isinstance(e, tuple) else e for e in ws]
    rows = arrays[0].shape[-1]
    sizes = [a.shape[-2] for a in arrays]
    specs = [spec(e, (f, tile), lambda r, d: (0, r)) for e, f in zip(gs, sizes, strict=True)]
    specs += [spec(e, (columns, f), lambda r, d: (d, 0)) for e, f in zip(ws, sizes, strict=True)]
    extra = []
    if base is not None:
        specs.append(pl.BlockSpec((tile, columns), lambda r, d: (r, d)))
        extra.append(base)
    if joined is not None:
        specs.append(pl.BlockSpec((joined.shape[0] * tile // rows, columns), lambda r, d: (r, d)))
        extra.append(joined)
    return pl.pallas_call(
        functools.partial(
            back_rows_kernel, pairs=len(gs), base=base is not None, joined=joined is not None
        ),
        grid=(rows // tile, width // columns),
        in_specs=specs,
        out_specs=pl.BlockSpec((tile, columns), lambda r, d: (r, d)),
        out_shape=jax.ShapeDtypeStruct((rows, width), low_type),
        cost_estimate=pl.CostEstimate(
            flops=2 * rows * width * sum(sizes),
            bytes_accessed=2 * (rows + width) * sum(sizes) + 6 * rows * width,
            transcendentals=0,
        ),
        compiler_params=pltpu.CompilerParams(vmem_limit_bytes=VMEM_LIMIT),
        name=name,
    )(*arrays, *weights, *extra)


def keys_and_values_kernel(x_ref, wk_ref, wv_ref, b_ref, k_ref, v_ref):
    x = x_ref[...]
    k_ref[...] = contract(wk_ref[...], x, 0, 1).astype(low_type)
    v_ref[...] = (contract(wv_ref[...], x, 0, 1) + b_ref[...]).astype(low_type)


def keys_and_values(x, weights, bias):
    rows, width = x.shape
    columns = width // SPLIT
    out = jax.ShapeDtypeStruct((width, rows), low_type)
    return pl.pallas_call(
        keys_and_values_kernel,
        grid=(SPLIT,),
        in_specs=[
            pl.BlockSpec((rows, width), lambda e: (0, 0)),
            pl.BlockSpec((None, width, columns), lambda e: (1, 0, e)),
            pl.BlockSpec((None, width, columns), lambda e: (2, 0, e)),
            pl.BlockSpec((columns, 1), lambda e: (e, 0)),
        ],
        out_specs=[pl.BlockSpec((columns, rows), lambda e: (e, 0))] * 2,
        out_shape=[out, out],
        cost_estimate=pl.CostEstimate(
            flops=4 * rows * width * width,
            bytes_accessed=2 * (3 * rows * width + 2 * width * width),
            transcendentals=0,
        ),
        compiler_params=pltpu.CompilerParams(vmem_limit_bytes=VMEM_LIMIT),
        name="keys_and_values",
    )(x, weights, weights, bias[:, None])


def ffn_kernel(x_ref, w_ref, b_ref, g_ref, slope_ref, *, step):
    x = x_ref[...]
    for at in range(0, w_ref.shape[1], step):
        u = contract(x, w_ref[:, at : at + step], 1, 0) + b_ref[:, at : at + step]
        t = 1.0 / (1.0 + (0.3275911 * 0.5**0.5) * jnp.abs(u))
        bell = jnp.exp2(u * u * (-0.5 / math.log(2.0)))
        poly = 0.7107068705 + t * (-0.7265760135 + t * 0.5307027145)
        tail = bell * (t * (0.127414796 + t * (-0.142248368 + t * poly)))
        phi = jnp.where(u < 0.0, tail, 1.0 - tail)
        g_ref[:, at : at + step] = (u * phi).astype(low_type)
        slope_ref[:, at : at + step] = (phi + u * (bell * (2.0 * math.pi) ** -0.5)).astype(low_type)


def ffn_first(x, w, b):
    rows, width = x.shape
    hidden = w.shape[1]
    tm, tn = math.gcd(rows, FFN_ROWS), math.gcd(hidden, FFN_COLS)
    block = pl.BlockSpec((tm, tn), lambda j, i: (i, j))
    out = jax.ShapeDtypeStruct((rows, hidden), low_type)
    return pl.pallas_call(
        functools.partial(ffn_kernel, step=FFN_STEP),
        grid=(hidden // tn, rows // tm),
        in_specs=[
            pl.BlockSpec((tm, width), lambda j, i: (i, 0)),
            pl.BlockSpec((width, tn), lambda j, i: (0, j)),
            pl.BlockSpec((1, tn), lambda j, i: (0, j)),
        ],
        out_specs=[block, block],
        out_shape=[out, out],
        cost_estimate=pl.CostEstimate(
            flops=2 * rows * width * hidden, bytes_accessed=4 * rows * hidden, transcendentals=rows * hidden
        ),
        compiler_params=pltpu.CompilerParams(vmem_limit_bytes=VMEM_LIMIT),
        name="ffn_first",
    )(x, w, b)


def column_sum(value):
    return jnp.sum(value.astype(high_type), 0)


def row_sum(value):
    return jnp.sum(value.astype(high_type), 1)


def dot(spec, left, right):
    return jnp.einsum(spec, left, right, preferred_element_type=high_type)


def norm_parts(value):
    center = value - jnp.mean(value, -1, keepdims=True)
    inverse = lax.rsqrt(jnp.mean(center * center, -1, keepdims=True) + EPSILON)
    return center * inverse, inverse


def norm_back(value, grad, gain):
    unit, inverse = norm_parts(value)
    scaled = grad * gain
    back = inverse * (
        scaled
        - jnp.mean(scaled, -1, keepdims=True)
        - unit * jnp.mean(scaled * unit, -1, keepdims=True)
    )
    return back, jnp.sum(grad * unit, 0), jnp.sum(grad, 0)


def rounded(value):
    return lax.optimization_barrier(value.astype(jnp.bfloat16)).astype(jnp.float32)


def layer_norm(value, gain, shift):
    center = value - jnp.mean(value, -1, keepdims=True)
    spread = jnp.mean(center * center, -1, keepdims=True)
    return center * lax.rsqrt(spread + EPSILON) * gain + shift


def gelu_exact(value):
    return jax.nn.gelu(value, approximate=False)


def bucket_of(distance):
    half = BUCKETS // 2
    counted = jnp.zeros_like(distance)
    for level in range(1, half):
        bound = math.ceil(half * (MAX_DIST / half) ** (level / half))
        counted = counted + (distance >= bound).astype(jnp.int32)
    return jnp.where(distance < half, distance, half + counted)


def self_logits(query_s, key_s, rel_s, keys_s, dec_len, offset_pos):
    streams, local_len, heads, size = query_s.shape
    full_len = keys_s.shape[0]
    scale = size ** (-0.5)
    positions = offset_pos + jnp.arange(local_len, dtype=jnp.int32)
    key_positions = jnp.arange(full_len, dtype=jnp.int32)
    distance = positions[:, None] - key_positions[None, :]
    one_hot = (
        bucket_of(jnp.maximum(distance, 0))[:, :, None] == jnp.arange(BUCKETS, dtype=jnp.int32)
    ).astype(jnp.float32)
    scores = scale * jnp.einsum(
        "sqhd,khd->shqk", query_s, keys_s, preferred_element_type=jnp.float32
    )
    scores = scores + jnp.einsum("sqhb,qkb->shqk", rel_s, one_hot, precision=lax.Precision.HIGHEST)
    stream_ids = jnp.arange(streams, dtype=jnp.int32)
    allowed = (distance[None] >= jnp.minimum(stream_ids, 1)[:, None, None]) & (
        key_positions < dec_len
    )[None, None, :]
    scores = jnp.where(allowed[:, None], scores, NEGATIVE)
    own_score = (
        scale * jnp.sum(query_s.astype(jnp.float32) * key_s.astype(jnp.float32), -1) + rel_s[..., 0]
    )
    own_score = jnp.where(
        (stream_ids > 0)[:, None, None], jnp.transpose(own_score, (0, 2, 1)), NEGATIVE
    )
    return (scores, own_score, one_hot)


def plain_self_forward(items, offset_pos):
    query_s, key_s, value_s, rel_s, keys_s, values_s, dec_len = items
    scores, own_score, one_hot = self_logits(query_s, key_s, rel_s, keys_s, dec_len, offset_pos)
    peak = jnp.maximum(jnp.max(scores, -1), own_score)
    log_total = peak + jnp.log(
        jnp.sum(jnp.exp(scores - peak[..., None]), -1) + jnp.exp(own_score - peak)
    )
    weights = jnp.exp(scores - log_total[..., None]).astype(jnp.bfloat16)
    own_weight = rounded(jnp.exp(own_score - log_total))
    mixed = jnp.einsum("shqk,khd->sqhd", weights, values_s, preferred_element_type=jnp.float32)
    mixed = mixed + jnp.transpose(own_weight, (0, 2, 1))[..., None] * value_s.astype(jnp.float32)
    return (mixed.astype(jnp.bfloat16), log_total)


def plain_self_backward(items, offset_pos):
    query_s, key_s, value_s, rel_s, keys_s, values_s, dec_len, log_total, grad_s = items
    scores, own_score, one_hot = self_logits(query_s, key_s, rel_s, keys_s, dec_len, offset_pos)
    scale = query_s.shape[3] ** (-0.5)
    weights = jnp.exp(scores - log_total[..., None])
    own_weight = jnp.exp(own_score - log_total)
    grad_float = grad_s.astype(jnp.float32)
    grad_weights = jnp.einsum(
        "sqhd,khd->shqk", grad_s, values_s, preferred_element_type=jnp.float32
    )
    grad_own = jnp.transpose(jnp.sum(grad_float * value_s.astype(jnp.float32), -1), (0, 2, 1))
    delta = jnp.sum(grad_weights * weights, -1) + grad_own * own_weight
    grad_scores = (weights * (grad_weights - delta[..., None])).astype(jnp.bfloat16)
    grad_own_score = rounded(own_weight * (grad_own - delta))
    own_term = jnp.transpose(grad_own_score, (0, 2, 1))[..., None]
    grad_query = scale * (
        jnp.einsum("shqk,khd->sqhd", grad_scores, keys_s, preferred_element_type=jnp.float32)
        + own_term * key_s.astype(jnp.float32)
    )
    grad_keys = scale * jnp.einsum(
        "shqk,sqhd->khd", grad_scores, query_s, preferred_element_type=jnp.float32
    )
    grad_key_own = scale * own_term * query_s.astype(jnp.float32)
    grad_values = jnp.einsum(
        "shqk,sqhd->khd", weights.astype(jnp.bfloat16), grad_s, preferred_element_type=jnp.float32
    )
    grad_value_own = jnp.transpose(rounded(own_weight), (0, 2, 1))[..., None] * grad_float
    grad_rel = jnp.einsum(
        "shqk,qkb->sqhb", grad_scores.astype(jnp.float32), one_hot, precision=lax.Precision.HIGHEST
    )
    grad_rel = grad_rel.at[..., 0].add(jnp.transpose(grad_own_score, (0, 2, 1)))
    return (grad_query, grad_key_own, grad_value_own, grad_keys, grad_values, grad_rel)


def cross_logits(query_s, keys_s, enc_len):
    scale = query_s.shape[3] ** (-0.5)
    scores = scale * jnp.einsum(
        "sqhd,khd->shqk", query_s, keys_s, preferred_element_type=jnp.float32
    )
    key_positions = jnp.arange(keys_s.shape[0], dtype=jnp.int32)
    return jnp.where(key_positions < enc_len, scores, NEGATIVE)


def plain_cross_forward(items):
    query_s, keys_s, values_s, enc_len = items
    scores = cross_logits(query_s, keys_s, enc_len)
    peak = jnp.max(scores, -1)
    log_total = peak + jnp.log(jnp.sum(jnp.exp(scores - peak[..., None]), -1))
    weights = jnp.exp(scores - log_total[..., None]).astype(jnp.bfloat16)
    mixed = jnp.einsum("shqk,khd->sqhd", weights, values_s, preferred_element_type=jnp.float32)
    return (mixed.astype(jnp.bfloat16), log_total)


def plain_cross_backward(items):
    query_s, keys_s, values_s, enc_len, log_total, grad_s = items
    scale = query_s.shape[3] ** (-0.5)
    scores = cross_logits(query_s, keys_s, enc_len)
    weights = jnp.exp(scores - log_total[..., None])
    grad_weights = jnp.einsum(
        "sqhd,khd->shqk", grad_s, values_s, preferred_element_type=jnp.float32
    )
    delta = jnp.sum(grad_weights * weights, -1)
    grad_scores = (weights * (grad_weights - delta[..., None])).astype(jnp.bfloat16)
    grad_query = scale * jnp.einsum(
        "shqk,khd->sqhd", grad_scores, keys_s, preferred_element_type=jnp.float32
    )
    grad_keys = scale * jnp.einsum(
        "shqk,sqhd->khd", grad_scores, query_s, preferred_element_type=jnp.float32
    )
    grad_values = jnp.einsum(
        "shqk,sqhd->khd", weights.astype(jnp.bfloat16), grad_s, preferred_element_type=jnp.float32
    )
    return (grad_query, grad_keys, grad_values)


def plain_on_device(
    hidden,
    encoder_out,
    cotangent,
    dec_lengths,
    enc_lengths,
    self_qkv,
    self_qv_bias,
    self_out,
    self_out_bias,
    rel_weight,
    rel_bias,
    cross_qkv,
    cross_qv_bias,
    cross_out,
    cross_out_bias,
    ffn_in,
    ffn_in_bias,
    ffn_out,
    ffn_out_bias,
    norm_gain,
    norm_bias,
):
    seq_count, streams, local_len, width = hidden.shape
    seq_parts = lax.axis_size("seq")
    dp_parts = lax.axis_size("dp")
    full_len = local_len * seq_parts
    offset_pos = lax.axis_index("seq") * local_len
    heads = HEADS
    size = width // heads
    head_shape = (seq_count, streams, local_len, heads, size)
    all_shape = (seq_count, full_len, heads, size)
    kv_shape = (seq_count, full_len, width)
    rows = hidden.reshape(-1, width)
    row_count = rows.shape[0]
    gains = norm_gain.astype(high_type)
    shifts = norm_bias.astype(high_type)
    self_bias = self_qv_bias.astype(high_type)
    cross_bias = cross_qv_bias.astype(high_type)
    projected = jnp.einsum("rd,cde->cre", rows, self_qkv, preferred_element_type=high_type)
    query = (projected[0] + self_bias[0]).astype(low_type)
    key = projected[1].astype(low_type)
    value = (projected[2] + self_bias[1]).astype(low_type)
    rel_logits = jnp.dot(rows, rel_weight, preferred_element_type=high_type) + rel_bias.astype(
        high_type
    )
    rel_heads = rel_logits.reshape(seq_count, streams, local_len, heads, BUCKETS)
    key_main = key.reshape(seq_count, streams, local_len, width)[:, 0]
    value_main = value.reshape(seq_count, streams, local_len, width)[:, 0]
    keys_all, values_all = (
        lax.all_gather(key_main, "seq", axis=1, tiled=True),
        lax.all_gather(value_main, "seq", axis=1, tiled=True),
    )
    self_items = (
        query.reshape(head_shape),
        key.reshape(head_shape),
        value.reshape(head_shape),
        rel_heads,
        keys_all.reshape(all_shape),
        values_all.reshape(all_shape),
        dec_lengths,
    )
    attended, self_total = lax.map(lambda items: plain_self_forward(items, offset_pos), self_items)
    attended = attended.reshape(row_count, width)
    self_branch = jnp.dot(
        attended, self_out, preferred_element_type=high_type
    ) + self_out_bias.astype(high_type)
    first_sum = rows.astype(high_type) + self_branch
    first_norm = layer_norm(first_sum, gains[0], shifts[0])
    first_low = first_norm.astype(low_type)
    cross_query = (
        jnp.dot(first_low, cross_qkv[0], preferred_element_type=high_type) + cross_bias[0]
    ).astype(low_type)
    encoder_rows = encoder_out.reshape(-1, width)
    encoder_proj = jnp.einsum(
        "rd,cde->cre", encoder_rows, cross_qkv[1:], preferred_element_type=high_type
    )
    cross_key = encoder_proj[0].astype(low_type).reshape(seq_count, local_len, width)
    cross_value = (
        (encoder_proj[1] + cross_bias[1]).astype(low_type).reshape(seq_count, local_len, width)
    )
    cross_keys, cross_values = (
        lax.all_gather(cross_key, "seq", axis=1, tiled=True),
        lax.all_gather(cross_value, "seq", axis=1, tiled=True),
    )
    cross_items = (
        cross_query.reshape(head_shape),
        cross_keys.reshape(all_shape),
        cross_values.reshape(all_shape),
        enc_lengths,
    )
    cross_mixed, cross_total = lax.map(plain_cross_forward, cross_items)
    cross_mixed = cross_mixed.reshape(row_count, width)
    cross_branch = jnp.dot(
        cross_mixed, cross_out, preferred_element_type=high_type
    ) + cross_out_bias.astype(high_type)
    second_sum = first_norm + cross_branch
    second_norm = layer_norm(second_sum, gains[1], shifts[1])
    second_low = second_norm.astype(low_type)
    hidden_pre = jnp.dot(second_low, ffn_in, preferred_element_type=high_type) + ffn_in_bias.astype(
        high_type
    )
    activated = gelu_exact(hidden_pre).astype(low_type)
    ffn_branch = jnp.dot(
        activated, ffn_out, preferred_element_type=high_type
    ) + ffn_out_bias.astype(high_type)
    third_sum = second_norm + ffn_branch
    output = layer_norm(third_sum, gains[2], shifts[2]).astype(low_type).reshape(hidden.shape)
    third_value, norm_pull = jax.vjp(layer_norm, third_sum, gains[2], shifts[2])
    grad_third, grad_gain_ffn, grad_shift_ffn = norm_pull(
        cotangent.reshape(-1, width).astype(high_type)
    )
    grad_ffn = grad_third.astype(low_type)
    grad_ffn_out = jnp.einsum("rf,rd->fd", activated, grad_ffn, preferred_element_type=high_type)
    grad_ffn_out_bias = column_sum(grad_ffn)
    grad_activated = jnp.einsum("rd,fd->rf", grad_ffn, ffn_out, preferred_element_type=high_type)
    gelu_value, gelu_pull = jax.vjp(gelu_exact, hidden_pre)
    grad_pre = gelu_pull(grad_activated)[0].astype(low_type)
    grad_ffn_in = jnp.einsum("rd,rf->df", second_low, grad_pre, preferred_element_type=high_type)
    grad_ffn_in_bias = column_sum(grad_pre)
    grad_second = grad_third + jnp.einsum(
        "rf,df->rd", grad_pre, ffn_in, preferred_element_type=high_type
    )
    second_value, norm_pull = jax.vjp(layer_norm, second_sum, gains[1], shifts[1])
    grad_second_sum, grad_gain_cross, grad_shift_cross = norm_pull(grad_second)
    grad_cross = grad_second_sum.astype(low_type)
    grad_cross_out = jnp.einsum(
        "rd,re->de", cross_mixed, grad_cross, preferred_element_type=high_type
    )
    grad_cross_out_bias = column_sum(grad_cross)
    grad_cross_mixed = jnp.einsum(
        "re,de->rd", grad_cross, cross_out, preferred_element_type=high_type
    ).astype(low_type)
    cross_back_items = (
        cross_query.reshape(head_shape),
        cross_keys.reshape(all_shape),
        cross_values.reshape(all_shape),
        enc_lengths,
        cross_total,
        grad_cross_mixed.reshape(head_shape),
    )
    grad_cross_query, grad_cross_keys, grad_cross_values = lax.map(plain_cross_backward, cross_back_items)
    cross_key_sum, cross_value_sum = (
        lax.psum_scatter(
            grad_cross_keys.reshape(kv_shape).astype(jnp.bfloat16),
            "seq",
            scatter_dimension=1,
            tiled=True,
        ).astype(jnp.float32),
        lax.psum_scatter(
            grad_cross_values.reshape(kv_shape).astype(jnp.bfloat16),
            "seq",
            scatter_dimension=1,
            tiled=True,
        ).astype(jnp.float32),
    )
    query_low = grad_cross_query.reshape(row_count, width).astype(low_type)
    encoder_grads = jnp.stack(
        [cross_key_sum.reshape(-1, width), cross_value_sum.reshape(-1, width)]
    ).astype(low_type)
    grad_cross_query_weight = jnp.einsum(
        "rd,re->de", first_low, query_low, preferred_element_type=high_type
    )
    grad_cross_kv_weight = jnp.einsum(
        "rd,cre->cde", encoder_rows, encoder_grads, preferred_element_type=high_type
    )
    grad_cross_qkv = jnp.concatenate([grad_cross_query_weight[None], grad_cross_kv_weight], 0)
    grad_cross_bias = jnp.stack([column_sum(query_low), column_sum(encoder_grads[1])])
    grad_encoder = jnp.einsum(
        "cre,cde->rd", encoder_grads, cross_qkv[1:], preferred_element_type=high_type
    )
    grad_encoder = grad_encoder.astype(low_type).reshape(encoder_out.shape)
    grad_first = grad_second_sum + jnp.einsum(
        "re,de->rd", query_low, cross_qkv[0], preferred_element_type=high_type
    )
    first_value, norm_pull = jax.vjp(layer_norm, first_sum, gains[0], shifts[0])
    grad_first_sum, grad_gain_self, grad_shift_self = norm_pull(grad_first)
    grad_self = grad_first_sum.astype(low_type)
    grad_self_out = jnp.einsum("rd,re->de", attended, grad_self, preferred_element_type=high_type)
    grad_self_out_bias = column_sum(grad_self)
    grad_attended = jnp.einsum(
        "re,de->rd", grad_self, self_out, preferred_element_type=high_type
    ).astype(low_type)
    self_back_items = (
        query.reshape(head_shape),
        key.reshape(head_shape),
        value.reshape(head_shape),
        rel_heads,
        keys_all.reshape(all_shape),
        values_all.reshape(all_shape),
        dec_lengths,
        self_total,
        grad_attended.reshape(head_shape),
    )
    grad_query, grad_key_own, grad_value_own, grad_keys, grad_values, grad_rel = lax.map(
        lambda items: plain_self_backward(items, offset_pos), self_back_items
    )
    key_sum, value_sum = (
        lax.psum_scatter(
            grad_keys.reshape(kv_shape).astype(jnp.bfloat16), "seq", scatter_dimension=1, tiled=True
        ).astype(jnp.float32),
        lax.psum_scatter(
            grad_values.reshape(kv_shape).astype(jnp.bfloat16),
            "seq",
            scatter_dimension=1,
            tiled=True,
        ).astype(jnp.float32),
    )
    own_shape = (seq_count, streams, local_len, width)
    key_total = jnp.concatenate([key_sum[:, None], grad_key_own.reshape(own_shape)[:, 1:]], 1)
    value_total = jnp.concatenate([value_sum[:, None], grad_value_own.reshape(own_shape)[:, 1:]], 1)
    stacked_grad = jnp.stack(
        [
            grad_query.reshape(row_count, width),
            key_total.reshape(row_count, width),
            value_total.reshape(row_count, width),
        ]
    ).astype(low_type)
    rel_low = grad_rel.reshape(row_count, heads * BUCKETS).astype(low_type)
    grad_self_qkv = jnp.einsum("rd,cre->cde", rows, stacked_grad, preferred_element_type=high_type)
    grad_self_bias = jnp.stack([column_sum(stacked_grad[0]), column_sum(stacked_grad[2])])
    grad_rel_weight = jnp.einsum("rd,rb->db", rows, rel_low, preferred_element_type=high_type)
    grad_rel_bias = column_sum(rel_low)
    grad_rows = grad_first_sum + jnp.einsum(
        "cre,cde->rd", stacked_grad, self_qkv, preferred_element_type=high_type
    )
    grad_rows = grad_rows + jnp.einsum(
        "rb,db->rd", rel_low, rel_weight, preferred_element_type=high_type
    )
    grad_hidden = grad_rows.astype(low_type).reshape(hidden.shape)
    matrices = [
        grad_self_qkv,
        grad_self_out,
        grad_rel_weight,
        grad_cross_qkv,
        grad_cross_out,
        grad_ffn_in,
        grad_ffn_out,
    ]
    vectors = [
        grad_self_bias.reshape(-1),
        grad_self_out_bias,
        grad_rel_bias,
        grad_cross_bias.reshape(-1),
        grad_cross_out_bias,
        grad_ffn_in_bias,
        grad_ffn_out_bias,
        jnp.stack([grad_gain_self, grad_gain_cross, grad_gain_ffn]).reshape(-1),
        jnp.stack([grad_shift_self, grad_shift_cross, grad_shift_ffn]).reshape(-1),
    ]
    vec_blocks = [piece.reshape(seq_parts, -1) for piece in vectors]
    mat_blocks = [piece.reshape(dp_parts, seq_parts, -1) for piece in matrices]
    reduced = (
        lax.psum_scatter(
            mat_blocks[0].astype(jnp.bfloat16), "seq", scatter_dimension=1, tiled=True
        ).astype(jnp.float32),
        lax.psum_scatter(
            mat_blocks[1].astype(jnp.bfloat16), "seq", scatter_dimension=1, tiled=True
        ).astype(jnp.float32),
        lax.psum_scatter(
            mat_blocks[2].astype(jnp.bfloat16), "seq", scatter_dimension=1, tiled=True
        ).astype(jnp.float32),
        lax.psum_scatter(
            mat_blocks[3].astype(jnp.bfloat16), "seq", scatter_dimension=1, tiled=True
        ).astype(jnp.float32),
        lax.psum_scatter(
            mat_blocks[4].astype(jnp.bfloat16), "seq", scatter_dimension=1, tiled=True
        ).astype(jnp.float32),
        lax.psum_scatter(
            mat_blocks[5].astype(jnp.bfloat16), "seq", scatter_dimension=1, tiled=True
        ).astype(jnp.float32),
        lax.psum_scatter(
            mat_blocks[6].astype(jnp.bfloat16), "seq", scatter_dimension=1, tiled=True
        ).astype(jnp.float32),
        lax.psum_scatter(
            vec_blocks[0].astype(jnp.bfloat16), "seq", scatter_dimension=0, tiled=True
        ).astype(jnp.float32),
        lax.psum_scatter(
            vec_blocks[1].astype(jnp.bfloat16), "seq", scatter_dimension=0, tiled=True
        ).astype(jnp.float32),
        lax.psum_scatter(
            vec_blocks[2].astype(jnp.bfloat16), "seq", scatter_dimension=0, tiled=True
        ).astype(jnp.float32),
        lax.psum_scatter(
            vec_blocks[3].astype(jnp.bfloat16), "seq", scatter_dimension=0, tiled=True
        ).astype(jnp.float32),
        lax.psum_scatter(
            vec_blocks[4].astype(jnp.bfloat16), "seq", scatter_dimension=0, tiled=True
        ).astype(jnp.float32),
        lax.psum_scatter(
            vec_blocks[5].astype(jnp.bfloat16), "seq", scatter_dimension=0, tiled=True
        ).astype(jnp.float32),
        lax.psum_scatter(
            vec_blocks[6].astype(jnp.bfloat16), "seq", scatter_dimension=0, tiled=True
        ).astype(jnp.float32),
        lax.psum_scatter(
            vec_blocks[7].astype(jnp.bfloat16), "seq", scatter_dimension=0, tiled=True
        ).astype(jnp.float32),
        lax.psum_scatter(
            vec_blocks[8].astype(jnp.bfloat16), "seq", scatter_dimension=0, tiled=True
        ).astype(jnp.float32),
    )
    mat_done = (
        lax.psum_scatter(
            reduced[0].astype(jnp.bfloat16), "dp", scatter_dimension=0, tiled=True
        ).astype(jnp.float32),
        lax.psum_scatter(
            reduced[1].astype(jnp.bfloat16), "dp", scatter_dimension=0, tiled=True
        ).astype(jnp.float32),
        lax.psum_scatter(
            reduced[2].astype(jnp.bfloat16), "dp", scatter_dimension=0, tiled=True
        ).astype(jnp.float32),
        lax.psum_scatter(
            reduced[3].astype(jnp.bfloat16), "dp", scatter_dimension=0, tiled=True
        ).astype(jnp.float32),
        lax.psum_scatter(
            reduced[4].astype(jnp.bfloat16), "dp", scatter_dimension=0, tiled=True
        ).astype(jnp.float32),
        lax.psum_scatter(
            reduced[5].astype(jnp.bfloat16), "dp", scatter_dimension=0, tiled=True
        ).astype(jnp.float32),
        lax.psum_scatter(
            reduced[6].astype(jnp.bfloat16), "dp", scatter_dimension=0, tiled=True
        ).astype(jnp.float32),
    )
    vec_part = [reduced[7 + index] for index in range(9)]
    vec_done = lax.psum(
        (
            vec_part[0],
            vec_part[1],
            vec_part[2],
            vec_part[3],
            vec_part[4],
            vec_part[5],
            vec_part[6],
            vec_part[7],
            vec_part[8],
        ),
        "dp",
    )
    mats = [piece.reshape(-1) for piece in mat_done]
    vecs = [piece.reshape(-1) for piece in vec_done]
    return (
        output,
        grad_hidden,
        grad_encoder,
        mats[0],
        vecs[0],
        mats[1],
        vecs[1],
        mats[2],
        vecs[2],
        mats[3],
        vecs[3],
        mats[4],
        vecs[4],
        mats[5],
        vecs[5],
        mats[6],
        vecs[6],
        vecs[7],
        vecs[8],
    )


def on_device(
    hidden,
    encoder_out,
    cotangent,
    dec_lengths,
    enc_lengths,
    self_qkv,
    self_qv_bias,
    self_out,
    self_out_bias,
    rel_weight,
    rel_bias,
    cross_qkv,
    cross_qv_bias,
    cross_out,
    cross_out_bias,
    ffn_in,
    ffn_in_bias,
    ffn_out,
    ffn_out_bias,
    norm_gain,
    norm_bias,
):
    B, S, T, width = hidden.shape
    if T % TILE or lax.axis_size("dp") != 8 or width % (32 * 8 * lax.axis_size("seq")):
        return plain_on_device(
            hidden,
            encoder_out,
            cotangent,
            dec_lengths,
            enc_lengths,
            self_qkv,
            self_qv_bias,
            self_out,
            self_out_bias,
            rel_weight,
            rel_bias,
            cross_qkv,
            cross_qv_bias,
            cross_out,
            cross_out_bias,
            ffn_in,
            ffn_in_bias,
            ffn_out,
            ffn_out_bias,
            norm_gain,
            norm_bias,
        )
    seq_parts = lax.axis_size("seq")
    keys = T * seq_parts
    far = keys - T
    place = lax.axis_index("seq")
    gains, shifts = norm_gain.astype(high_type), norm_bias.astype(high_type)
    self_bias, cross_bias = self_qv_bias.astype(high_type), cross_qv_bias.astype(high_type)
    table = jnp.asarray(bucket_table(), low_type)

    after = lax.optimization_barrier
    x = hidden.reshape(B * S * T, width)
    rows = B * S * T
    far_rows = []
    for b in range(B):
        sent = hidden[b, 0]
        if b:
            sent, far_rows[b - 1] = after((sent, far_rows[b - 1]))
        pieces = [
            lax.ppermute(sent, "seq", [(i, i + hop) for i in range(seq_parts - hop)])
            for hop in range(seq_parts - 1, 0, -1)
        ]
        far_rows.append(jnp.concatenate(pieces, 0))
    key_at = place * T - far + jnp.arange(keys, dtype=jnp.int32)
    self_mark = key_features((key_at >= 0) & (key_at < dec_lengths[:, None]))
    cross_mark = key_features(jnp.arange(keys, dtype=jnp.int32) < enc_lengths[:, None])

    q = ((dot("de,rd->er", self_qkv[0], x) + self_bias[0][:, None]) * SCALE).astype(low_type)
    rel = dot("db,rd->br", rel_weight, x) + rel_bias.astype(high_type)[:, None]
    k = dot("de,rd->er", self_qkv[1], x).astype(low_type)
    v = (dot("de,rd->er", self_qkv[2], x) + self_bias[1][:, None]).astype(low_type)
    self_inputs, results = [], ()
    for b in range(B):
        k_far, v_far = keys_and_values(far_rows[b], self_qkv, self_bias[1])
        if b == 0:
            e_own, k_far = after((encoder_out, k_far))
            e_all = lax.all_gather(e_own, "seq", axis=1, tiled=True).reshape(-1, width)
        self_inputs.append((q, k, v, k_far, v_far, rel, self_mark, table))
        results = self_forward(b, self_inputs[b], results, T, S)
        if b + 1 < B:
            far_rows[b + 1], results = after((far_rows[b + 1], results))
    attended, self_total = results
    first_sum = (
        x.astype(high_type)
        + dot("er,ed->rd", attended, self_out)
        + self_out_bias.astype(high_type)
    )
    first_unit, _ = norm_parts(first_sum)
    first_norm = first_unit * gains[0] + shifts[0]
    first_low = first_norm.astype(low_type)

    qc = ((dot("de,rd->er", cross_qkv[0], first_low) + cross_bias[0][:, None]) * SCALE).astype(
        low_type
    )
    kc, vc = keys_and_values(e_all, cross_qkv, cross_bias[1])
    cross_mixed, cross_total = cross_forward(qc, kc, vc, cross_mark)
    second_sum = (
        first_norm
        + dot("er,ed->rd", cross_mixed, cross_out)
        + cross_out_bias.astype(high_type)
    )
    second_unit, _ = norm_parts(second_sum)
    second_norm = second_unit * gains[1] + shifts[1]
    second_low = second_norm.astype(low_type)

    activated, slope = ffn_first(second_low, ffn_in, ffn_in_bias.astype(high_type)[None])
    third_sum = (
        second_norm + dot("rf,fd->rd", activated, ffn_out) + ffn_out_bias.astype(high_type)
    )
    third_unit, _ = norm_parts(third_sum)
    output = (third_unit * gains[2] + shifts[2]).astype(low_type).reshape(hidden.shape)

    grad_third, grad_gain_ffn, grad_shift_ffn = norm_back(
        third_sum, cotangent.reshape(rows, width).astype(high_type), gains[2]
    )
    grad_ffn = grad_third.astype(low_type)

    def over_dp(piece):
        return lax.psum_scatter(piece, "dp", scatter_dimension=0, tiled=True)

    def over_dp_by_steps(piece, beside_first, first_inputs, beside_second, second_inputs):
        me = lax.axis_index("dp")

        def swap(pair, bit):
            mine = (me >> bit) & 1
            sent = lax.dynamic_index_in_dim(pair, 1 - mine, 0, keepdims=False)
            kept = lax.dynamic_index_in_dim(pair, mine, 0, keepdims=False)
            came = lax.ppermute(sent, "dp", [(i, i ^ (1 << bit)) for i in range(8)])
            return low(came.astype(high_type) + kept.astype(high_type))

        count = piece.shape[0] // 8
        chip = swap(jnp.swapaxes(piece.reshape(4, 2, count, width), 0, 1), 0)
        chip, first_inputs = after((chip, first_inputs))
        first, second = chip[:, : count // 2], chip[:, count // 2 :]
        first = swap(jnp.swapaxes(first.reshape(2, 2, count // 2, width), 0, 1), 1)
        second = swap(second.reshape(2, 2, count // 2, width), 2)
        first, second, done_first, second_inputs = after(
            (first, second, beside_first(first_inputs), second_inputs)
        )
        first, second, done_second = after(
            (swap(first, 2), swap(second, 1), beside_second((done_first[1], *second_inputs)))
        )
        return jnp.concatenate([first, second], 0), done_first, done_second

    def over_seq(*pieces):
        cut = [piece.reshape(seq_parts, -1, width) for piece in pieces]
        joined = jnp.concatenate(cut, 1)

        def block(hop):
            return lax.dynamic_index_in_dim(
                joined, (place - hop) % seq_parts, 0, keepdims=False
            ).astype(high_type)

        ring = [(i, (i + 1) % seq_parts) for i in range(seq_parts)]
        held = block(1)
        for hop in range(2, seq_parts + 1):
            came = yield lax.ppermute(held.astype(low_type), "seq", ring)
            held = came.astype(high_type) + block(hop)
        ends = np.cumsum([piece.shape[1] for piece in cut])
        yield [
            held[end - piece.shape[1] : end].reshape(-1)
            for piece, end in zip(cut, ends, strict=True)
        ]

    def finish(steps, item):
        for _ in range(seq_parts - 2):
            item = steps.send(item)
        return steps.send(item)

    def low(value):
        return value.astype(low_type)

    part_ffn_out, grad_ffn = after((low(dot("rf,rd->fd", activated, grad_ffn)), grad_ffn))
    mat_ffn_out = over_dp(part_ffn_out)
    grad_pre = (dot("rd,fd->rf", grad_ffn, ffn_out) * slope.astype(high_type)).astype(low_type)
    part_ffn_in, grad_pre = after((low(dot("rd,rf->df", second_low, grad_pre)), grad_pre))
    mat_ffn_in = over_dp(part_ffn_in)
    grad_second = grad_third + dot("rf,df->rd", grad_pre, ffn_in)
    grad_second_sum, grad_gain_cross, grad_shift_cross = norm_back(
        second_sum, grad_second, gains[1]
    )
    grad_cross = grad_second_sum.astype(low_type)
    part_cross_out, grad_cross = after((low(dot("er,rd->ed", cross_mixed, grad_cross)), grad_cross))
    grad_cross_mixed = dot("ed,rd->er", cross_out, grad_cross).astype(low_type)
    dqc, dkc, dvc = cross_backward(
        qc, kc, vc, cross_mark, cross_mixed, cross_total, grad_cross_mixed
    )
    dqc, dkc, dvc, mat_ffn_out, mat_ffn_in = after((dqc, dkc, dvc, mat_ffn_out, mat_ffn_in))
    ffn_steps = over_seq(mat_ffn_in, mat_ffn_out)
    ffn_item = next(ffn_steps)
    part_encoder = back_rows(
        (dkc, dvc), ((cross_qkv, 1), (cross_qkv, 2)), None, None, keys, "encoder_rows"
    ).reshape(B, keys, width)
    grad_encoder = lax.psum_scatter(part_encoder, "seq", scatter_dimension=1, tiled=True)
    e_all, part_encoder, part_cross_out = after((e_all, part_encoder, part_cross_out))
    mat_cross_out = over_dp(part_cross_out)
    third = 3 * width // 8

    def cut(step, size, blocks):
        found = []
        for block in range(blocks):
            low_at, high_at = max(size * block, width * step), min(size * (block + 1), width * (step + 1))
            if low_at < high_at:
                found.append(((block, low_at - size * block), low_at - width * step, high_at - low_at, 0))
        return found

    columns = width // SPLIT
    part_cross_qkv, cross_sums = weight_grads(
        (first_low, e_all),
        (dqc, dkc, dvc),
        [
            pl.BlockSpec((columns, rows), lambda e, c: (e, 0)),
            pl.BlockSpec((columns, B * keys), lambda e, c: (e, 0)),
            pl.BlockSpec((columns, B * keys), lambda e, c: (e, 0)),
        ],
        [[(0, 0)], [(1, 1)], [(1, 2)]],
        [cut(step, third, 8) for step in range(3)],
        [True, False, True],
        (8, third, width),
        "cross_weights",
    )
    part_cross_qkv = part_cross_qkv.reshape(3 * width, width)
    part_encoder, part_cross_qkv, dqc, ffn_item = after(
        (part_encoder, part_cross_qkv, dqc, ffn_item)
    )
    ffn_item = ffn_steps.send(ffn_item)
    mat_cross_qkv = over_dp(part_cross_qkv)

    grad_first = grad_second_sum + dot("er,de->rd", dqc, cross_qkv[0])
    grad_first_sum, grad_gain_self, grad_shift_self = norm_back(first_sum, grad_first, gains[0])
    grad_self = grad_first_sum.astype(low_type)
    part_self_out, grad_self = after((low(dot("er,rd->ed", attended, grad_self)), grad_self))
    mat_self_out = over_dp(part_self_out)
    grad_attended = dot("ed,rd->er", self_out, grad_self).astype(low_type)
    def give_back(far_grads):
        away = back_rows(
            ((far_grads, 0), (far_grads, 1)), ((self_qkv, 1), (self_qkv, 2)), None, None, far, "far_rows"
        )
        return away, [
            lax.ppermute(
                away[(seq_parts - 1 - hop) * T : (seq_parts - hop) * T],
                "seq",
                [(i + hop, i) for i in range(seq_parts - hop)],
            )
            for hop in range(1, seq_parts)
        ]

    results, came, far_columns = (), [], []
    for b in range(B):
        *results, far_grads = self_backward(
            b, self_inputs[b], (attended, self_total, grad_attended), tuple(results), T, S
        )
        if b:
            far_grads, came[b - 1], grad_encoder, ffn_item = after(
                (far_grads, came[b - 1], grad_encoder, ffn_item)
            )
            done_ffn_in, done_ffn_out = ffn_steps.send(ffn_item)
        far_columns.append(far_grads)
        away, pieces = give_back(far_grads)
        came.append(pieces)
        if b + 1 < B:
            results[0], self_inputs[b + 1], away, ffn_item = after(
                (results[0], self_inputs[b + 1], away, ffn_item)
            )
            for _ in range(seq_parts - 3):
                ffn_item = ffn_steps.send(ffn_item)
    results[0], away = after((results[0], away))
    dq, dkv, drel = results
    blocks, size, rel_size = 8 * seq_parts, 3 * width // (8 * seq_parts), width // (16 * seq_parts)
    part_self, part_sums = weight_grads(
        (x, *far_rows),
        (dq, dkv, dkv, drel) + tuple(far_columns) * 2,
        [
            pl.BlockSpec((columns, rows), lambda e, c: (e, 0)),
            pl.BlockSpec((None, columns, rows), lambda e, c: (0, e, 0)),
            pl.BlockSpec((None, columns, rows), lambda e, c: (1, e, 0)),
            pl.BlockSpec((width // 2, rows), lambda e, c: (0, 0)),
        ]
        + [pl.BlockSpec((None, columns, far), lambda e, c: (0, e, 0))] * B
        + [pl.BlockSpec((None, columns, far), lambda e, c: (1, e, 0))] * B,
        [
            [(0, 0)],
            [(0, 1)] + [(1 + b, 4 + b) for b in range(B)],
            [(0, 2)] + [(1 + b, 4 + B + b) for b in range(B)],
            [(0, 3)],
        ],
        [cut(step, size, blocks) for step in range(3)]
        + [[((block, size), 2 * rel_size * block, rel_size, 1) for block in range(blocks)]],
        [True, False, True, True],
        (blocks, size + rel_size, width),
        "self_weights",
    )
    part_self, came[-1] = after((part_self, came[-1]))

    def near_rows(arrays):
        dq, came = arrays
        moved = jnp.concatenate(
            [functools.reduce(jnp.add, [piece.astype(high_type) for piece in came[b]]) for b in range(B)], 0
        )
        return back_rows(
            (dq, (dkv, 0), (dkv, 1), drel),
            ((self_qkv, 0), (self_qkv, 1), (self_qkv, 2), rel_weight),
            grad_first_sum,
            moved,
            S * T,
            "near_rows",
        )

    lengths = []

    def vector_sums(arrays):
        sums, part_sums, cross_sums = arrays
        vectors = [
            jnp.stack([part_sums[0, :, 0], part_sums[2, :, 0]]),
            sums[0],
            part_sums[3, : width // 2, 0],
            jnp.stack([cross_sums[0, :, 0], cross_sums[2, :, 0]]),
            sums[1],
            sums[2],
            sums[3],
            jnp.stack([grad_gain_self, grad_gain_cross, grad_gain_ffn]),
            jnp.stack([grad_shift_self, grad_shift_cross, grad_shift_ffn]),
        ]
        blocks = [piece.reshape(seq_parts, -1) for piece in vectors]
        lengths.extend(piece.shape[1] for piece in blocks)
        return pairwise(jnp.concatenate(blocks, 1), 0)

    def pairwise(value, bit):
        return value + lax.ppermute(value, "dp", [(i, i ^ (1 << bit)) for i in range(8)])

    cross_steps = None

    def second_window(arrays):
        nonlocal cross_steps
        cross_steps = over_seq(*arrays[1:])
        return pairwise(pairwise(arrays[0], 1), 2), next(cross_steps)

    part_self, summands = after((part_self, (grad_self, grad_cross, grad_pre, grad_ffn)))
    sums = [column_sum(summand) for summand in summands]
    def first_window(arrays):
        return near_rows(arrays[:2]), vector_sums(arrays[2:])

    mat_self, (grad_hidden, _), (summed, cross_item) = over_dp_by_steps(
        part_self.reshape(-1, width),
        first_window,
        (dq, came, sums, part_sums, cross_sums),
        second_window,
        (mat_cross_out, mat_cross_qkv, mat_self_out),
    )
    grad_hidden = grad_hidden.reshape(hidden.shape)
    done_cross_out, done_cross_qkv, done_self_out = finish(cross_steps, cross_item)
    ends = np.cumsum(lengths)
    lines = -(-int(ends[-1]) // (16 * width)) * 16
    summed = jnp.pad(summed, ((0, 0), (0, lines * width - int(ends[-1]))))
    self_steps = over_seq(mat_self, low(summed))
    done_self, mine = finish(self_steps, next(self_steps))
    done_self = done_self.reshape(size + rel_size, width)
    done_self_qkv = done_self[:size].reshape(-1)
    half = width // 2
    done_rel = jnp.concatenate([done_self[size:, :half], done_self[size:, half:]], 0).reshape(-1)
    vecs = [mine[end - count : end] for count, end in zip(lengths, ends, strict=True)]
    return (
        output,
        grad_hidden,
        grad_encoder,
        done_self_qkv,
        vecs[0],
        done_self_out,
        vecs[1],
        done_rel,
        vecs[2],
        done_cross_qkv,
        vecs[3],
        done_cross_out,
        vecs[4],
        done_ffn_in,
        vecs[5],
        done_ffn_out,
        vecs[6],
        vecs[7],
        vecs[8],
    )


def solution(mesh):
    rows, vector, matrix = P("dp", None, "seq", None), P("seq"), P(("dp", "seq"))
    return jax.shard_map(
        on_device,
        mesh=mesh,
        in_specs=(rows, P("dp", "seq", None), rows, P("dp"), P("dp")) + (P(),) * 16,
        out_specs=(rows, rows, P("dp", "seq", None))
        + (matrix, vector) * 7
        + (vector, vector),
        check_vma=False,
    )
```
